32 devices in a mesh: member: 2 (over x), tile: 16 (over z, y, core).
Axes of the slice: x: 2, y: 2, z: 4, core: 2. Of those that a mesh axis runs over, the one named last changes fastest.
Arguments:
- state: float32 [32, 6, 6, 128, 128], P(('member', 'tile')), parts along dimension 0, may hold values from -6 to 6
- wave_coef: float32 [3], replicated, may hold values from 0.08 to 0.3
- visc_coef: float32 [3], replicated, may hold values from 0.03 to 0.2
- stencil_start: int32 [3, 128], replicated, may hold values from 0 to 124, as said below
- stencil_offset: float32 [3, 128], replicated, may hold values from 0.5 to 2.5
Outputs:
- new_state: float32 [32, 6, 6, 128, 128], P(('member', 'tile')), parts along dimension 0
The draws below stay inside these ranges and needn't reach their ends.
There are 2 independent parts, one for each index of `member`. The reference program is written for one: setup_inputs(seed, part) draws one part's arguments, and reference() takes and returns one part's arrays. A program takes and returns all parts, laid end to end along the dimension named above; an argument that names none is the same for every part. Nothing has to cross between parts.
Inputs may be any that keep to these rules, and one draw needn't show every extreme that they name: stencil_start[h, k] lies within one cell of k - 1, kept inside the segment.
All inputs are finite; a program needn't handle non-finite values.
Results may differ from the reference program's by a relative error of at most 0.0001.
Values sent between devices are 32-bit elements; how exact they have to be, the bound alone decides.
No kernel may reach another device: no remote copies, remote signals or barrier semaphores. Data moves between devices by JAX's collectives and lax.ppermute only.
A program may use at most 128 MiB of HBM per device.

```python
import math
import jax
import jax.numpy as jnp
from jax import lax

FACES = 6
LEV = 3
CH = 6
DEPTH = 3
SUBSTEPS = 4
BLK = 128
SIDE = 4
BLOCKS = 16


def draw_stencil_start(key, part):
    key = jax.random.fold_in(key, 11)
    jitter = jax.random.randint(key, (DEPTH, BLK), -1, 2)
    cells = jnp.arange(BLK, dtype=jnp.int32)[None, :]
    return jnp.clip(cells - 1 + jitter, 0, BLK - 4).astype(jnp.int32)


def shard_levels(own_key, extent, shards, low, high):
    level = 1.0
    for position, parts in shards:
        heights = jax.random.uniform(jax.random.fold_in(jax.random.fold_in(own_key, 6), position), (parts,), jnp.float32, low / len(shards), high / len(shards))
        level = level * jnp.repeat(jnp.exp(heights), extent[position] // parts).reshape((-1,) + (1,) * (len(extent) - 1 - position))
    return level


def scatter_about(rng, shape, spread, limit, split=(), kind=jnp.bfloat16):
    array = spread * jax.random.normal(rng, shape, jnp.float32)
    if split:
        array = array * shard_levels(rng, shape, split, -0.22, 0.18)
    return jnp.clip(array, -limit, limit).astype(kind)


def setup_inputs(seed: int = 0, part: int = 0) -> dict:
    splits = jax.random.split(jax.random.key(seed), 6)
    own_keys = jax.random.split(jax.random.fold_in(splits[5], part), 6)
    state = scatter_about(own_keys[0], (BLOCKS, FACES, CH, BLK, BLK), 1.0, 6.0, ((0, 16),), jnp.float32)
    wave_coef = jnp.clip(jnp.exp(jax.random.uniform(splits[1], (LEV,), jnp.float32, math.log(0.08), math.log(0.3))), 0.08, 0.3)
    visc_coef = jnp.clip(jnp.exp(jax.random.uniform(splits[2], (LEV,), jnp.float32, math.log(0.03), math.log(0.2))), 0.03, 0.2)
    stencil_start = draw_stencil_start(jax.random.fold_in(splits[5], 71), part)
    stencil_offset = jnp.clip(jax.random.uniform(splits[4], (DEPTH, BLK), jnp.float32, 0.5, 2.5), 0.5, 2.5)
    return dict(state=state, wave_coef=wave_coef, visc_coef=visc_coef, stencil_start=stencil_start, stencil_offset=stencil_offset)


HALO_WEIGHTS = (0.45, 0.35, 0.2)


def lagrange_weights(offset_value):
    return (-(offset_value - 1.0) * (offset_value - 2.0) * (offset_value - 3.0) / 6.0,
            offset_value * (offset_value - 2.0) * (offset_value - 3.0) / 2.0,
            -offset_value * (offset_value - 1.0) * (offset_value - 3.0) / 2.0,
            offset_value * (offset_value - 1.0) * (offset_value - 2.0) / 6.0)


def interp_matrix(stencil_start, stencil_offset):
    halo_depth, seg_width = stencil_start.shape
    source_rows = jnp.arange(seg_width, dtype=jnp.int32)[None, :, None]
    matrix = jnp.zeros((halo_depth, seg_width, seg_width), jnp.float32)
    for shift_count, weight_row in enumerate(lagrange_weights(stencil_offset)):
        chosen = source_rows == (stencil_start[:, None, :] + shift_count).astype(jnp.int32)
        matrix = matrix + jnp.where(chosen, weight_row[:, None, :], 0.0)
    return matrix


def edge_strips(field_data, halo_depth):
    strip_east = jnp.swapaxes(jnp.flip(field_data[..., -halo_depth:], -1), -1, -2)
    strip_west = jnp.swapaxes(field_data[..., :halo_depth], -1, -2)
    strip_north = jnp.flip(field_data[..., -halo_depth:, :], -2)
    strip_south = field_data[..., :halo_depth, :]
    return strip_east, strip_west, strip_north, strip_south


def apply_operator(field_data, ghost_east, ghost_west, ghost_north, ghost_south):
    halo_depth = len(HALO_WEIGHTS)
    row_count = field_data.shape[-2]
    col_count = field_data.shape[-1]
    wide_grid = jnp.concatenate([jnp.swapaxes(jnp.flip(ghost_west, -2), -1, -2), field_data,
                                 jnp.swapaxes(ghost_east, -1, -2)], axis=-1)
    tall_grid = jnp.concatenate([jnp.flip(ghost_south, -2), field_data, ghost_north], axis=-2)
    tendency = jnp.zeros_like(field_data)
    for reach, weight_value in enumerate(HALO_WEIGHTS, start=1):
        left_cells = wide_grid[..., halo_depth - reach: halo_depth - reach + col_count]
        right_cells = wide_grid[..., halo_depth + reach: halo_depth + reach + col_count]
        lower_cells = tall_grid[..., halo_depth - reach: halo_depth - reach + row_count, :]
        upper_cells = tall_grid[..., halo_depth + reach: halo_depth + reach + row_count, :]
        tendency = tendency + weight_value * (left_cells + right_cells + lower_cells + upper_cells - 4.0 * field_data)
    return tendency


def advance_fields(field_data, tendency, wave_coef, visc_coef):
    levels = wave_coef.shape[0]
    rate_new = (field_data[:, levels:] + wave_coef[:, None, None] * tendency[:, :levels]
                + visc_coef[:, None, None] * tendency[:, levels:])
    pres_new = field_data[:, :levels] + rate_new
    return jnp.concatenate([pres_new, rate_new], axis=1)


def reverse_edge(strip_data):
    return jnp.flip(strip_data, -1)


def interp_global(raw_ghost, matrix):
    faces, channels, halo_depth, edge_len = raw_ghost.shape
    seg_width = matrix.shape[-1]
    pieces = raw_ghost.reshape(faces, channels, halo_depth, edge_len // seg_width, seg_width)
    done = jnp.einsum("fchpj,hjk->fchpk", pieces, matrix, precision=lax.Precision.HIGHEST)
    return done.reshape(faces, channels, halo_depth, edge_len)


def reference(state, wave_coef, visc_coef, stencil_start, stencil_offset):
    faces, channels, block_len = state.shape[1], state.shape[2], state.shape[-1]
    face_len = SIDE * block_len
    grid = state.reshape(SIDE, SIDE, faces, channels, block_len, block_len)
    grid = grid.transpose(2, 3, 0, 4, 1, 5).reshape(faces, channels, face_len, face_len)
    matrix = interp_matrix(stencil_start, stencil_offset)
    for step_index in range(SUBSTEPS):
        strip_east, strip_west, strip_north, strip_south = edge_strips(grid, len(HALO_WEIGHTS))
        raw_east = jnp.stack([strip_west[1], reverse_edge(strip_south[3]), strip_west[3],
                              reverse_edge(strip_south[5]), strip_west[5], reverse_edge(strip_south[1])])
        raw_west = jnp.stack([reverse_edge(strip_north[4]), strip_east[0], reverse_edge(strip_north[0]),
                              strip_east[2], reverse_edge(strip_north[2]), strip_east[4]])
        raw_north = jnp.stack([reverse_edge(strip_west[2]), strip_south[2], reverse_edge(strip_west[4]),
                               strip_south[4], reverse_edge(strip_west[0]), strip_south[0]])
        raw_south = jnp.stack([strip_north[5], reverse_edge(strip_east[5]), strip_north[1],
                               reverse_edge(strip_east[1]), strip_north[3], reverse_edge(strip_east[3])])
        tendency = apply_operator(grid, interp_global(raw_east, matrix), interp_global(raw_west, matrix),
                                  interp_global(raw_north, matrix), interp_global(raw_south, matrix))
        grid = advance_fields(grid, tendency, wave_coef, visc_coef)
    blocks = grid.reshape(faces, channels, SIDE, block_len, SIDE, block_len).transpose(2, 4, 0, 1, 3, 5)
    return blocks.reshape(SIDE * SIDE, faces, channels, block_len, block_len)
```

```python
import math

import jax
import jax.numpy as jnp
from jax import lax
from jax.experimental import pallas as pl
from jax.experimental.pallas import tpu as pltpu
from jax.sharding import PartitionSpec as P

SUBSTEPS = 4
FACES = 6
LEV = 3
DEPTH = 3
BLK = 128
PER_FACE = LEV * DEPTH
ROWS = 56
HALF = 64
WEST, EAST, SOUTH, NORTH = 0, 1, 2, 3
SCALE = 20.0
VMEM_LIMIT = 50 * 1024 * 1024


def whole_vmem():
    return pl.BlockSpec(memory_space=pltpu.VMEM)


def iota(shape, dim):
    return lax.broadcasted_iota(jnp.int32, shape, dim)


def weight_of(distance):
    return jnp.where(
        distance == 1, 9.0, jnp.where(distance == 2, 7.0, jnp.where(distance == 3, 4.0, 0.0))
    )


def split2(x):
    high = x.astype(jnp.bfloat16)
    low = (x - high.astype(jnp.float32)).astype(jnp.bfloat16)
    return high, low


def lagrange_weights(t):
    return (
        -(t - 1.0) * (t - 2.0) * (t - 3.0) / 6.0,
        t * (t - 2.0) * (t - 3.0) / 2.0,
        -t * (t - 1.0) * (t - 3.0) / 2.0,
        t * (t - 1.0) * (t - 2.0) / 6.0,
    )


def band_matrix():
    gap = jnp.abs(iota((BLK, BLK), 0) - iota((BLK, BLK), 1))
    return jnp.where(gap == 0, -40.0, weight_of(gap)).astype(jnp.bfloat16)


def edge_matrix():
    shape = (BLK, BLK)
    to, src = iota(shape, 0), iota(shape, 1)
    lower = to < HALF
    to_row = jnp.where(lower, to, to - HALF)
    src_row = jnp.where(src < HALF, src, src - HALF)
    to_plane = (to_row * 171) >> 9
    src_plane = (src_row * 171) >> 9
    to_j = to_row - 3 * to_plane
    src_j = src_row - 3 * src_plane
    same = ((to < HALF) == (src < HALF)) & (to_plane == src_plane)
    distance = jnp.where(lower, 3 + to_j - src_j, 3 + src_j - to_j)
    return jnp.where(same, weight_of(distance), 0.0).astype(jnp.bfloat16)


def seam_matrices(start_ref, offset_ref, out_ref):
    j = iota((BLK, BLK), 0)
    back = BLK - 1 - j
    for h in range(DEPTH):
        first = start_ref[h : h + 1, :]
        weights = lagrange_weights(offset_ref[h : h + 1, :])
        plain = jnp.zeros((BLK, BLK), jnp.float32)
        turned = jnp.zeros((BLK, BLK), jnp.float32)
        for m, weight in enumerate(weights):
            plain = plain + jnp.where(j == first + m, weight, 0.0)
            turned = turned + jnp.where(back == first + m, weight, 0.0)
        out_ref[:, h * BLK : (h + 1) * BLK] = plain
        out_ref[:, (DEPTH + h) * BLK : (DEPTH + h + 1) * BLK] = turned


def position(side):
    index = lax.axis_index("tile")
    return lax.rem(index, side), lax.div(index, side)


def row_codes(shape):
    row = iota(shape, 0)
    block = (row * 57) >> 9
    odd = (block & 1) == 1
    depth = row - 3 * ((row * 171) >> 9)
    return odd, depth


def take_edges(q, plane, columns, strips_ref):
    lane = iota((BLK, BLK), 1)
    low, high = 3 * plane, HALF + 3 * plane
    columns = jnp.where((lane >= low) & (lane < low + 3), pltpu.roll(q, low, 1), columns)
    turn = (high - (BLK - 3)) % BLK
    columns = jnp.where((lane >= high) & (lane < high + 3), pltpu.roll(q, turn, 1), columns)
    face, level = divmod(plane, LEV)
    strips_ref[SOUTH, face, 3 * level : 3 * level + 3, :] = q[:3, :]
    strips_ref[NORTH, face, 3 * level : 3 * level + 3, :] = q[BLK - 3 :, :]
    return columns


def pack(columns, strips_ref, side, outs):
    core_ref, mirror_ref, near_ref, far_ref, turn_ref, own_a_ref, own_b_ref = outs
    col, row = position(side)
    edges = columns.T
    for face in range(FACES):
        at = PER_FACE * face
        strips_ref[WEST, face, :PER_FACE, :] = edges[at : at + PER_FACE, :]
        strips_ref[EAST, face, :PER_FACE, :] = edges[HALF + at : HALF + at + PER_FACE, :]
    even_col, even_row = lax.rem(col, 2) == 0, lax.rem(row, 2) == 0

    def shift(place):
        return jnp.where(place == 0, 1, jnp.where(place == side - 1, FACES - 1, 0))

    plans = (
        (core_ref, jnp.where(even_col, EAST, WEST), 0),
        (mirror_ref, jnp.where(even_col, WEST, EAST), shift(col)),
        (near_ref, jnp.where(even_row, NORTH, SOUTH), 0),
        (far_ref, jnp.where(even_row, SOUTH, NORTH), shift(row)),
    )
    for out_ref, which, by in plans:
        for face in range(FACES):
            at = PER_FACE * face
            source = face + by
            source = jnp.where(source >= FACES, source - FACES, source)
            out_ref[at : at + PER_FACE, :] = strips_ref[which, source, :PER_FACE, :]
        out_ref[FACES * PER_FACE :, :] = jnp.zeros((ROWS - FACES * PER_FACE, BLK), jnp.float32)
    for face in range(FACES):
        at = PER_FACE * face
        if face % 2:
            a, b = (SOUTH, face + 2), (EAST, face - 2)
        else:
            a, b = (NORTH, face - 2), (WEST, face + 2)
        own_a_ref[at : at + PER_FACE, :] = strips_ref[a[0], a[1] % FACES, :PER_FACE, :]
        own_b_ref[at : at + PER_FACE, :] = strips_ref[b[0], b[1] % FACES, :PER_FACE, :]
    rest = jnp.zeros((ROWS - FACES * PER_FACE, BLK), jnp.float32)
    own_a_ref[FACES * PER_FACE :, :] = rest
    own_b_ref[FACES * PER_FACE :, :] = rest
    odd, _ = row_codes((ROWS, BLK))
    use_a = jnp.where(odd, (row == 0).astype(jnp.int32), (row == side - 1).astype(jnp.int32))
    turn_ref[...] = jnp.where(use_a == 1, own_a_ref[...], own_b_ref[...])


def first_kernel(side, wave_ref, visc_ref, state_ref, start_ref, offset_ref, *rest):
    matrix_ref, outs, strips_ref = rest[0], rest[1:-1], rest[-1]
    seam_matrices(start_ref, offset_ref, matrix_ref)
    columns = jnp.zeros((BLK, BLK), jnp.float32)
    for plane in range(FACES * LEV):
        face, level = divmod(plane, LEV)
        a, b = wave_ref[level] * (1.0 / SCALE), visc_ref[level] * (1.0 / SCALE)
        q = a * state_ref[face, level] + b * state_ref[face, LEV + level]
        columns = take_edges(q, plane, columns, strips_ref)
    pack(columns, strips_ref, side, outs)


def ghosts_of(side, received, own_a_ref, own_b_ref, matrix_ref):
    core, mirror, near, far, turned = [ref[...] for ref in received]
    col, row = position(side)
    even_col, even_row = lax.rem(col, 2) == 0, lax.rem(row, 2) == 0
    odd, depth = row_codes((ROWS, BLK))
    alone = ((row == 0) & (col == side - 1)) | ((col == 0) & (row == side - 1))
    turned_a = jnp.where(alone, own_a_ref[...], turned)
    turned_b = jnp.where(alone, own_b_ref[...], turned)
    sides = (
        (jnp.where(even_col, mirror, core), turned_a, col == 0, False, True),
        (jnp.where(even_col, core, mirror), turned_a, col == side - 1, True, False),
        (jnp.where(even_row, far, near), turned_b, row == 0, True, True),
        (jnp.where(even_row, near, far), turned_b, row == side - 1, False, False),
    )
    raws = []
    for straight, crossed, at_seam, turned_odd, _ in sides:
        is_turned = odd if turned_odd else ~odd
        raws.append(jnp.where(at_seam & is_turned, crossed, straight))
    mixed = jnp.dot(
        jnp.concatenate(raws, axis=0),
        matrix_ref[...],
        precision=lax.Precision.HIGHEST,
        preferred_element_type=jnp.float32,
    )
    ghosts = []
    for place, (_, _, at_seam, turned_odd, reverse) in enumerate(sides):
        part = mixed[place * ROWS : (place + 1) * ROWS, :]
        is_turned = odd if turned_odd else ~odd
        made = raws[place]
        for h in range(DEPTH):
            index = (DEPTH - 1 - h) if reverse else h
            plain = part[:, h * BLK : (h + 1) * BLK]
            turn = part[:, (DEPTH + h) * BLK : (DEPTH + h + 1) * BLK]
            made = jnp.where(at_seam & (depth == index), jnp.where(is_turned, turn, plain), made)
        ghosts.append(made)
    rest = jnp.zeros((HALF - ROWS, BLK), jnp.float32)
    west, east, south, north = ghosts
    return (
        jnp.concatenate([west, rest, east, rest], axis=0),
        jnp.concatenate([south, rest, north, rest], axis=0),
    )


def step_kernel(side, last, wave_ref, visc_ref, state_ref, matrix_ref, *rest):
    received, rest = rest[:5], rest[5:]
    own_a_ref, own_b_ref, new_ref = rest[:3]
    outs = rest[3:-1]
    strips_ref = rest[-1]
    across, along = ghosts_of(side, received, own_a_ref, own_b_ref, matrix_ref)
    edge = edge_matrix()
    both = jnp.concatenate([across, along], axis=1)
    high, low = split2(both)
    adds = jnp.dot(
        jnp.concatenate([edge, edge], axis=1),
        jnp.concatenate([high, low], axis=0),
        preferred_element_type=jnp.float32,
    )
    add_x = adds[:, :BLK].T
    add_y = adds[:, BLK:]
    band = band_matrix()
    band_x = jnp.concatenate([band, band], axis=0)
    band_y = jnp.concatenate([band, band], axis=1)
    lane = iota((BLK, BLK), 1)
    pad = jnp.zeros((5, BLK), jnp.float32)
    columns = jnp.zeros((BLK, BLK), jnp.float32)
    for plane in range(FACES * LEV):
        face, level = divmod(plane, LEV)
        a, b = wave_ref[level] * (1.0 / SCALE), visc_ref[level] * (1.0 / SCALE)
        pressure, rate = state_ref[face, level], state_ref[face, LEV + level]
        high, low = split2(a * pressure + b * rate)
        by_x = jnp.dot(
            jnp.concatenate([high, low], axis=1), band_x, preferred_element_type=jnp.float32
        )
        by_y = jnp.dot(
            band_y, jnp.concatenate([high, low], axis=0), preferred_element_type=jnp.float32
        )
        at_west = pltpu.roll(add_x, (-3 * plane) % BLK, 1)
        at_east = pltpu.roll(add_x, (BLK - 3 - HALF - 3 * plane) % BLK, 1)
        edge_x = jnp.where(lane < 3, at_west, jnp.where(lane >= BLK - 3, at_east, 0.0))
        rate = rate + by_x + by_y + edge_x
        at = 3 * plane
        bottom = rate[:8] + jnp.concatenate([add_y[at : at + 3], pad], axis=0)
        top = rate[BLK - 8 :] + jnp.concatenate([pad, add_y[HALF + at : HALF + at + 3]], axis=0)
        rate = jnp.concatenate([bottom, rate[8 : BLK - 8], top], axis=0)
        pressure = pressure + rate
        new_ref[face, level] = pressure
        new_ref[face, LEV + level] = rate
        if not last:
            columns = take_edges(a * pressure + b * rate, plane, columns, strips_ref)
    if not last:
        pack(columns, strips_ref, side, outs)


def exchange(payloads, side):
    def at(row, col):
        return row * side + col

    cells = [(row, col) for row in range(side) for col in range(side)]

    def swap(place, odd_first):
        return (place ^ 1) if not odd_first else (place + (1 if place % 2 else -1)) % side

    core = [(at(r, c), at(r, swap(c, False))) for r, c in cells]
    mirror = [(at(r, c), at(r, swap(c, True))) for r, c in cells]
    near = [(at(r, c), at(swap(r, False), c)) for r, c in cells]
    far = [(at(r, c), at(swap(r, True), c)) for r, c in cells]
    edge = side - 1
    turn = set()
    for x in range(edge):
        turn |= {(at(0, x), at(edge - x, edge)), (at(edge - x, edge), at(0, x))}
    for x in range(1, side):
        turn |= {(at(edge, x), at(edge - x, 0)), (at(edge - x, 0), at(edge, x))}
    core_out, mirror_out, near_out, far_out, turn_out = payloads
    core_in = lax.ppermute(core_out, "tile", core)
    mirror_in = lax.ppermute(mirror_out, "tile", mirror)
    near_in = lax.ppermute(near_out, "tile", near)
    far_in = lax.ppermute(far_out, "tile", far)
    turn_in = lax.ppermute(turn_out, "tile", sorted(turn))
    return core_in, mirror_in, near_in, far_in, turn_in


def on_device(state, wave_coef, visc_coef, stencil_start, stencil_offset):
    side = math.isqrt(lax.axis_size("tile"))
    current = state[0]
    scalars = pl.BlockSpec(memory_space=pltpu.SMEM)
    params = pltpu.CompilerParams(vmem_limit_bytes=VMEM_LIMIT)
    strip = jax.ShapeDtypeStruct((ROWS, BLK), jnp.float32)
    strips = pltpu.VMEM((4, FACES, 16, BLK), jnp.float32)
    matrix, *sent = pl.pallas_call(
        lambda *refs: first_kernel(side, *refs),
        out_shape=[jax.ShapeDtypeStruct((BLK, 2 * DEPTH * BLK), jnp.float32)] + [strip] * 7,
        in_specs=[scalars] * 2 + [whole_vmem()] * 3,
        out_specs=[whole_vmem()] * 8,
        scratch_shapes=[strips],
        compiler_params=params,
        name="first_edges",
    )(wave_coef, visc_coef, current, stencil_start, stencil_offset)
    for step in range(SUBSTEPS):
        last = step == SUBSTEPS - 1
        received = exchange(sent[:5], side)
        extra = 0 if last else 7
        current, *sent_next = pl.pallas_call(
            lambda *refs, last=last: step_kernel(side, last, *refs),
            out_shape=[jax.ShapeDtypeStruct(current.shape, jnp.float32)] + [strip] * extra,
            in_specs=[scalars] * 2 + [whole_vmem()] * 9,
            out_specs=[whole_vmem()] * (1 + extra),
            scratch_shapes=[strips],
            compiler_params=params,
            name="substep",
        )(wave_coef, visc_coef, current, matrix, *received, *sent[5:])
        sent = sent_next
    return current[None]


def solution(mesh):
    placed = (P(("member", "tile"), None, None, None, None), P(), P(), P(), P())
    return jax.shard_map(
        on_device,
        mesh=mesh,
        in_specs=placed,
        out_specs=P(("member", "tile"), None, None, None, None),
        check_vma=False,
    )
```

```python
import math

import jax
import jax.numpy as jnp
from jax import lax
from jax.experimental import pallas as pl
from jax.experimental.pallas import tpu as pltpu
from jax.sharding import PartitionSpec as P

SUBSTEPS = 4
FACES = 6
LEV = 3
DEPTH = 3
BLK = 128
PER_FACE = LEV * DEPTH
ROWS = 56
HALF = 64
WEST, EAST, SOUTH, NORTH = 0, 1, 2, 3
SCALE = 20.0
VMEM_LIMIT = 16 * 1024 * 1024


def whole_vmem():
    return pl.BlockSpec(memory_space=pltpu.VMEM)


def iota(shape, dim):
    return lax.broadcasted_iota(jnp.int32, shape, dim)


def weight_of(distance):
    return jnp.where(
        distance == 1, 9.0, jnp.where(distance == 2, 7.0, jnp.where(distance == 3, 4.0, 0.0))
    )


def split2(x):
    high = x.astype(jnp.bfloat16)
    low = (x - high.astype(jnp.float32)).astype(jnp.bfloat16)
    return high, low


def lagrange_weights(t):
    return (
        -(t - 1.0) * (t - 2.0) * (t - 3.0) / 6.0,
        t * (t - 2.0) * (t - 3.0) / 2.0,
        -t * (t - 1.0) * (t - 3.0) / 2.0,
        t * (t - 1.0) * (t - 2.0) / 6.0,
    )


def band_matrix():
    gap = jnp.abs(iota((BLK, BLK), 0) - iota((BLK, BLK), 1))
    return jnp.where(gap == 0, -40.0, weight_of(gap)).astype(jnp.bfloat16)


def edge_matrix():
    shape = (BLK, BLK)
    to, src = iota(shape, 0), iota(shape, 1)
    lower = to < HALF
    to_row = jnp.where(lower, to, to - HALF)
    src_row = jnp.where(src < HALF, src, src - HALF)
    to_plane = (to_row * 171) >> 9
    src_plane = (src_row * 171) >> 9
    to_j = to_row - 3 * to_plane
    src_j = src_row - 3 * src_plane
    same = ((to < HALF) == (src < HALF)) & (to_plane == src_plane)
    distance = jnp.where(lower, 3 + to_j - src_j, 3 + src_j - to_j)
    return jnp.where(same, weight_of(distance), 0.0).astype(jnp.bfloat16)


def seam_matrices(starts, offsets, out_ref):
    j = iota((BLK, BLK), 0)
    back = BLK - 1 - j
    for h in range(DEPTH):
        first = starts[h : h + 1, :]
        weights = lagrange_weights(offsets[h : h + 1, :])
        for turned, place in ((0, j), (1, back)):
            matrix = jnp.zeros((BLK, BLK), jnp.float32)
            for m, weight in enumerate(weights):
                matrix = matrix + jnp.where(place == first + m, weight, 0.0)
            high, low = split2(matrix)
            at = (turned * DEPTH + h) * BLK
            out_ref[:BLK, at : at + BLK] = high
            out_ref[BLK : 2 * BLK, at : at + BLK] = high
            out_ref[2 * BLK :, at : at + BLK] = low


def position(side):
    index = lax.axis_index("tile")
    return lax.rem(index, side), lax.div(index, side)


def row_codes(shape):
    row = iota(shape, 0)
    block = (row * 57) >> 9
    odd = (block & 1) == 1
    depth = row - 3 * ((row * 171) >> 9)
    return odd, depth


def plane_row(shape, dim):
    row = iota(shape, dim)
    lower = row < HALF
    inside = jnp.where(lower, row, row - HALF)
    plane = (inside * 171) >> 9
    return lower, plane, inside - 3 * plane


def take_edges(q, plane, columns, rows_ref):
    lane = iota((BLK, BLK), 1)
    low, high = 3 * plane, HALF + 3 * plane
    columns = jnp.where((lane >= low) & (lane < low + 3), pltpu.roll(q, low, 1), columns)
    turn = (high - (BLK - 3)) % BLK
    columns = jnp.where((lane >= high) & (lane < high + 3), pltpu.roll(q, turn, 1), columns)
    rows_ref[low : low + 3, :] = q[:3, :]
    rows_ref[high : high + 3, :] = q[BLK - 3 :, :]
    return columns


def clear_rest(rows_ref):
    used = FACES * PER_FACE
    rest = jnp.zeros((HALF - used, BLK), jnp.float32)
    rows_ref[used:HALF, :] = rest
    rows_ref[HALF + used :, :] = rest


def pack(columns_ref, rows_ref, side, outs, strips_ref):
    core_ref, mirror_ref, near_ref, far_ref, turn_ref, own_a_ref, own_b_ref = outs
    col, row = position(side)
    for face in range(FACES):
        at = PER_FACE * face
        strips_ref[WEST, face, :PER_FACE, :] = columns_ref[at : at + PER_FACE, :]
        strips_ref[EAST, face, :PER_FACE, :] = columns_ref[HALF + at : HALF + at + PER_FACE, :]
        strips_ref[SOUTH, face, :PER_FACE, :] = rows_ref[at : at + PER_FACE, :]
        strips_ref[NORTH, face, :PER_FACE, :] = rows_ref[HALF + at : HALF + at + PER_FACE, :]
    even_col, even_row = lax.rem(col, 2) == 0, lax.rem(row, 2) == 0

    def shift(place):
        return jnp.where(place == 0, 1, jnp.where(place == side - 1, FACES - 1, 0))

    plans = (
        (core_ref, jnp.where(even_col, EAST, WEST), 0),
        (mirror_ref, jnp.where(even_col, WEST, EAST), shift(col)),
        (near_ref, jnp.where(even_row, NORTH, SOUTH), 0),
        (far_ref, jnp.where(even_row, SOUTH, NORTH), shift(row)),
    )
    rest = jnp.zeros((ROWS - FACES * PER_FACE, BLK), jnp.float32)
    for out_ref, which, by in plans:
        for face in range(FACES):
            at = PER_FACE * face
            source = face + by
            source = jnp.where(source >= FACES, source - FACES, source)
            out_ref[at : at + PER_FACE, :] = strips_ref[which, source, :PER_FACE, :]
        out_ref[FACES * PER_FACE :, :] = rest
    for face in range(FACES):
        at = PER_FACE * face
        if face % 2:
            a, b = (SOUTH, face + 2), (EAST, face - 2)
        else:
            a, b = (NORTH, face - 2), (WEST, face + 2)
        own_a_ref[at : at + PER_FACE, :] = strips_ref[a[0], a[1] % FACES, :PER_FACE, :]
        own_b_ref[at : at + PER_FACE, :] = strips_ref[b[0], b[1] % FACES, :PER_FACE, :]
    own_a_ref[FACES * PER_FACE :, :] = rest
    own_b_ref[FACES * PER_FACE :, :] = rest
    odd, _ = row_codes((ROWS, BLK))
    use_a = jnp.where(odd, (row == 0).astype(jnp.int32), (row == side - 1).astype(jnp.int32))
    turn_ref[...] = jnp.where(use_a == 1, own_a_ref[...], own_b_ref[...])


def first_kernel(side, state_hbm, wave_hbm, visc_hbm, start_hbm, offset_hbm, *rest):
    state_ref, coef_ref, gain_ref, matrix_ref = rest[:4]
    outs = rest[4:11]
    wave, visc, starts, offsets, columns_ref, rows_ref, strips_ref, sems = rest[11:]
    small = [
        pltpu.make_async_copy(src, dst, sems.at[FACES + place])
        for place, (src, dst) in enumerate(
            ((wave_hbm, wave), (visc_hbm, visc), (start_hbm, starts), (offset_hbm, offsets))
        )
    ]
    faces = [
        pltpu.make_async_copy(state_hbm.at[face], state_ref.at[face], sems.at[face])
        for face in range(FACES)
    ]
    for copy in small + faces:
        copy.start()
    clear_rest(rows_ref)
    for copy in small:
        copy.wait()
    seam_matrices(starts[...], offsets[...], matrix_ref)
    gain = jnp.zeros((BLK, BLK), jnp.float32)
    _, plane_of, _ = plane_row((BLK, BLK), 0)
    level_of = plane_of - 3 * ((plane_of * 171) >> 9)
    for level in range(LEV):
        a, b = wave[level] * (1.0 / SCALE), visc[level] * (1.0 / SCALE)
        coef_ref[level : level + 1, :] = jnp.full((1, BLK), a, jnp.float32)
        coef_ref[LEV + level : LEV + level + 1, :] = jnp.full((1, BLK), b, jnp.float32)
        gain = jnp.where(level_of == level, a + b, gain)
    coef_ref[2 * LEV :, :] = jnp.zeros((8 - 2 * LEV, BLK), jnp.float32)
    gain_ref[...] = gain
    columns = jnp.zeros((BLK, BLK), jnp.float32)
    for plane in range(FACES * LEV):
        face, level = divmod(plane, LEV)
        if level == 0:
            faces[face].wait()
        a, b = coef_ref[level : level + 1, :], coef_ref[LEV + level : LEV + level + 1, :]
        q = a * state_ref[face, level] + b * state_ref[face, LEV + level]
        columns = take_edges(q, plane, columns, rows_ref)
    columns_ref[...] = columns.T
    pack(columns_ref, rows_ref, side, outs, strips_ref)


def ghosts_of(side, received, own_a_ref, own_b_ref, matrix_ref):
    core, mirror, near, far, turned = [ref[...] for ref in received]
    col, row = position(side)
    even_col, even_row = lax.rem(col, 2) == 0, lax.rem(row, 2) == 0
    odd, depth = row_codes((ROWS, BLK))
    alone = ((row == 0) & (col == side - 1)) | ((col == 0) & (row == side - 1))
    turned_a = jnp.where(alone, own_a_ref[...], turned)
    turned_b = jnp.where(alone, own_b_ref[...], turned)
    sides = (
        (jnp.where(even_col, mirror, core), turned_a, col == 0, False, True),
        (jnp.where(even_col, core, mirror), turned_a, col == side - 1, True, False),
        (jnp.where(even_row, far, near), turned_b, row == 0, True, True),
        (jnp.where(even_row, near, far), turned_b, row == side - 1, False, False),
    )
    raws = []
    for straight, crossed, at_seam, turned_odd, _ in sides:
        is_turned = odd if turned_odd else ~odd
        raws.append(jnp.where(at_seam & is_turned, crossed, straight))
    high, low = split2(jnp.concatenate(raws, axis=0))
    mixed = jnp.dot(
        jnp.concatenate([high, low, high], axis=1),
        matrix_ref[...],
        preferred_element_type=jnp.float32,
    )
    ghosts = []
    for place, (_, _, at_seam, turned_odd, reverse) in enumerate(sides):
        part = mixed[place * ROWS : (place + 1) * ROWS, :]
        is_turned = odd if turned_odd else ~odd
        made = raws[place]
        for h in range(DEPTH):
            index = (DEPTH - 1 - h) if reverse else h
            plain = part[:, h * BLK : (h + 1) * BLK]
            turn = part[:, (DEPTH + h) * BLK : (DEPTH + h + 1) * BLK]
            made = jnp.where(at_seam & (depth == index), jnp.where(is_turned, turn, plain), made)
        ghosts.append(made)
    rest = jnp.zeros((HALF - ROWS, BLK), jnp.float32)
    west, east, south, north = ghosts
    return (
        jnp.concatenate([west, rest, east, rest], axis=0),
        jnp.concatenate([south, rest, north, rest], axis=0),
    )


def corner_part(adds_turned):
    shape = (BLK, BLK)
    lower, plane, cell = plane_row(shape, 0)
    lower_src, plane_src, cell_src = plane_row(shape, 1)
    low = jnp.where(
        cell == 0, adds_turned[0:1, :], jnp.where(cell == 1, adds_turned[1:2, :], adds_turned[2:3, :])
    )
    end = BLK - 3
    high = jnp.where(
        cell == 0,
        adds_turned[end : end + 1, :],
        jnp.where(cell == 1, adds_turned[end + 1 : end + 2, :], adds_turned[end + 2 : end + 3, :]),
    )
    kept = jnp.where(plane == plane_src, jnp.where(lower, low, high), 0.0)
    from_lower, from_plane, from_cell = plane_row(shape, 0)
    to = iota(shape, 1)
    fold = jnp.where(to == jnp.where(from_lower, from_cell, from_cell + end), 1.0, 0.0)
    fold = jnp.where(from_plane < FACES * LEV, fold, 0.0).astype(jnp.bfloat16)
    first, second = split2(kept)
    return jnp.dot(
        jnp.concatenate([first, second], axis=1),
        jnp.concatenate([fold, fold], axis=0),
        preferred_element_type=jnp.float32,
    )


def edge_kernel(side, last, *refs):
    received, refs = refs[:5], refs[5:]
    own_a_ref, own_b_ref, matrix_ref = refs[:3]
    refs = refs[3:]
    across, along = ghosts_of(side, received, own_a_ref, own_b_ref, matrix_ref)
    edge = edge_matrix()
    high, low = split2(jnp.concatenate([across, along], axis=1))
    adds = jnp.dot(
        jnp.concatenate([edge, edge], axis=1),
        jnp.concatenate([high, low], axis=0),
        preferred_element_type=jnp.float32,
    )
    add_x, add_y = adds[:, :BLK], adds[:, BLK:]
    turned_x = add_x.T
    if last:
        add_x_ref, add_y_ref = refs
        add_x_ref[...] = turned_x
        add_y_ref[...] = add_y
        return
    gain_ref, old_columns_ref, old_rows_ref, add_x_ref, add_y_ref = refs[:5]
    outs = refs[5:12]
    columns_ref, rows_ref, strips_ref = refs[12:]
    add_x_ref[...] = turned_x
    add_y_ref[...] = add_y
    gain = gain_ref[...]
    columns_ref[...] = old_columns_ref[...] + gain * (add_x + corner_part(add_y.T))
    rows_ref[...] = old_rows_ref[...] + gain * (add_y + corner_part(turned_x))
    pack(columns_ref, rows_ref, side, outs, strips_ref)


def edge_additions(plane, add_x, add_y, lane):
    at_west = pltpu.roll(add_x, (-3 * plane) % BLK, 1)
    at_east = pltpu.roll(add_x, (BLK - 3 - HALF - 3 * plane) % BLK, 1)
    add = jnp.where(lane < 3, at_west, jnp.where(lane >= BLK - 3, at_east, 0.0))
    at = 3 * plane
    pad = jnp.zeros((5, BLK), jnp.float32)
    bottom = add[:8] + jnp.concatenate([add_y[at : at + 3], pad], axis=0)
    top = add[BLK - 8 :] + jnp.concatenate([pad, add_y[HALF + at : HALF + at + 3]], axis=0)
    return jnp.concatenate([bottom, add[8 : BLK - 8], top], axis=0)


def inner_kernel(first, last, state_ref, coef_ref, *refs):
    if not first:
        add_x_ref, add_y_ref = refs[:2]
        refs = refs[2:]
        add_x, add_y = add_x_ref[...], add_y_ref[...]
    new_ref = refs[0]
    if not last:
        columns_ref, rows_ref = refs[1:]
        clear_rest(rows_ref)
    band = band_matrix()
    band_x = jnp.concatenate([band, band], axis=0)
    band_y = jnp.concatenate([band, band], axis=1)
    lane = iota((BLK, BLK), 1)
    columns = jnp.zeros((BLK, BLK), jnp.float32)
    for plane in range(FACES * LEV):
        face, level = divmod(plane, LEV)
        a, b = coef_ref[level : level + 1, :], coef_ref[LEV + level : LEV + level + 1, :]
        pressure, rate = state_ref[face, level], state_ref[face, LEV + level]
        if not first:
            add = edge_additions(plane, add_x, add_y, lane)
            pressure, rate = pressure + add, rate + add
        high, low = split2(a * pressure + b * rate)
        by_x = jnp.dot(
            jnp.concatenate([high, low], axis=1), band_x, preferred_element_type=jnp.float32
        )
        by_y = jnp.dot(
            band_y, jnp.concatenate([high, low], axis=0), preferred_element_type=jnp.float32
        )
        rate = rate + by_x + by_y
        pressure = pressure + rate
        new_ref[face, level] = pressure
        new_ref[face, LEV + level] = rate
        if not last:
            columns = take_edges(a * pressure + b * rate, plane, columns, rows_ref)
    if not last:
        columns_ref[...] = columns.T


def final_kernel(state_ref, add_x_ref, add_y_ref, out_hbm, buffer, sems):
    add_x, add_y = add_x_ref[...], add_y_ref[...]
    lane = iota((BLK, BLK), 1)
    copies = []
    for face in range(FACES):
        for level in range(LEV):
            add = edge_additions(face * LEV + level, add_x, add_y, lane)
            buffer[face, level] = state_ref[face, level] + add
            buffer[face, LEV + level] = state_ref[face, LEV + level] + add
        copy = pltpu.make_async_copy(buffer.at[face], out_hbm.at[face], sems.at[face])
        copy.start()
        copies.append(copy)
    for copy in copies:
        copy.wait()


def exchange(payloads, side):
    def at(row, col):
        return row * side + col

    cells = [(row, col) for row in range(side) for col in range(side)]

    def swap(place, odd_first):
        return (place ^ 1) if not odd_first else (place + (1 if place % 2 else -1)) % side

    core = [(at(r, c), at(r, swap(c, False))) for r, c in cells]
    mirror = [(at(r, c), at(r, swap(c, True))) for r, c in cells]
    near = [(at(r, c), at(swap(r, False), c)) for r, c in cells]
    far = [(at(r, c), at(swap(r, True), c)) for r, c in cells]
    edge = side - 1
    turn = set()
    for x in range(edge):
        turn |= {(at(0, x), at(edge - x, edge)), (at(edge - x, edge), at(0, x))}
    for x in range(1, side):
        turn |= {(at(edge, x), at(edge - x, 0)), (at(edge - x, 0), at(edge, x))}
    core_out, mirror_out, near_out, far_out, turn_out = payloads
    turn_in = lax.ppermute(turn_out, "tile", sorted(turn))
    far_in = lax.ppermute(far_out, "tile", far)
    near_in = lax.ppermute(near_out, "tile", near)
    mirror_in = lax.ppermute(mirror_out, "tile", mirror)
    core_in = lax.ppermute(core_out, "tile", core)
    return core_in, mirror_in, near_in, far_in, turn_in


def call(kernel, name, outs, ins, scratch=(), out_hbm=False, in_hbm=False, cost=0, aliases=None):
    hbm = pl.BlockSpec(memory_space=pltpu.HBM)
    vmem = pl.BlockSpec(memory_space=pltpu.VMEM)
    return pl.pallas_call(
        kernel,
        out_shape=outs,
        in_specs=[hbm if in_hbm else vmem] * len(ins),
        out_specs=[hbm if out_hbm else vmem] * len(outs),
        scratch_shapes=list(scratch),
        compiler_params=pltpu.CompilerParams(vmem_limit_bytes=VMEM_LIMIT),
        cost_estimate=pl.CostEstimate(flops=cost, bytes_accessed=cost // 500, transcendentals=0),
        input_output_aliases=aliases or {},
        name=name,
    )(*ins)


def on_device(state, wave_coef, visc_coef, stencil_start, stencil_offset):
    side = math.isqrt(lax.axis_size("tile"))
    field = state[0]

    def array(*shape, dtype=jnp.float32):
        return jax.ShapeDtypeStruct(shape, dtype)

    tile = array(BLK, BLK)
    strip = array(ROWS, BLK)
    whole = array(*field.shape)
    tile_scratch = pltpu.VMEM((BLK, BLK), jnp.float32)
    strips = pltpu.VMEM((4, FACES, 16, BLK), jnp.float32)
    field, coef, gain, matrix, *sent = call(
        lambda *refs: first_kernel(side, *refs),
        "first_edges",
        [whole, array(8, BLK), tile, array(3 * BLK, 2 * DEPTH * BLK, dtype=jnp.bfloat16)]
        + [strip] * 7,
        [field, wave_coef, visc_coef, stencil_start, stencil_offset],
        [
            pltpu.SMEM((LEV,), jnp.float32),
            pltpu.SMEM((LEV,), jnp.float32),
            pltpu.VMEM((DEPTH, BLK), jnp.int32),
            pltpu.VMEM((DEPTH, BLK), jnp.float32),
            tile_scratch,
            tile_scratch,
            strips,
            pltpu.SemaphoreType.DMA((FACES + 4,)),
        ],
        in_hbm=True,
    )
    adds = []
    for step in range(SUBSTEPS):
        last = step == SUBSTEPS - 1
        received = exchange(sent[:5], side)
        field, *edges = call(
            lambda *refs, first=step == 0, last=last: inner_kernel(first, last, *refs),
            "inner",
            [whole] + ([] if last else [tile] * 2),
            [field, coef, *adds],
            cost=2_000_000_000,
            aliases={0: 0},
        )
        adds_and_sent = call(
            lambda *refs, last=last: edge_kernel(side, last, *refs),
            "edges",
            [tile] * 2 + ([] if last else [strip] * 7),
            [*received, *sent[5:], matrix] + ([] if last else [gain, *edges]),
            [] if last else [tile_scratch, tile_scratch, strips],
        )
        adds, sent = adds_and_sent[:2], adds_and_sent[2:]
    (field,) = call(
        final_kernel,
        "final",
        [whole],
        [field, *adds],
        [pltpu.VMEM(field.shape, jnp.float32), pltpu.SemaphoreType.DMA((FACES,))],
        out_hbm=True,
    )
    return field[None]


def solution(mesh):
    placed = (P(("member", "tile"), None, None, None, None), P(), P(), P(), P())
    return jax.shard_map(
        on_device,
        mesh=mesh,
        in_specs=placed,
        out_specs=P(("member", "tile"), None, None, None, None),
        check_vma=False,
    )
```

```python
import math

import jax
import jax.numpy as jnp
from jax import lax
from jax.experimental import pallas as pl
from jax.experimental.pallas import tpu as pltpu
from jax.sharding import PartitionSpec as P

SUBSTEPS = 4
FACES = 6
LEV = 3
DEPTH = 3
BLK = 128
PER_FACE = LEV * DEPTH
ROWS = 56
HALF = 64
WEST, EAST, SOUTH, NORTH = 0, 1, 2, 3
SCALE = 20.0
VMEM_LIMIT = 16 * 1024 * 1024
FIRST_LIMIT = 60 * 1024 * 1024


def whole_vmem():
    return pl.BlockSpec(memory_space=pltpu.VMEM)


def iota(shape, dim):
    return lax.broadcasted_iota(jnp.int32, shape, dim)


def weight_of(distance):
    return jnp.where(
        distance == 1, 9.0, jnp.where(distance == 2, 7.0, jnp.where(distance == 3, 4.0, 0.0))
    )


def split2(x):
    high = x.astype(jnp.bfloat16)
    low = (x - high.astype(jnp.float32)).astype(jnp.bfloat16)
    return high, low


def lagrange_weights(t):
    return (
        -(t - 1.0) * (t - 2.0) * (t - 3.0) / 6.0,
        t * (t - 2.0) * (t - 3.0) / 2.0,
        -t * (t - 1.0) * (t - 3.0) / 2.0,
        t * (t - 1.0) * (t - 2.0) / 6.0,
    )


def band_matrix():
    gap = jnp.abs(iota((BLK, BLK), 0) - iota((BLK, BLK), 1))
    return jnp.where(gap == 0, -40.0, weight_of(gap)).astype(jnp.bfloat16)


def edge_matrix():
    shape = (BLK, BLK)
    to, src = iota(shape, 0), iota(shape, 1)
    lower = to < HALF
    to_row = jnp.where(lower, to, to - HALF)
    src_row = jnp.where(src < HALF, src, src - HALF)
    to_plane = (to_row * 171) >> 9
    src_plane = (src_row * 171) >> 9
    to_j = to_row - 3 * to_plane
    src_j = src_row - 3 * src_plane
    same = ((to < HALF) == (src < HALF)) & (to_plane == src_plane)
    distance = jnp.where(lower, 3 + to_j - src_j, 3 + src_j - to_j)
    return jnp.where(same, weight_of(distance), 0.0).astype(jnp.bfloat16)


def seam_matrices(starts, offsets, out_ref):
    j = iota((BLK, BLK), 0)
    back = BLK - 1 - j
    for h in range(DEPTH):
        first = starts[h : h + 1, :]
        weights = lagrange_weights(offsets[h : h + 1, :])
        for turned, place in ((0, j), (1, back)):
            matrix = jnp.zeros((BLK, BLK), jnp.float32)
            for m, weight in enumerate(weights):
                matrix = matrix + jnp.where(place == first + m, weight, 0.0)
            high, low = split2(matrix)
            at = (turned * DEPTH + h) * BLK
            out_ref[:BLK, at : at + BLK] = high
            out_ref[BLK : 2 * BLK, at : at + BLK] = high
            out_ref[2 * BLK :, at : at + BLK] = low


def position(side):
    index = lax.axis_index("tile")
    return lax.rem(index, side), lax.div(index, side)


def row_codes(shape):
    row = iota(shape, 0)
    block = (row * 57) >> 9
    odd = (block & 1) == 1
    depth = row - 3 * ((row * 171) >> 9)
    return odd, depth


def plane_row(shape, dim):
    row = iota(shape, dim)
    lower = row < HALF
    inside = jnp.where(lower, row, row - HALF)
    plane = (inside * 171) >> 9
    return lower, plane, inside - 3 * plane


def tiles_of(plane_value):
    return plane_value.reshape(BLK // 8, 8, BLK)


def lane_of_tile():
    return iota((1, 8, BLK), 2)


def take_edges(q, plane, columns, rows_ref):
    lane, at = lane_of_tile(), 6 * plane
    turned = pltpu.roll(q, (at + 3) % BLK, 2)
    columns = jnp.where((lane >= at) & (lane < at + 6), turned, columns)
    low, high = 3 * plane, HALF + 3 * plane
    rows_ref[low : low + 3, :] = q[0, :3, :]
    rows_ref[high : high + 3, :] = q[BLK // 8 - 1, 5:, :]
    return columns


def lane_order():
    lower, plane, cell = plane_row((BLK, BLK), 0)
    lane = 6 * plane + cell + jnp.where(lower, 3, 0)
    right = (lane == iota((BLK, BLK), 1)) & (plane < FACES * LEV)
    return jnp.where(right, 1.0, 0.0).astype(jnp.bfloat16)


def rows_from_columns(columns, order):
    high, low = split2(columns.reshape(BLK, BLK))
    return lax.dot_general(
        order,
        jnp.concatenate([high, low], axis=1),
        (((1,), (1,)), ((), ())),
        preferred_element_type=jnp.float32,
    )


def clear_rest(rows_ref):
    used = FACES * PER_FACE
    rest = jnp.zeros((HALF - used, BLK), jnp.float32)
    rows_ref[used:HALF, :] = rest
    rows_ref[HALF + used :, :] = rest


def pack(columns_ref, rows_ref, side, outs, strips_ref):
    turn_ref, far_ref, near_ref, mirror_ref, core_ref, own_a_ref, own_b_ref = outs
    col, row = position(side)
    for face in range(FACES):
        at = PER_FACE * face
        strips_ref[WEST, face, :PER_FACE, :] = columns_ref[at : at + PER_FACE, :]
        strips_ref[EAST, face, :PER_FACE, :] = columns_ref[HALF + at : HALF + at + PER_FACE, :]
        strips_ref[SOUTH, face, :PER_FACE, :] = rows_ref[at : at + PER_FACE, :]
        strips_ref[NORTH, face, :PER_FACE, :] = rows_ref[HALF + at : HALF + at + PER_FACE, :]
    even_col, even_row = lax.rem(col, 2) == 0, lax.rem(row, 2) == 0

    def shift(place):
        return jnp.where(place == 0, 1, jnp.where(place == side - 1, FACES - 1, 0))

    plans = (
        (core_ref, jnp.where(even_col, EAST, WEST), 0),
        (mirror_ref, jnp.where(even_col, WEST, EAST), shift(col)),
        (near_ref, jnp.where(even_row, NORTH, SOUTH), 0),
        (far_ref, jnp.where(even_row, SOUTH, NORTH), shift(row)),
    )
    rest = jnp.zeros((ROWS - FACES * PER_FACE, BLK), jnp.float32)
    for out_ref, which, by in plans:
        for face in range(FACES):
            at = PER_FACE * face
            source = face + by
            source = jnp.where(source >= FACES, source - FACES, source)
            out_ref[at : at + PER_FACE, :] = strips_ref[which, source, :PER_FACE, :]
        out_ref[FACES * PER_FACE :, :] = rest
    for face in range(FACES):
        at = PER_FACE * face
        if face % 2:
            a, b = (SOUTH, face + 2), (EAST, face - 2)
        else:
            a, b = (NORTH, face - 2), (WEST, face + 2)
        own_a_ref[at : at + PER_FACE, :] = strips_ref[a[0], a[1] % FACES, :PER_FACE, :]
        own_b_ref[at : at + PER_FACE, :] = strips_ref[b[0], b[1] % FACES, :PER_FACE, :]
    own_a_ref[FACES * PER_FACE :, :] = rest
    own_b_ref[FACES * PER_FACE :, :] = rest
    odd, _ = row_codes((ROWS, BLK))
    use_a = jnp.where(odd, (row == 0).astype(jnp.int32), (row == side - 1).astype(jnp.int32))
    turn_ref[...] = jnp.where(use_a == 1, own_a_ref[...], own_b_ref[...])


CONSTANTS = (
    ("coef", (8, BLK), jnp.float32),
    ("gain", (BLK, BLK), jnp.float32),
    ("matrix", (3 * BLK, 2 * DEPTH * BLK), jnp.bfloat16),
    ("edge", (BLK, 2 * BLK), jnp.bfloat16),
    ("fold", (2 * BLK, BLK), jnp.bfloat16),
    ("same", (BLK, BLK), jnp.float32),
    ("order", (BLK, 2 * BLK), jnp.bfloat16),
    ("spread", (2 * BLK, BLK), jnp.bfloat16),
    ("band_x", (2 * BLK, BLK), jnp.bfloat16),
    ("band_y", (BLK, 2 * BLK), jnp.bfloat16),
)


def make_constants(wave, visc, starts, offsets, refs):
    coef, gain, matrix, edge, fold, same, order, spread, band_x, band_y = refs
    seam_matrices(starts, offsets, matrix)
    _, plane, cell = plane_row((BLK, BLK), 0)
    lower, _, _ = plane_row((BLK, BLK), 0)
    _, plane_src, _ = plane_row((BLK, BLK), 1)
    level_of = plane - 3 * ((plane * 171) >> 9)
    total = jnp.zeros((BLK, BLK), jnp.float32)
    for level in range(LEV):
        a, b = wave[level] * (1.0 / SCALE), visc[level] * (1.0 / SCALE)
        coef[level : level + 1, :] = jnp.full((1, BLK), a, jnp.float32)
        coef[LEV + level : LEV + level + 1, :] = jnp.full((1, BLK), b, jnp.float32)
        total = jnp.where(level_of == level, a + b, total)
    coef[2 * LEV :, :] = jnp.zeros((8 - 2 * LEV, BLK), jnp.float32)
    gain[...] = total
    for ref, value, axis in (
        (edge, edge_matrix(), 1),
        (order, lane_order(), 1),
        (band_x, band_matrix(), 0),
        (band_y, band_matrix(), 1),
    ):
        ref[...] = jnp.concatenate([value, value], axis=axis)
    used = plane < FACES * LEV
    to = iota((BLK, BLK), 1)
    back = jnp.where(lower, cell, cell + BLK - 3)
    value = jnp.where((to == back) & used, 1.0, 0.0).astype(jnp.bfloat16)
    fold[...] = jnp.concatenate([value, value], axis=0)
    spread[...] = jnp.concatenate([lane_order()] * 2, axis=0)
    same[...] = jnp.where(plane == plane_src, 1.0, 0.0)


def first_kernel(side, state_hbm, wave_hbm, visc_hbm, *rest):
    outs = rest[:7]
    state_ref, wave, visc, columns_ref, rows_ref, strips_ref, sems = rest[7:]
    small = [
        pltpu.make_async_copy(wave_hbm, wave, sems.at[FACES]),
        pltpu.make_async_copy(visc_hbm, visc, sems.at[FACES + 1]),
    ]
    faces = [
        pltpu.make_async_copy(state_hbm.at[face], state_ref.at[face], sems.at[face])
        for face in range(FACES)
    ]
    for copy in small + faces:
        copy.start()
    clear_rest(rows_ref)
    for copy in small:
        copy.wait()
    columns = jnp.zeros((BLK // 8, 8, BLK), jnp.float32)
    for plane in range(FACES * LEV):
        face, level = divmod(plane, LEV)
        if level == 0:
            faces[face].wait()
        a, b = wave[level] * (1.0 / SCALE), visc[level] * (1.0 / SCALE)
        q = a * state_ref[face, level] + b * state_ref[face, LEV + level]
        columns = take_edges(tiles_of(q), plane, columns, rows_ref)
    order = lane_order()
    columns_ref[...] = rows_from_columns(columns, jnp.concatenate([order, order], axis=1))
    pack(columns_ref, rows_ref, side, outs, strips_ref)


def ghosts_of(side, received, own_a_ref, own_b_ref, matrix_ref):
    turned, far, near, mirror, core = [ref[...] for ref in received]
    col, row = position(side)
    even_col, even_row = lax.rem(col, 2) == 0, lax.rem(row, 2) == 0
    odd, depth = row_codes((ROWS, BLK))
    alone = ((row == 0) & (col == side - 1)) | ((col == 0) & (row == side - 1))
    pairs = (
        (
            jnp.where(even_col, mirror, core),
            jnp.where(even_col, core, mirror),
            jnp.where(alone, own_a_ref[...], turned),
            col,
            0,
        ),
        (
            jnp.where(even_row, far, near),
            jnp.where(even_row, near, far),
            jnp.where(alone, own_b_ref[...], turned),
            row,
            1,
        ),
    )
    seams, marks = [], []
    for low, high, crossed, place, low_turned in pairs:
        at_low = (place == 0).astype(jnp.int32)
        parity = at_low ^ (1 - low_turned)
        is_turned = odd.astype(jnp.int32) == parity
        seams.append(jnp.where(is_turned, crossed, jnp.where(place == 0, low, high)))
        marks.append((is_turned, jnp.where(place == 0, DEPTH - 1 - depth, depth)))
    first, second = split2(jnp.concatenate(seams, axis=0))
    mixed = jnp.dot(
        jnp.concatenate([first, second, first], axis=1),
        matrix_ref[...],
        preferred_element_type=jnp.float32,
    )
    rest = jnp.zeros((HALF - ROWS, BLK), jnp.float32)
    ghosts = []
    for index, (low, high, _, place, _) in enumerate(pairs):
        part = mixed[index * ROWS : (index + 1) * ROWS, :]
        is_turned, h_of = marks[index]
        made = jnp.zeros((ROWS, BLK), jnp.float32)
        for h in range(DEPTH):
            plain = part[:, h * BLK : (h + 1) * BLK]
            turn = part[:, (DEPTH + h) * BLK : (DEPTH + h + 1) * BLK]
            made = jnp.where(h_of == h, jnp.where(is_turned, turn, plain), made)
        ghosts.append(
            jnp.concatenate(
                [
                    jnp.where(place == 0, made, low),
                    rest,
                    jnp.where(place == side - 1, made, high),
                    rest,
                ],
                axis=0,
            )
        )
    return ghosts


def ghost_additions(side, received, own_a_ref, own_b_ref, matrix_ref, edge_ref):
    ghosts = ghosts_of(side, received, own_a_ref, own_b_ref, matrix_ref)
    high, low = split2(jnp.concatenate(ghosts, axis=1))
    adds = jnp.dot(
        edge_ref[...],
        jnp.concatenate([high, low], axis=0),
        preferred_element_type=jnp.float32,
    )
    return adds[:, :BLK], adds[:, BLK:]


def corner_part(adds_turned, same):
    cell = plane_row((HALF, BLK), 0)[2]
    halves = []
    for first in (0, BLK - 3):
        lines = [adds_turned[first + at : first + at + 1, :] for at in range(3)]
        halves.append(jnp.where(cell == 0, lines[0], jnp.where(cell == 1, lines[1], lines[2])))
    return split2(jnp.concatenate(halves, axis=0) * same)


def edge_kernel(side, *refs):
    add_x, add_y = ghost_additions(side, refs[:5], *refs[5:9])
    fold_ref, same_ref, gain_ref, old_columns_ref, old_rows_ref = refs[9:14]
    add_x_ref, add_y_ref = refs[14:16]
    outs = refs[16:23]
    columns_ref, rows_ref, strips_ref = refs[23:]
    turned_x, turned_y = add_x.T, add_y.T
    add_x_ref[...] = turned_x
    add_y_ref[...] = add_y
    same = same_ref[...]
    corners = jnp.dot(
        jnp.concatenate(
            [
                jnp.concatenate(corner_part(turned_y, same), axis=1),
                jnp.concatenate(corner_part(turned_x, same), axis=1),
            ],
            axis=0,
        ),
        fold_ref[...],
        preferred_element_type=jnp.float32,
    )
    gain = gain_ref[...]
    columns_ref[...] = old_columns_ref[...] + gain * (add_x + corners[:BLK])
    rows_ref[...] = old_rows_ref[...] + gain * (add_y + corners[BLK:])
    pack(columns_ref, rows_ref, side, outs, strips_ref)


def spread_lanes(turned_x, spread_ref):
    high, low = split2(turned_x)
    return tiles_of(
        jnp.dot(
            jnp.concatenate([high, low], axis=1),
            spread_ref[...],
            preferred_element_type=jnp.float32,
        )
    )


def edge_additions(plane, add_x, add_y):
    lane = lane_of_tile()
    turned = pltpu.roll(add_x, (BLK - 3 - 6 * plane) % BLK, 2)
    add = jnp.where((lane < 3) | (lane >= BLK - 3), turned, 0.0)
    at = 3 * plane
    pad = jnp.zeros((5, BLK), jnp.float32)
    bottom = add[:1] + jnp.concatenate([add_y[at : at + 3], pad], axis=0)[None]
    top = add[-1:] + jnp.concatenate([pad, add_y[HALF + at : HALF + at + 3]], axis=0)[None]
    return jnp.concatenate([bottom, add[1:-1], top], axis=0)


def inner_kernel(first, last, state_ref, *refs):
    if first:
        wave, visc, starts, offsets = refs[:4]
        new_ref, columns_ref, rows_ref = refs[4:7]
        made = refs[7:]
        make_constants(wave, visc, starts[...], offsets[...], made)
        coef_ref, band_x_ref, band_y_ref, order_ref = made[0], made[8], made[9], made[6]
    else:
        coef_ref, band_x_ref, band_y_ref, order_ref, spread_ref = refs[:5]
        add_x_ref, add_y_ref = refs[5:7]
        new_ref = refs[7]
        add_x, add_y = spread_lanes(add_x_ref[...], spread_ref), add_y_ref[...]
        if not last:
            columns_ref, rows_ref = refs[8:]
    if not last:
        clear_rest(rows_ref)
    columns = jnp.zeros((BLK // 8, 8, BLK), jnp.float32)
    group = 2
    for begin in range(0, FACES * LEV, group):
        fields, highs, lows = [], [], []
        for plane in range(begin, begin + group):
            face, level = divmod(plane, LEV)
            a, b = coef_ref[level : level + 1, :], coef_ref[LEV + level : LEV + level + 1, :]
            pressure = tiles_of(state_ref[face, level])
            rate = tiles_of(state_ref[face, LEV + level])
            if not first:
                add = edge_additions(plane, add_x, add_y)
                pressure, rate = pressure + add, rate + add
            high, low = split2((a * pressure + b * rate).reshape(BLK, BLK))
            fields.append((pressure, rate))
            highs.append(high)
            lows.append(low)
        by_x = jnp.dot(
            jnp.concatenate(
                [jnp.concatenate(pair, axis=1) for pair in zip(highs, lows)], axis=0
            ),
            band_x_ref[...],
            preferred_element_type=jnp.float32,
        )
        by_y = jnp.dot(
            band_y_ref[...],
            jnp.concatenate(
                [jnp.concatenate(highs, axis=1), jnp.concatenate(lows, axis=1)], axis=0
            ),
            preferred_element_type=jnp.float32,
        )
        for place, (pressure, rate) in enumerate(fields):
            plane = begin + place
            face, level = divmod(plane, LEV)
            a, b = coef_ref[level : level + 1, :], coef_ref[LEV + level : LEV + level + 1, :]
            at = place * BLK
            rate = rate + tiles_of(by_x[at : at + BLK, :] + by_y[:, at : at + BLK])
            pressure = pressure + rate
            new_ref[face, level] = pressure.reshape(BLK, BLK)
            new_ref[face, LEV + level] = rate.reshape(BLK, BLK)
            if not last:
                columns = take_edges(a * pressure + b * rate, plane, columns, rows_ref)
    if not last:
        columns_ref[...] = rows_from_columns(columns, order_ref[...])


def final_kernel(side, *refs):
    add_x, add_y = ghost_additions(side, refs[:5], *refs[5:9])
    spread_ref, state_ref, out_hbm, buffer, sems = refs[9:]
    add_x = spread_lanes(add_x.T, spread_ref)
    copies = []
    for face in range(FACES):
        for level in range(LEV):
            add = edge_additions(face * LEV + level, add_x, add_y)
            for channel in (level, LEV + level):
                value = tiles_of(state_ref[face, channel]) + add
                buffer[face, channel] = value.reshape(BLK, BLK)
        copy = pltpu.make_async_copy(buffer.at[face], out_hbm.at[face], sems.at[face])
        copy.start()
        copies.append(copy)
    for copy in copies:
        copy.wait()


def exchange(payloads, side):
    def at(row, col):
        return row * side + col

    cells = [(row, col) for row in range(side) for col in range(side)]

    def swap(place, odd_first):
        return (place ^ 1) if not odd_first else (place + (1 if place % 2 else -1)) % side

    core = [(at(r, c), at(r, swap(c, False))) for r, c in cells]
    mirror = [(at(r, c), at(r, swap(c, True))) for r, c in cells]
    near = [(at(r, c), at(swap(r, False), c)) for r, c in cells]
    far = [(at(r, c), at(swap(r, True), c)) for r, c in cells]
    edge = side - 1
    turn = set()
    for x in range(edge):
        turn |= {(at(0, x), at(edge - x, edge)), (at(edge - x, edge), at(0, x))}
    for x in range(1, side):
        turn |= {(at(edge, x), at(edge - x, 0)), (at(edge - x, 0), at(edge, x))}
    turn_out, far_out, near_out, mirror_out, core_out = payloads
    turn_in = lax.ppermute(turn_out, "tile", sorted(turn))
    far_in = lax.ppermute(far_out, "tile", far)
    near_in = lax.ppermute(near_out, "tile", near)
    mirror_in = lax.ppermute(mirror_out, "tile", mirror)
    core_in = lax.ppermute(core_out, "tile", core)
    return turn_in, far_in, near_in, mirror_in, core_in


def call(
    kernel,
    name,
    outs,
    ins,
    scratch=(),
    scalars=(),
    out_hbm=False,
    in_hbm=False,
    limit=VMEM_LIMIT,
    cost=0,
    aliases=None,
):
    hbm = pl.BlockSpec(memory_space=pltpu.HBM)
    vmem = pl.BlockSpec(memory_space=pltpu.VMEM)
    smem = pl.BlockSpec(memory_space=pltpu.SMEM)
    in_specs = [hbm if in_hbm else smem if at in scalars else vmem for at in range(len(ins))]
    return pl.pallas_call(
        kernel,
        out_shape=outs,
        in_specs=in_specs,
        out_specs=[hbm if out_hbm else vmem] * len(outs),
        scratch_shapes=list(scratch),
        compiler_params=pltpu.CompilerParams(vmem_limit_bytes=limit),
        cost_estimate=pl.CostEstimate(flops=cost, bytes_accessed=cost // 500, transcendentals=0),
        input_output_aliases=aliases or {},
        name=name,
    )(*ins)


def on_device(state, wave_coef, visc_coef, stencil_start, stencil_offset):
    side = math.isqrt(lax.axis_size("tile"))
    field = state[0]

    def array(*shape, dtype=jnp.float32):
        return jax.ShapeDtypeStruct(shape, dtype)

    tile = array(BLK, BLK)
    strip = array(ROWS, BLK)
    whole = array(*field.shape)
    work = [
        pltpu.VMEM((BLK, BLK), jnp.float32),
        pltpu.VMEM((BLK, BLK), jnp.float32),
        pltpu.VMEM((4, FACES, 16, BLK), jnp.float32),
    ]
    scalars = pltpu.SMEM((LEV,), jnp.float32)
    sent = call(
        lambda *refs: first_kernel(side, *refs),
        "first_edges",
        [strip] * 7,
        [field, wave_coef, visc_coef],
        [
            pltpu.VMEM(field.shape, jnp.float32),
            scalars,
            scalars,
            *work,
            pltpu.SemaphoreType.DMA((FACES + 2,)),
        ],
        in_hbm=True,
        limit=FIRST_LIMIT,
        cost=1_000_000_000,
    )
    made = {}
    adds = []
    for step in range(SUBSTEPS):
        first, last = step == 0, step == SUBSTEPS - 1
        received = exchange(sent[:5], side)

        def inner(*refs, first=first, last=last):
            inner_kernel(first, last, *refs)

        if first:
            field, *rest = call(
                inner,
                "inner",
                [whole] + [tile] * 2 + [array(*shape, dtype=kind) for _, shape, kind in CONSTANTS],
                [field, wave_coef, visc_coef, stencil_start, stencil_offset],
                scalars=(1, 2),
                cost=2_000_000_000,
            )
            edges = rest[:2]
            made = dict(zip((name for name, _, _ in CONSTANTS), rest[2:]))
        else:
            names = ("coef", "band_x", "band_y", "order", "spread")
            field, *edges = call(
                inner,
                "inner",
                [whole] + ([] if last else [tile] * 2),
                [field, *(made[name] for name in names), *adds],
                cost=2_000_000_000,
                aliases={0: 0},
            )
        ghosts = [*received, *sent[5:], made["matrix"], made["edge"]]
        if last:
            break
        updates = call(
            lambda *refs: edge_kernel(side, *refs),
            "edges",
            [tile] * 2 + [strip] * 7,
            [*ghosts, made["fold"], made["same"], made["gain"], *edges],
            work,
        )
        adds, sent = updates[:2], updates[2:]
    (field,) = call(
        lambda *refs: final_kernel(side, *refs),
        "final",
        [whole],
        [*ghosts, made["spread"], field],
        [pltpu.VMEM(field.shape, jnp.float32), pltpu.SemaphoreType.DMA((FACES,))],
        out_hbm=True,
    )
    return field[None]


def solution(mesh):
    placed = (P(("member", "tile"), None, None, None, None), P(), P(), P(), P())
    return jax.shard_map(
        on_device,
        mesh=mesh,
        in_specs=placed,
        out_specs=P(("member", "tile"), None, None, None, None),
        check_vma=False,
    )
```

```python
import math

import jax
import jax.numpy as jnp
from jax import lax
from jax.experimental import pallas as pl
from jax.experimental.pallas import tpu as pltpu
from jax.sharding import PartitionSpec as P

SUBSTEPS = 4
FACES = 6
LEV = 3
DEPTH = 3
BLK = 128
PER_FACE = LEV * DEPTH
ROWS = 56
HALF = 64
WEST, EAST, SOUTH, NORTH = 0, 1, 2, 3
SCALE = 20.0
VMEM_LIMIT = 16 * 1024 * 1024
FIRST_LIMIT = 60 * 1024 * 1024


def whole_vmem():
    return pl.BlockSpec(memory_space=pltpu.VMEM)


def iota(shape, dim):
    return lax.broadcasted_iota(jnp.int32, shape, dim)


def weight_of(distance):
    return jnp.where(
        distance == 1, 9.0, jnp.where(distance == 2, 7.0, jnp.where(distance == 3, 4.0, 0.0))
    )


def split2(x):
    high = x.astype(jnp.bfloat16)
    low = (x - high.astype(jnp.float32)).astype(jnp.bfloat16)
    return high, low


def lagrange_weights(t):
    return (
        -(t - 1.0) * (t - 2.0) * (t - 3.0) / 6.0,
        t * (t - 2.0) * (t - 3.0) / 2.0,
        -t * (t - 1.0) * (t - 3.0) / 2.0,
        t * (t - 1.0) * (t - 2.0) / 6.0,
    )


def band_matrix():
    gap = jnp.abs(iota((BLK, BLK), 0) - iota((BLK, BLK), 1))
    return jnp.where(gap == 0, -40.0, weight_of(gap)).astype(jnp.bfloat16)


def edge_matrix():
    shape = (BLK, BLK)
    to, src = iota(shape, 0), iota(shape, 1)
    lower = to < HALF
    to_row = jnp.where(lower, to, to - HALF)
    src_row = jnp.where(src < HALF, src, src - HALF)
    to_plane = (to_row * 171) >> 9
    src_plane = (src_row * 171) >> 9
    to_j = to_row - 3 * to_plane
    src_j = src_row - 3 * src_plane
    same = ((to < HALF) == (src < HALF)) & (to_plane == src_plane)
    distance = jnp.where(lower, 3 + to_j - src_j, 3 + src_j - to_j)
    return jnp.where(same, weight_of(distance), 0.0).astype(jnp.bfloat16)


def seam_matrices(starts, offsets, out_ref):
    j = iota((BLK, BLK), 0)
    back = BLK - 1 - j
    for h in range(DEPTH):
        first = starts[h : h + 1, :]
        weights = lagrange_weights(offsets[h : h + 1, :])
        for turned, place in ((0, j), (1, back)):
            matrix = jnp.zeros((BLK, BLK), jnp.float32)
            for m, weight in enumerate(weights):
                matrix = matrix + jnp.where(place == first + m, weight, 0.0)
            high, low = split2(matrix)
            at = (turned * DEPTH + h) * BLK
            out_ref[:BLK, at : at + BLK] = high
            out_ref[BLK : 2 * BLK, at : at + BLK] = high
            out_ref[2 * BLK :, at : at + BLK] = low


def position(side):
    index = lax.axis_index("tile")
    return lax.rem(index, side), lax.div(index, side)


def is_inner(row, col, side):
    return 0 < row < side - 1 and 0 < col < side - 1


def row_codes(shape):
    row = iota(shape, 0)
    block = (row * 57) >> 9
    odd = (block & 1) == 1
    depth = row - 3 * ((row * 171) >> 9)
    return odd, depth


def plane_row(shape, dim):
    row = iota(shape, dim)
    lower = row < HALF
    inside = jnp.where(lower, row, row - HALF)
    plane = (inside * 171) >> 9
    return lower, plane, inside - 3 * plane


def tiles_of(plane_value):
    return plane_value.reshape(BLK // 8, 8, BLK)


def lane_of_tile():
    return iota((1, 8, BLK), 2)


def take_edges(q, plane, columns, rows_ref):
    lane, at = lane_of_tile(), 6 * plane
    turned = pltpu.roll(q, (at + 3) % BLK, 2)
    columns = jnp.where((lane >= at) & (lane < at + 6), turned, columns)
    low, high = 3 * plane, HALF + 3 * plane
    rows_ref[low : low + 3, :] = q[0, :3, :]
    rows_ref[high : high + 3, :] = q[BLK // 8 - 1, 5:, :]
    return columns


def lane_order():
    lower, plane, cell = plane_row((BLK, BLK), 0)
    lane = 6 * plane + cell + jnp.where(lower, 3, 0)
    right = (lane == iota((BLK, BLK), 1)) & (plane < FACES * LEV)
    return jnp.where(right, 1.0, 0.0).astype(jnp.bfloat16)


def rows_from_columns(columns, order):
    high, low = split2(columns.reshape(BLK, BLK))
    return lax.dot_general(
        order,
        jnp.concatenate([high, low], axis=1),
        (((1,), (1,)), ((), ())),
        preferred_element_type=jnp.float32,
    )


def clear_rest(rows_ref):
    used = FACES * PER_FACE
    rest = jnp.zeros((HALF - used, BLK), jnp.float32)
    rows_ref[used:HALF, :] = rest
    rows_ref[HALF + used :, :] = rest


def pack(columns_ref, rows_ref, side, outs, strips_ref):
    turn_ref, far_ref, near_ref, mirror_ref, core_ref, own_a_ref, own_b_ref = outs
    col, row = position(side)
    for face in range(FACES):
        at = PER_FACE * face
        strips_ref[WEST, face, :PER_FACE, :] = columns_ref[at : at + PER_FACE, :]
        strips_ref[EAST, face, :PER_FACE, :] = columns_ref[HALF + at : HALF + at + PER_FACE, :]
        strips_ref[SOUTH, face, :PER_FACE, :] = rows_ref[at : at + PER_FACE, :]
        strips_ref[NORTH, face, :PER_FACE, :] = rows_ref[HALF + at : HALF + at + PER_FACE, :]
    even_col, even_row = lax.rem(col, 2) == 0, lax.rem(row, 2) == 0

    def shift(place):
        return jnp.where(place == 0, 1, jnp.where(place == side - 1, FACES - 1, 0))

    plans = (
        (core_ref, jnp.where(even_col, EAST, WEST), 0),
        (mirror_ref, jnp.where(even_col, WEST, EAST), shift(col)),
        (near_ref, jnp.where(even_row, NORTH, SOUTH), 0),
        (far_ref, jnp.where(even_row, SOUTH, NORTH), shift(row)),
    )
    rest = jnp.zeros((ROWS - FACES * PER_FACE, BLK), jnp.float32)
    for out_ref, which, by in plans:
        for face in range(FACES):
            at = PER_FACE * face
            source = face + by
            source = jnp.where(source >= FACES, source - FACES, source)
            out_ref[at : at + PER_FACE, :] = strips_ref[which, source, :PER_FACE, :]
        out_ref[FACES * PER_FACE :, :] = rest
    for face in range(FACES):
        at = PER_FACE * face
        if face % 2:
            a, b = (SOUTH, face + 2), (EAST, face - 2)
        else:
            a, b = (NORTH, face - 2), (WEST, face + 2)
        own_a_ref[at : at + PER_FACE, :] = strips_ref[a[0], a[1] % FACES, :PER_FACE, :]
        own_b_ref[at : at + PER_FACE, :] = strips_ref[b[0], b[1] % FACES, :PER_FACE, :]
    own_a_ref[FACES * PER_FACE :, :] = rest
    own_b_ref[FACES * PER_FACE :, :] = rest
    odd, _ = row_codes((ROWS, BLK))
    use_a = jnp.where(odd, (row == 0).astype(jnp.int32), (row == side - 1).astype(jnp.int32))
    turn_ref[...] = jnp.where(use_a == 1, own_a_ref[...], own_b_ref[...])


CONSTANTS = (
    ("coef", (8, BLK), jnp.float32),
    ("gain", (BLK, BLK), jnp.float32),
    ("matrix", (3 * BLK, 2 * DEPTH * BLK), jnp.bfloat16),
    ("edge", (BLK, 2 * BLK), jnp.bfloat16),
    ("fold", (2 * BLK, BLK), jnp.bfloat16),
    ("same", (BLK, BLK), jnp.float32),
    ("order", (BLK, 2 * BLK), jnp.bfloat16),
    ("spread", (2 * BLK, BLK), jnp.bfloat16),
    ("band_x", (2 * BLK, BLK), jnp.bfloat16),
    ("band_y", (BLK, 2 * BLK), jnp.bfloat16),
)


def make_constants(wave, visc, starts, offsets, refs):
    coef, gain, matrix, edge, fold, same, order, spread, band_x, band_y = refs
    seam_matrices(starts, offsets, matrix)
    _, plane, cell = plane_row((BLK, BLK), 0)
    lower, _, _ = plane_row((BLK, BLK), 0)
    _, plane_src, _ = plane_row((BLK, BLK), 1)
    level_of = plane - 3 * ((plane * 171) >> 9)
    total = jnp.zeros((BLK, BLK), jnp.float32)
    for level in range(LEV):
        a, b = wave[level] * (1.0 / SCALE), visc[level] * (1.0 / SCALE)
        coef[level : level + 1, :] = jnp.full((1, BLK), a, jnp.float32)
        coef[LEV + level : LEV + level + 1, :] = jnp.full((1, BLK), b, jnp.float32)
        total = jnp.where(level_of == level, a + b, total)
    coef[2 * LEV :, :] = jnp.zeros((8 - 2 * LEV, BLK), jnp.float32)
    gain[...] = total
    for ref, value, axis in (
        (edge, edge_matrix(), 1),
        (order, lane_order(), 1),
        (band_x, band_matrix(), 0),
        (band_y, band_matrix(), 1),
    ):
        ref[...] = jnp.concatenate([value, value], axis=axis)
    used = plane < FACES * LEV
    to = iota((BLK, BLK), 1)
    back = jnp.where(lower, cell, cell + BLK - 3)
    value = jnp.where((to == back) & used, 1.0, 0.0).astype(jnp.bfloat16)
    fold[...] = jnp.concatenate([value, value], axis=0)
    spread[...] = jnp.concatenate([lane_order()] * 2, axis=0)
    same[...] = jnp.where(plane == plane_src, 1.0, 0.0)


def first_kernel(side, state_hbm, wave_hbm, visc_hbm, *rest):
    outs = rest[:7]
    state_ref, wave, visc, columns_ref, rows_ref, strips_ref, sems = rest[7:]
    small = [
        pltpu.make_async_copy(wave_hbm, wave, sems.at[FACES]),
        pltpu.make_async_copy(visc_hbm, visc, sems.at[FACES + 1]),
    ]
    faces = [
        pltpu.make_async_copy(state_hbm.at[face], state_ref.at[face], sems.at[face])
        for face in range(FACES)
    ]
    for copy in small + faces:
        copy.start()
    clear_rest(rows_ref)
    for copy in small:
        copy.wait()
    columns = jnp.zeros((BLK // 8, 8, BLK), jnp.float32)
    for plane in range(FACES * LEV):
        face, level = divmod(plane, LEV)
        if level == 0:
            faces[face].wait()
        a, b = wave[level] * (1.0 / SCALE), visc[level] * (1.0 / SCALE)
        q = a * state_ref[face, level] + b * state_ref[face, LEV + level]
        columns = take_edges(tiles_of(q), plane, columns, rows_ref)
    order = lane_order()
    columns_ref[...] = rows_from_columns(columns, jnp.concatenate([order, order], axis=1))
    pack(columns_ref, rows_ref, side, outs, strips_ref)


def ghosts_of(side, received, own_a_ref, own_b_ref, matrix_ref):
    turned, far, near, mirror, core = [ref[...] for ref in received]
    col, row = position(side)
    even_col, even_row = lax.rem(col, 2) == 0, lax.rem(row, 2) == 0
    odd, depth = row_codes((ROWS, BLK))
    alone = ((row == 0) & (col == side - 1)) | ((col == 0) & (row == side - 1))
    pairs = (
        (
            jnp.where(even_col, mirror, core),
            jnp.where(even_col, core, mirror),
            jnp.where(alone, own_a_ref[...], turned),
            col,
            0,
        ),
        (
            jnp.where(even_row, far, near),
            jnp.where(even_row, near, far),
            jnp.where(alone, own_b_ref[...], turned),
            row,
            1,
        ),
    )
    seams, marks = [], []
    for low, high, crossed, place, low_turned in pairs:
        at_low = (place == 0).astype(jnp.int32)
        parity = at_low ^ (1 - low_turned)
        is_turned = odd.astype(jnp.int32) == parity
        seams.append(jnp.where(is_turned, crossed, jnp.where(place == 0, low, high)))
        marks.append((is_turned, jnp.where(place == 0, DEPTH - 1 - depth, depth)))
    first, second = split2(jnp.concatenate(seams, axis=0))
    mixed = jnp.dot(
        jnp.concatenate([first, second, first], axis=1),
        matrix_ref[...],
        preferred_element_type=jnp.float32,
    )
    rest = jnp.zeros((HALF - ROWS, BLK), jnp.float32)
    ghosts = []
    for index, (low, high, _, place, _) in enumerate(pairs):
        part = mixed[index * ROWS : (index + 1) * ROWS, :]
        is_turned, h_of = marks[index]
        made = jnp.zeros((ROWS, BLK), jnp.float32)
        for h in range(DEPTH):
            plain = part[:, h * BLK : (h + 1) * BLK]
            turn = part[:, (DEPTH + h) * BLK : (DEPTH + h + 1) * BLK]
            made = jnp.where(h_of == h, jnp.where(is_turned, turn, plain), made)
        ghosts.append(
            jnp.concatenate(
                [
                    jnp.where(place == 0, made, low),
                    rest,
                    jnp.where(place == side - 1, made, high),
                    rest,
                ],
                axis=0,
            )
        )
    return ghosts


def ghost_additions(side, received, own_a_ref, own_b_ref, matrix_ref, edge_ref):
    ghosts = ghosts_of(side, received, own_a_ref, own_b_ref, matrix_ref)
    high, low = split2(jnp.concatenate(ghosts, axis=1))
    adds = jnp.dot(
        edge_ref[...],
        jnp.concatenate([high, low], axis=0),
        preferred_element_type=jnp.float32,
    )
    return adds[:, :BLK], adds[:, BLK:]


def corner_part(adds_turned, same):
    cell = plane_row((HALF, BLK), 0)[2]
    halves = []
    for first in (0, BLK - 3):
        lines = [adds_turned[first + at : first + at + 1, :] for at in range(3)]
        halves.append(jnp.where(cell == 0, lines[0], jnp.where(cell == 1, lines[1], lines[2])))
    return split2(jnp.concatenate(halves, axis=0) * same)


def edge_kernel(side, *refs):
    add_x, add_y = ghost_additions(side, refs[:5], *refs[5:9])
    fold_ref, same_ref, gain_ref, old_columns_ref, old_rows_ref = refs[9:14]
    add_x_ref, add_y_ref = refs[14:16]
    outs = refs[16:23]
    columns_ref, rows_ref, strips_ref = refs[23:]
    turned_x, turned_y = add_x.T, add_y.T
    add_x_ref[...] = turned_x
    add_y_ref[...] = add_y
    same = same_ref[...]
    corners = jnp.dot(
        jnp.concatenate(
            [
                jnp.concatenate(corner_part(turned_y, same), axis=1),
                jnp.concatenate(corner_part(turned_x, same), axis=1),
            ],
            axis=0,
        ),
        fold_ref[...],
        preferred_element_type=jnp.float32,
    )
    gain = gain_ref[...]
    columns_ref[...] = old_columns_ref[...] + gain * (add_x + corners[:BLK])
    rows_ref[...] = old_rows_ref[...] + gain * (add_y + corners[BLK:])
    pack(columns_ref, rows_ref, side, outs, strips_ref)


def spread_lanes(turned_x, spread_ref):
    high, low = split2(turned_x)
    return tiles_of(
        jnp.dot(
            jnp.concatenate([high, low], axis=1),
            spread_ref[...],
            preferred_element_type=jnp.float32,
        )
    )


def edge_additions(plane, add_x, add_y):
    lane = lane_of_tile()
    turned = pltpu.roll(add_x, (BLK - 3 - 6 * plane) % BLK, 2)
    add = jnp.where((lane < 3) | (lane >= BLK - 3), turned, 0.0)
    at = 3 * plane
    pad = jnp.zeros((5, BLK), jnp.float32)
    bottom = add[:1] + jnp.concatenate([add_y[at : at + 3], pad], axis=0)[None]
    top = add[-1:] + jnp.concatenate([pad, add_y[HALF + at : HALF + at + 3]], axis=0)[None]
    return jnp.concatenate([bottom, add[1:-1], top], axis=0)


def inner_kernel(first, last, state_ref, *refs):
    if first:
        wave, visc, starts, offsets = refs[:4]
        new_ref, columns_ref, rows_ref = refs[4:7]
        made = refs[7:]
        make_constants(wave, visc, starts[...], offsets[...], made)
        coef_ref, band_x_ref, band_y_ref, order_ref = made[0], made[8], made[9], made[6]
    else:
        coef_ref, band_x_ref, band_y_ref, order_ref, spread_ref = refs[:5]
        add_x_ref, add_y_ref = refs[5:7]
        new_ref = refs[7]
        add_x, add_y = spread_lanes(add_x_ref[...], spread_ref), add_y_ref[...]
        if not last:
            columns_ref, rows_ref = refs[8:]
    if not last:
        clear_rest(rows_ref)
    columns = jnp.zeros((BLK // 8, 8, BLK), jnp.float32)
    group = 2
    for begin in range(0, FACES * LEV, group):
        fields, highs, lows = [], [], []
        for plane in range(begin, begin + group):
            face, level = divmod(plane, LEV)
            a, b = coef_ref[level : level + 1, :], coef_ref[LEV + level : LEV + level + 1, :]
            pressure = tiles_of(state_ref[face, level])
            rate = tiles_of(state_ref[face, LEV + level])
            if not first:
                add = edge_additions(plane, add_x, add_y)
                pressure, rate = pressure + add, rate + add
            high, low = split2((a * pressure + b * rate).reshape(BLK, BLK))
            fields.append((pressure, rate))
            highs.append(high)
            lows.append(low)
        by_x = jnp.dot(
            jnp.concatenate(
                [jnp.concatenate(pair, axis=1) for pair in zip(highs, lows)], axis=0
            ),
            band_x_ref[...],
            preferred_element_type=jnp.float32,
        )
        by_y = jnp.dot(
            band_y_ref[...],
            jnp.concatenate(
                [jnp.concatenate(highs, axis=1), jnp.concatenate(lows, axis=1)], axis=0
            ),
            preferred_element_type=jnp.float32,
        )
        for place, (pressure, rate) in enumerate(fields):
            plane = begin + place
            face, level = divmod(plane, LEV)
            a, b = coef_ref[level : level + 1, :], coef_ref[LEV + level : LEV + level + 1, :]
            at = place * BLK
            rate = rate + tiles_of(by_x[at : at + BLK, :] + by_y[:, at : at + BLK])
            pressure = pressure + rate
            new_ref[face, level] = pressure.reshape(BLK, BLK)
            new_ref[face, LEV + level] = rate.reshape(BLK, BLK)
            if not last:
                columns = take_edges(a * pressure + b * rate, plane, columns, rows_ref)
    if not last:
        columns_ref[...] = rows_from_columns(columns, order_ref[...])


def final_kernel(side, *refs):
    add_x, add_y = ghost_additions(side, refs[:5], *refs[5:9])
    spread_ref, state_ref, out_hbm, buffer, sems = refs[9:]
    add_x = spread_lanes(add_x.T, spread_ref)
    copies = []
    for face in range(FACES):
        for level in range(LEV):
            add = edge_additions(face * LEV + level, add_x, add_y)
            for channel in (level, LEV + level):
                value = tiles_of(state_ref[face, channel]) + add
                buffer[face, channel] = value.reshape(BLK, BLK)
        copy = pltpu.make_async_copy(buffer.at[face], out_hbm.at[face], sems.at[face])
        copy.start()
        copies.append(copy)
    for copy in copies:
        copy.wait()


def exchange(payloads, side):
    def at(row, col):
        return row * side + col

    cells = [(row, col) for row in range(side) for col in range(side)]

    def swap(place, odd_first):
        return (place ^ 1) if not odd_first else (place + (1 if place % 2 else -1)) % side

    core = [(at(r, c), at(r, swap(c, False))) for r, c in cells]
    mirror = [(at(r, c), at(r, swap(c, True))) for r, c in cells]
    near = [(at(r, c), at(swap(r, False), c)) for r, c in cells]
    far = [(at(r, c), at(swap(r, True), c)) for r, c in cells]
    edge = side - 1
    turn = set()
    for x in range(edge):
        turn |= {(at(0, x), at(edge - x, edge)), (at(edge - x, edge), at(0, x))}
    for x in range(1, side):
        turn |= {(at(edge, x), at(edge - x, 0)), (at(edge - x, 0), at(edge, x))}
    spare = [pair for pair in mirror if is_inner(pair[0] // side, pair[0] % side, side)]
    first_end, last_end = at(1, edge - 1), at(edge - 1, 1)
    left = [b for a, b in spare if a in (first_end, last_end)]
    spare = [pair for pair in spare if not {*pair} & {first_end, last_end}]
    spare += [(at(0, edge), first_end), (at(edge, 0), last_end), (left[0], left[1])]
    turn |= {(a, b) for a, b in spare} | {(b, a) for a, b in spare}
    turn_out, far_out, near_out, mirror_out, core_out = payloads
    turn_in = lax.ppermute(turn_out, "tile", sorted(turn))
    far_in = lax.ppermute(far_out, "tile", far)
    near_in = lax.ppermute(near_out, "tile", near)
    mirror_in = lax.ppermute(mirror_out, "tile", mirror)
    core_in = lax.ppermute(core_out, "tile", core)
    return turn_in, far_in, near_in, mirror_in, core_in


def call(
    kernel,
    name,
    outs,
    ins,
    scratch=(),
    scalars=(),
    out_hbm=False,
    in_hbm=False,
    limit=VMEM_LIMIT,
    cost=0,
    aliases=None,
):
    hbm = pl.BlockSpec(memory_space=pltpu.HBM)
    vmem = pl.BlockSpec(memory_space=pltpu.VMEM)
    smem = pl.BlockSpec(memory_space=pltpu.SMEM)
    in_specs = [hbm if in_hbm else smem if at in scalars else vmem for at in range(len(ins))]
    return pl.pallas_call(
        kernel,
        out_shape=outs,
        in_specs=in_specs,
        out_specs=[hbm if out_hbm else vmem] * len(outs),
        scratch_shapes=list(scratch),
        compiler_params=pltpu.CompilerParams(vmem_limit_bytes=limit),
        cost_estimate=pl.CostEstimate(flops=cost, bytes_accessed=cost // 500, transcendentals=0),
        input_output_aliases=aliases or {},
        name=name,
    )(*ins)


def on_device(state, wave_coef, visc_coef, stencil_start, stencil_offset):
    side = math.isqrt(lax.axis_size("tile"))
    field = state[0]

    def array(*shape, dtype=jnp.float32):
        return jax.ShapeDtypeStruct(shape, dtype)

    tile = array(BLK, BLK)
    strip = array(ROWS, BLK)
    whole = array(*field.shape)
    work = [
        pltpu.VMEM((BLK, BLK), jnp.float32),
        pltpu.VMEM((BLK, BLK), jnp.float32),
        pltpu.VMEM((4, FACES, 16, BLK), jnp.float32),
    ]
    scalars = pltpu.SMEM((LEV,), jnp.float32)
    sent = call(
        lambda *refs: first_kernel(side, *refs),
        "first_edges",
        [strip] * 7,
        [field, wave_coef, visc_coef],
        [
            pltpu.VMEM(field.shape, jnp.float32),
            scalars,
            scalars,
            *work,
            pltpu.SemaphoreType.DMA((FACES + 2,)),
        ],
        in_hbm=True,
        limit=FIRST_LIMIT,
        cost=1_000_000_000,
    )
    made = {}
    adds = []
    for step in range(SUBSTEPS):
        first, last = step == 0, step == SUBSTEPS - 1
        received = exchange(sent[:5], side)

        def inner(*refs, first=first, last=last):
            inner_kernel(first, last, *refs)

        if first:
            field, *rest = call(
                inner,
                "inner",
                [whole] + [tile] * 2 + [array(*shape, dtype=kind) for _, shape, kind in CONSTANTS],
                [field, wave_coef, visc_coef, stencil_start, stencil_offset],
                scalars=(1, 2),
                cost=2_000_000_000,
            )
            edges = rest[:2]
            made = dict(zip((name for name, _, _ in CONSTANTS), rest[2:]))
        else:
            names = ("coef", "band_x", "band_y", "order", "spread")
            field, *edges = call(
                inner,
                "inner",
                [whole] + ([] if last else [tile] * 2),
                [field, *(made[name] for name in names), *adds],
                cost=2_000_000_000,
                aliases={0: 0},
            )
        ghosts = [*received, *sent[5:], made["matrix"], made["edge"]]
        if last:
            break
        updates = call(
            lambda *refs: edge_kernel(side, *refs),
            "edges",
            [tile] * 2 + [strip] * 7,
            [*ghosts, made["fold"], made["same"], made["gain"], *edges],
            work,
        )
        adds, sent = updates[:2], updates[2:]
    (field,) = call(
        lambda *refs: final_kernel(side, *refs),
        "final",
        [whole],
        [*ghosts, made["spread"], field],
        [pltpu.VMEM(field.shape, jnp.float32), pltpu.SemaphoreType.DMA((FACES,))],
        out_hbm=True,
    )
    return field[None]


def solution(mesh):
    placed = (P(("member", "tile"), None, None, None, None), P(), P(), P(), P())
    return jax.shard_map(
        on_device,
        mesh=mesh,
        in_specs=placed,
        out_specs=P(("member", "tile"), None, None, None, None),
        check_vma=False,
    )
```

```python
import math

import jax
import jax.numpy as jnp
from jax import lax
from jax.experimental import pallas as pl
from jax.experimental.pallas import tpu as pltpu
from jax.sharding import PartitionSpec as P

SUBSTEPS = 4
FACES = 6
LEV = 3
DEPTH = 3
BLK = 128
PER_FACE = LEV * DEPTH
ROWS = 56
HALF = 64
WEST, EAST, SOUTH, NORTH = 0, 1, 2, 3
SCALE = 20.0
VMEM_LIMIT = 16 * 1024 * 1024


def whole_vmem():
    return pl.BlockSpec(memory_space=pltpu.VMEM)


def iota(shape, dim):
    return lax.broadcasted_iota(jnp.int32, shape, dim)


def weight_of(distance):
    return jnp.where(
        distance == 1, 9.0, jnp.where(distance == 2, 7.0, jnp.where(distance == 3, 4.0, 0.0))
    )


def split2(x):
    high = x.astype(jnp.bfloat16)
    low = (x - high.astype(jnp.float32)).astype(jnp.bfloat16)
    return high, low


def lagrange_weights(t):
    return (
        -(t - 1.0) * (t - 2.0) * (t - 3.0) / 6.0,
        t * (t - 2.0) * (t - 3.0) / 2.0,
        -t * (t - 1.0) * (t - 3.0) / 2.0,
        t * (t - 1.0) * (t - 2.0) / 6.0,
    )


def band_matrix():
    gap = jnp.abs(iota((BLK, BLK), 0) - iota((BLK, BLK), 1))
    return jnp.where(gap == 0, -40.0, weight_of(gap)).astype(jnp.bfloat16)


def edge_matrix():
    shape = (BLK, BLK)
    to, src = iota(shape, 0), iota(shape, 1)
    lower = to < HALF
    to_row = jnp.where(lower, to, to - HALF)
    src_row = jnp.where(src < HALF, src, src - HALF)
    to_plane = (to_row * 171) >> 9
    src_plane = (src_row * 171) >> 9
    to_j = to_row - 3 * to_plane
    src_j = src_row - 3 * src_plane
    same = ((to < HALF) == (src < HALF)) & (to_plane == src_plane)
    distance = jnp.where(lower, 3 + to_j - src_j, 3 + src_j - to_j)
    return jnp.where(same, weight_of(distance), 0.0).astype(jnp.bfloat16)


def seam_matrices(starts, offsets, out_ref):
    j = iota((BLK, BLK), 0)
    back = BLK - 1 - j
    for h in range(DEPTH):
        first = starts[h : h + 1, :]
        weights = lagrange_weights(offsets[h : h + 1, :])
        for turned, place in ((0, j), (1, back)):
            matrix = jnp.zeros((BLK, BLK), jnp.float32)
            for m, weight in enumerate(weights):
                matrix = matrix + jnp.where(place == first + m, weight, 0.0)
            high, low = split2(matrix)
            at = (turned * DEPTH + h) * BLK
            out_ref[:BLK, at : at + BLK] = high
            out_ref[BLK : 2 * BLK, at : at + BLK] = high
            out_ref[2 * BLK :, at : at + BLK] = low


def position(side):
    index = lax.axis_index("tile")
    return lax.rem(index, side), lax.div(index, side)


def is_inner(row, col, side):
    return 0 < row < side - 1 and 0 < col < side - 1


def row_codes(shape):
    row = iota(shape, 0)
    block = (row * 57) >> 9
    odd = (block & 1) == 1
    depth = row - 3 * ((row * 171) >> 9)
    return odd, depth


def plane_row(shape, dim):
    row = iota(shape, dim)
    lower = row < HALF
    inside = jnp.where(lower, row, row - HALF)
    plane = (inside * 171) >> 9
    return lower, plane, inside - 3 * plane


def tiles_of(plane_value):
    return plane_value.reshape(BLK // 8, 8, BLK)


def lane_of_tile():
    return iota((1, 8, BLK), 2)


def take_edges(q, plane, columns, rows_ref):
    lane, at = lane_of_tile(), 6 * plane
    turned = pltpu.roll(q, (at + 3) % BLK, 2)
    columns = jnp.where((lane >= at) & (lane < at + 6), turned, columns)
    low, high = 3 * plane, HALF + 3 * plane
    rows_ref[low : low + 3, :] = q[0, :3, :]
    rows_ref[high : high + 3, :] = q[BLK // 8 - 1, 5:, :]
    return columns


def lane_order():
    lower, plane, cell = plane_row((BLK, BLK), 0)
    lane = 6 * plane + cell + jnp.where(lower, 3, 0)
    right = (lane == iota((BLK, BLK), 1)) & (plane < FACES * LEV)
    return jnp.where(right, 1.0, 0.0).astype(jnp.bfloat16)


def rows_from_columns(columns, order):
    high, low = split2(columns.reshape(BLK, BLK))
    return lax.dot_general(
        order,
        jnp.concatenate([high, low], axis=1),
        (((1,), (1,)), ((), ())),
        preferred_element_type=jnp.float32,
    )


def clear_rest(rows_ref):
    used = FACES * PER_FACE
    rest = jnp.zeros((HALF - used, BLK), jnp.float32)
    rows_ref[used:HALF, :] = rest
    rows_ref[HALF + used :, :] = rest


def pack(columns_ref, rows_ref, side, outs, strips_ref):
    turn_ref, far_ref, near_ref, mirror_ref, core_ref, own_a_ref, own_b_ref = outs
    col, row = position(side)
    for face in range(FACES):
        at = PER_FACE * face
        strips_ref[WEST, face, :PER_FACE, :] = columns_ref[at : at + PER_FACE, :]
        strips_ref[EAST, face, :PER_FACE, :] = columns_ref[HALF + at : HALF + at + PER_FACE, :]
        strips_ref[SOUTH, face, :PER_FACE, :] = rows_ref[at : at + PER_FACE, :]
        strips_ref[NORTH, face, :PER_FACE, :] = rows_ref[HALF + at : HALF + at + PER_FACE, :]
    even_col, even_row = lax.rem(col, 2) == 0, lax.rem(row, 2) == 0

    def shift(place):
        return jnp.where(place == 0, 1, jnp.where(place == side - 1, FACES - 1, 0))

    plans = (
        (core_ref, jnp.where(even_col, EAST, WEST), 0),
        (mirror_ref, jnp.where(even_col, WEST, EAST), shift(col)),
        (near_ref, jnp.where(even_row, NORTH, SOUTH), 0),
        (far_ref, jnp.where(even_row, SOUTH, NORTH), shift(row)),
    )
    rest = jnp.zeros((ROWS - FACES * PER_FACE, BLK), jnp.float32)
    for out_ref, which, by in plans:
        for face in range(FACES):
            at = PER_FACE * face
            source = face + by
            source = jnp.where(source >= FACES, source - FACES, source)
            out_ref[at : at + PER_FACE, :] = strips_ref[which, source, :PER_FACE, :]
        out_ref[FACES * PER_FACE :, :] = rest
    for face in range(FACES):
        at = PER_FACE * face
        if face % 2:
            a, b = (SOUTH, face + 2), (EAST, face - 2)
        else:
            a, b = (NORTH, face - 2), (WEST, face + 2)
        own_a_ref[at : at + PER_FACE, :] = strips_ref[a[0], a[1] % FACES, :PER_FACE, :]
        own_b_ref[at : at + PER_FACE, :] = strips_ref[b[0], b[1] % FACES, :PER_FACE, :]
    own_a_ref[FACES * PER_FACE :, :] = rest
    own_b_ref[FACES * PER_FACE :, :] = rest
    odd, _ = row_codes((ROWS, BLK))
    use_a = jnp.where(odd, (row == 0).astype(jnp.int32), (row == side - 1).astype(jnp.int32))
    turn_ref[...] = jnp.where(use_a == 1, own_a_ref[...], own_b_ref[...])


TABLES = (
    ("edge", (BLK, 2 * BLK), jnp.bfloat16),
    ("reach", (2 * BLK, BLK), jnp.bfloat16),
    ("same", (BLK, BLK), jnp.float32),
    ("order", (BLK, 2 * BLK), jnp.bfloat16),
    ("spread", (2 * BLK, BLK), jnp.bfloat16),
    ("band_x", (2 * BLK, BLK), jnp.bfloat16),
    ("band_y", (BLK, 2 * BLK), jnp.bfloat16),
)
CONSTANTS = (
    ("coef", (8, BLK), jnp.float32),
    ("gain", (BLK, BLK), jnp.float32),
    ("matrix", (3 * BLK, 2 * DEPTH * BLK), jnp.bfloat16),
)


def tables_kernel(edge, reach, same, order, spread, band_x, band_y):
    lower, plane, cell = plane_row((BLK, BLK), 0)
    _, plane_src, _ = plane_row((BLK, BLK), 1)
    for ref, value, axis in (
        (edge, edge_matrix(), 1),
        (order, lane_order(), 1),
        (band_x, band_matrix(), 0),
        (band_y, band_matrix(), 1),
    ):
        ref[...] = jnp.concatenate([value, value], axis=axis)
    to = iota((BLK, BLK), 1)
    low = weight_of(jnp.where(to < 3, 3 + to - cell, 0))
    high = weight_of(jnp.where(to >= BLK - 3, 3 + cell - (to - (BLK - 3)), 0))
    value = jnp.where(plane < FACES * LEV, jnp.where(lower, low, high), 0.0).astype(jnp.bfloat16)
    reach[...] = jnp.concatenate([value, value], axis=0)
    spread[...] = jnp.concatenate([lane_order()] * 2, axis=0)
    same[...] = jnp.where(plane == plane_src, 1.0, 0.0)


def constants_kernel(wave_ref, visc_ref, start_ref, offset_ref, coef_ref, gain_ref, matrix_ref):
    seam_matrices(start_ref[...], offset_ref[...], matrix_ref)
    _, plane, _ = plane_row((BLK, BLK), 0)
    level_of = plane - 3 * ((plane * 171) >> 9)
    gain = jnp.zeros((BLK, BLK), jnp.float32)
    for level in range(LEV):
        a, b = [
            jnp.broadcast_to(ref[:, level : level + 1] * (1.0 / SCALE), (1, BLK))
            for ref in (wave_ref, visc_ref)
        ]
        coef_ref[level : level + 1, :] = a
        coef_ref[LEV + level : LEV + level + 1, :] = b
        gain = jnp.where(level_of == level, a + b, gain)
    coef_ref[2 * LEV :, :] = jnp.zeros((8 - 2 * LEV, BLK), jnp.float32)
    gain_ref[...] = gain


def first_kernel(side, state_ref, coef_ref, order_ref, *rest):
    outs = rest[:7]
    columns_ref, rows_ref, strips_ref = rest[7:]
    clear_rest(rows_ref)
    columns = jnp.zeros((BLK // 8, 8, BLK), jnp.float32)
    for plane in range(FACES * LEV):
        face, level = divmod(plane, LEV)
        a, b = coef_ref[level : level + 1, :], coef_ref[LEV + level : LEV + level + 1, :]
        q = a * state_ref[face, level] + b * state_ref[face, LEV + level]
        columns = take_edges(tiles_of(q), plane, columns, rows_ref)
    columns_ref[...] = rows_from_columns(columns, order_ref[...])
    pack(columns_ref, rows_ref, side, outs, strips_ref)


def ghosts_of(side, received, own_a_ref, own_b_ref, matrix_ref):
    turned, far, near, mirror, core = [ref[...] for ref in received]
    col, row = position(side)
    even_col, even_row = lax.rem(col, 2) == 0, lax.rem(row, 2) == 0
    odd, depth = row_codes((ROWS, BLK))
    alone = ((row == 0) & (col == side - 1)) | ((col == 0) & (row == side - 1))
    pairs = (
        (
            jnp.where(even_col, mirror, core),
            jnp.where(even_col, core, mirror),
            jnp.where(alone, own_a_ref[...], turned),
            col,
            0,
        ),
        (
            jnp.where(even_row, far, near),
            jnp.where(even_row, near, far),
            jnp.where(alone, own_b_ref[...], turned),
            row,
            1,
        ),
    )
    seams, marks = [], []
    for low, high, crossed, place, low_turned in pairs:
        at_low = (place == 0).astype(jnp.int32)
        parity = at_low ^ (1 - low_turned)
        is_turned = odd.astype(jnp.int32) == parity
        seams.append(jnp.where(is_turned, crossed, jnp.where(place == 0, low, high)))
        marks.append((is_turned, jnp.where(place == 0, DEPTH - 1 - depth, depth)))
    first, second = split2(jnp.concatenate(seams, axis=0))
    mixed = jnp.dot(
        jnp.concatenate([first, second, first], axis=1),
        matrix_ref[...],
        preferred_element_type=jnp.float32,
    )
    rest = jnp.zeros((HALF - ROWS, BLK), jnp.float32)
    ghosts = []
    for index, (low, high, _, place, _) in enumerate(pairs):
        part = mixed[index * ROWS : (index + 1) * ROWS, :]
        is_turned, h_of = marks[index]
        made = jnp.zeros((ROWS, BLK), jnp.float32)
        for h in range(DEPTH):
            plain = part[:, h * BLK : (h + 1) * BLK]
            turn = part[:, (DEPTH + h) * BLK : (DEPTH + h + 1) * BLK]
            made = jnp.where(h_of == h, jnp.where(is_turned, turn, plain), made)
        ghosts.append(
            jnp.concatenate(
                [
                    jnp.where(place == 0, made, low),
                    rest,
                    jnp.where(place == side - 1, made, high),
                    rest,
                ],
                axis=0,
            )
        )
    return ghosts


def ghost_additions(ghosts, edge_ref):
    high, low = split2(jnp.concatenate(ghosts, axis=1))
    adds = jnp.dot(
        edge_ref[...],
        jnp.concatenate([high, low], axis=0),
        preferred_element_type=jnp.float32,
    )
    return adds[:, :BLK], adds[:, BLK:]


def corner_part(ghosts, same):
    turned = ghosts.T
    cell = plane_row((HALF, BLK), 0)[2]
    halves = []
    for first in (0, BLK - 3):
        lines = [turned[first + at : first + at + 1, :] for at in range(3)]
        halves.append(jnp.where(cell == 0, lines[0], jnp.where(cell == 1, lines[1], lines[2])))
    return jnp.concatenate(split2(jnp.concatenate(halves, axis=0) * same), axis=1)


def edge_kernel(side, *refs):
    across, along = ghosts_of(side, refs[:5], *refs[5:8])
    edge_ref, reach_ref, same_ref, gain_ref, old_columns_ref, old_rows_ref = refs[8:14]
    add_x_ref, add_y_ref = refs[14:16]
    outs = refs[16:23]
    columns_ref, rows_ref, strips_ref = refs[23:]
    add_x, add_y = ghost_additions((across, along), edge_ref)
    same = same_ref[...]
    corners = jnp.dot(
        jnp.concatenate([corner_part(along, same), corner_part(across, same)], axis=0),
        reach_ref[...],
        preferred_element_type=jnp.float32,
    )
    gain = gain_ref[...]
    columns_ref[...] = old_columns_ref[...] + gain * (add_x + corners[:BLK])
    rows_ref[...] = old_rows_ref[...] + gain * (add_y + corners[BLK:])
    add_x_ref[...] = add_x
    add_y_ref[...] = add_y
    pack(columns_ref, rows_ref, side, outs, strips_ref)


def spread_lanes(add_x, spread_ref):
    high, low = split2(add_x.T)
    return tiles_of(
        jnp.dot(
            jnp.concatenate([high, low], axis=1),
            spread_ref[...],
            preferred_element_type=jnp.float32,
        )
    )


def edge_additions(plane, add_x, add_y):
    lane = lane_of_tile()
    turned = pltpu.roll(add_x, (BLK - 3 - 6 * plane) % BLK, 2)
    add = jnp.where((lane < 3) | (lane >= BLK - 3), turned, 0.0)
    at = 3 * plane
    pad = jnp.zeros((5, BLK), jnp.float32)
    bottom = add[:1] + jnp.concatenate([add_y[at : at + 3], pad], axis=0)[None]
    top = add[-1:] + jnp.concatenate([pad, add_y[HALF + at : HALF + at + 3]], axis=0)[None]
    return jnp.concatenate([bottom, add[1:-1], top], axis=0)


def inner_kernel(first, last, state_ref, *refs):
    coef_ref, band_x_ref, band_y_ref, order_ref, spread_ref = refs[:5]
    refs = refs[5:]
    if not first:
        add_x, add_y = spread_lanes(refs[0][...], spread_ref), refs[1][...]
        refs = refs[2:]
    new_ref = refs[0]
    if not last:
        columns_ref, rows_ref = refs[1:]
    if not last:
        clear_rest(rows_ref)
    columns = jnp.zeros((BLK // 8, 8, BLK), jnp.float32)
    group = 2
    for begin in range(0, FACES * LEV, group):
        fields, highs, lows = [], [], []
        for plane in range(begin, begin + group):
            face, level = divmod(plane, LEV)
            a, b = coef_ref[level : level + 1, :], coef_ref[LEV + level : LEV + level + 1, :]
            pressure = tiles_of(state_ref[face, level])
            rate = tiles_of(state_ref[face, LEV + level])
            if not first:
                add = edge_additions(plane, add_x, add_y)
                pressure, rate = pressure + add, rate + add
            high, low = split2((a * pressure + b * rate).reshape(BLK, BLK))
            fields.append((pressure, rate))
            highs.append(high)
            lows.append(low)
        by_x = jnp.dot(
            jnp.concatenate(
                [jnp.concatenate(pair, axis=1) for pair in zip(highs, lows)], axis=0
            ),
            band_x_ref[...],
            preferred_element_type=jnp.float32,
        )
        by_y = jnp.dot(
            band_y_ref[...],
            jnp.concatenate(
                [jnp.concatenate(highs, axis=1), jnp.concatenate(lows, axis=1)], axis=0
            ),
            preferred_element_type=jnp.float32,
        )
        for place, (pressure, rate) in enumerate(fields):
            plane = begin + place
            face, level = divmod(plane, LEV)
            a, b = coef_ref[level : level + 1, :], coef_ref[LEV + level : LEV + level + 1, :]
            at = place * BLK
            rate = rate + tiles_of(by_x[at : at + BLK, :] + by_y[:, at : at + BLK])
            pressure = pressure + rate
            new_ref[face, level] = pressure.reshape(BLK, BLK)
            new_ref[face, LEV + level] = rate.reshape(BLK, BLK)
            if not last:
                columns = take_edges(a * pressure + b * rate, plane, columns, rows_ref)
    if not last:
        columns_ref[...] = rows_from_columns(columns, order_ref[...])


def final_kernel(side, *refs):
    edge_ref, spread_ref, state_ref, out_hbm, buffer, sems = refs[8:]
    add_x, add_y = ghost_additions(ghosts_of(side, refs[:5], *refs[5:8]), edge_ref)
    add_x = spread_lanes(add_x, spread_ref)
    copies = []
    for face in range(FACES):
        for level in range(LEV):
            add = edge_additions(face * LEV + level, add_x, add_y)
            for channel in (level, LEV + level):
                value = tiles_of(state_ref[face, channel]) + add
                buffer[face, channel] = value.reshape(BLK, BLK)
        copy = pltpu.make_async_copy(buffer.at[face], out_hbm.at[face], sems.at[face])
        copy.start()
        copies.append(copy)
    for copy in copies:
        copy.wait()


def exchange(payloads, side):
    def at(row, col):
        return row * side + col

    cells = [(row, col) for row in range(side) for col in range(side)]

    def swap(place, odd_first):
        return (place ^ 1) if not odd_first else (place + (1 if place % 2 else -1)) % side

    core = [(at(r, c), at(r, swap(c, False))) for r, c in cells]
    mirror = [(at(r, c), at(r, swap(c, True))) for r, c in cells]
    near = [(at(r, c), at(swap(r, False), c)) for r, c in cells]
    far = [(at(r, c), at(swap(r, True), c)) for r, c in cells]
    edge = side - 1
    turn = set()
    for x in range(edge):
        turn |= {(at(0, x), at(edge - x, edge)), (at(edge - x, edge), at(0, x))}
    for x in range(1, side):
        turn |= {(at(edge, x), at(edge - x, 0)), (at(edge - x, 0), at(edge, x))}
    spare = [pair for pair in mirror if is_inner(pair[0] // side, pair[0] % side, side)]
    first_end, last_end = at(1, edge - 1), at(edge - 1, 1)
    left = [b for a, b in spare if a in (first_end, last_end)]
    spare = [pair for pair in spare if not {*pair} & {first_end, last_end}]
    spare += [(at(0, edge), first_end), (at(edge, 0), last_end), (left[0], left[1])]
    turn |= {(a, b) for a, b in spare} | {(b, a) for a, b in spare}
    turn_out, far_out, near_out, mirror_out, core_out = payloads
    turn_in = lax.ppermute(turn_out, "tile", sorted(turn))
    far_in = lax.ppermute(far_out, "tile", far)
    near_in = lax.ppermute(near_out, "tile", near)
    mirror_in = lax.ppermute(mirror_out, "tile", mirror)
    core_in = lax.ppermute(core_out, "tile", core)
    return turn_in, far_in, near_in, mirror_in, core_in


def call(kernel, name, outs, ins, scratch=(), out_hbm=False, cost=0, aliases=None):
    hbm = pl.BlockSpec(memory_space=pltpu.HBM)
    vmem = pl.BlockSpec(memory_space=pltpu.VMEM)
    return pl.pallas_call(
        kernel,
        out_shape=outs,
        in_specs=[vmem] * len(ins),
        out_specs=[hbm if out_hbm else vmem] * len(outs),
        scratch_shapes=list(scratch),
        compiler_params=pltpu.CompilerParams(vmem_limit_bytes=VMEM_LIMIT),
        cost_estimate=pl.CostEstimate(flops=cost, bytes_accessed=cost // 500, transcendentals=0),
        input_output_aliases=aliases or {},
        name=name,
    )(*ins)


def on_device(state, wave_coef, visc_coef, stencil_start, stencil_offset):
    side = math.isqrt(lax.axis_size("tile"))
    field = state[0]

    def array(*shape, dtype=jnp.float32):
        return jax.ShapeDtypeStruct(shape, dtype)

    tile = array(BLK, BLK)
    strip = array(ROWS, BLK)
    whole = array(*field.shape)
    work = [
        pltpu.VMEM((BLK, BLK), jnp.float32),
        pltpu.VMEM((BLK, BLK), jnp.float32),
        pltpu.VMEM((4, FACES, 16, BLK), jnp.float32),
    ]
    values = call(
        tables_kernel,
        "tables",
        [array(*shape, dtype=kind) for _, shape, kind in TABLES],
        [],
        cost=4_000_000_000,
    )
    made = dict(zip((name for name, _, _ in TABLES), values))
    values = call(
        constants_kernel,
        "constants",
        [array(*shape, dtype=kind) for _, shape, kind in CONSTANTS],
        [wave_coef[None], visc_coef[None], stencil_start, stencil_offset],
        cost=1_000_000_000,
    )
    made.update(zip((name for name, _, _ in CONSTANTS), values))
    sent = call(
        lambda *refs: first_kernel(side, *refs),
        "first_edges",
        [strip] * 7,
        [field, made["coef"], made["order"]],
        work,
        cost=1_000_000_000,
    )
    adds = []
    names = ("coef", "band_x", "band_y", "order", "spread")
    for step in range(SUBSTEPS):
        first, last = step == 0, step == SUBSTEPS - 1
        received = exchange(sent[:5], side)
        field, *edges = call(
            lambda *refs, first=first, last=last: inner_kernel(first, last, *refs),
            "inner",
            [whole] + ([] if last else [tile] * 2),
            [field, *(made[name] for name in names), *adds],
            cost=2_000_000_000,
            aliases=None if first else {0: 0},
        )
        ghosts = [*received, *sent[5:], made["matrix"], made["edge"]]
        if last:
            break
        updates = call(
            lambda *refs: edge_kernel(side, *refs),
            "edges",
            [tile] * 2 + [strip] * 7,
            [*ghosts, made["reach"], made["same"], made["gain"], *edges],
            work,
        )
        adds, sent = updates[:2], updates[2:]
    (field,) = call(
        lambda *refs: final_kernel(side, *refs),
        "final",
        [whole],
        [*ghosts, made["spread"], field],
        [pltpu.VMEM(field.shape, jnp.float32), pltpu.SemaphoreType.DMA((FACES,))],
        out_hbm=True,
    )
    return field[None]


def solution(mesh):
    placed = (P(("member", "tile"), None, None, None, None), P(), P(), P(), P())
    return jax.shard_map(
        on_device,
        mesh=mesh,
        in_specs=placed,
        out_specs=P(("member", "tile"), None, None, None, None),
        check_vma=False,
    )
```

```python
import math

import jax
import jax.numpy as jnp
from jax import lax
from jax.experimental import pallas as pl
from jax.experimental.pallas import tpu as pltpu
from jax.sharding import PartitionSpec as P

SUBSTEPS = 4
FACES = 6
LEV = 3
DEPTH = 3
BLK = 128
PER_FACE = LEV * DEPTH
ROWS = 56
TAPS = 4
HALF = 64
WEST, EAST, SOUTH, NORTH = 0, 1, 2, 3
SCALE = 20.0
VMEM_LIMIT = 16 * 1024 * 1024


def whole_vmem():
    return pl.BlockSpec(memory_space=pltpu.VMEM)


def iota(shape, dim):
    return lax.broadcasted_iota(jnp.int32, shape, dim)


def weight_of(distance):
    return jnp.where(
        distance == 1, 9.0, jnp.where(distance == 2, 7.0, jnp.where(distance == 3, 4.0, 0.0))
    )


def split2(x):
    high = x.astype(jnp.bfloat16)
    low = (x - high.astype(jnp.float32)).astype(jnp.bfloat16)
    return high, low


def lagrange_weights(t):
    return (
        -(t - 1.0) * (t - 2.0) * (t - 3.0) / 6.0,
        t * (t - 2.0) * (t - 3.0) / 2.0,
        -t * (t - 1.0) * (t - 3.0) / 2.0,
        t * (t - 1.0) * (t - 2.0) / 6.0,
    )


def band_matrix():
    gap = jnp.abs(iota((BLK, BLK), 0) - iota((BLK, BLK), 1))
    return jnp.where(gap == 0, -40.0, weight_of(gap)).astype(jnp.bfloat16)


def position(side):
    index = lax.axis_index("tile")
    return lax.rem(index, side), lax.div(index, side)


def is_inner(row, col, side):
    return 0 < row < side - 1 and 0 < col < side - 1


def row_codes(shape):
    row = iota(shape, 0)
    block = (row * 57) >> 9
    odd = (block & 1) == 1
    depth = row - 3 * ((row * 171) >> 9)
    return odd, depth


def plane_row(shape, dim):
    row = iota(shape, dim)
    lower = row < HALF
    inside = jnp.where(lower, row, row - HALF)
    plane = (inside * 171) >> 9
    return lower, plane, inside - 3 * plane


def tiles_of(plane_value):
    return plane_value.reshape(BLK // 8, 8, BLK)


def lane_of_tile():
    return iota((1, 8, BLK), 2)


def take_edges(q, plane, columns, rows_ref):
    lane, at = lane_of_tile(), 6 * plane
    turned = pltpu.roll(q, (at + 3) % BLK, 2)
    columns = jnp.where((lane >= at) & (lane < at + 6), turned, columns)
    low, high = 3 * plane, HALF + 3 * plane
    rows_ref[low : low + 3, :] = q[0, :3, :]
    rows_ref[high : high + 3, :] = q[BLK // 8 - 1, 5:, :]
    return columns


def lane_order():
    lower, plane, cell = plane_row((BLK, BLK), 0)
    lane = 6 * plane + cell + jnp.where(lower, 3, 0)
    right = (lane == iota((BLK, BLK), 1)) & (plane < FACES * LEV)
    return jnp.where(right, 1.0, 0.0).astype(jnp.bfloat16)


def rows_from_columns(columns, order):
    high, low = split2(columns.reshape(BLK, BLK))
    return lax.dot_general(
        order,
        jnp.concatenate([high, low], axis=1),
        (((1,), (1,)), ((), ())),
        preferred_element_type=jnp.float32,
    )


def clear_rest(rows_ref):
    used = FACES * PER_FACE
    rest = jnp.zeros((HALF - used, BLK), jnp.float32)
    rows_ref[used:HALF, :] = rest
    rows_ref[HALF + used :, :] = rest


def pack(columns_ref, rows_ref, side, outs, strips_ref):
    turn_ref, far_ref, near_ref, mirror_ref, core_ref, own_a_ref, own_b_ref = outs
    col, row = position(side)
    for face in range(FACES):
        at = PER_FACE * face
        strips_ref[WEST, face, :PER_FACE, :] = columns_ref[at : at + PER_FACE, :]
        strips_ref[EAST, face, :PER_FACE, :] = columns_ref[HALF + at : HALF + at + PER_FACE, :]
        strips_ref[SOUTH, face, :PER_FACE, :] = rows_ref[at : at + PER_FACE, :]
        strips_ref[NORTH, face, :PER_FACE, :] = rows_ref[HALF + at : HALF + at + PER_FACE, :]
    even_col, even_row = lax.rem(col, 2) == 0, lax.rem(row, 2) == 0

    def shift(place):
        return jnp.where(place == 0, 1, jnp.where(place == side - 1, FACES - 1, 0))

    plans = (
        (core_ref, jnp.where(even_col, EAST, WEST), 0),
        (mirror_ref, jnp.where(even_col, WEST, EAST), shift(col)),
        (near_ref, jnp.where(even_row, NORTH, SOUTH), 0),
        (far_ref, jnp.where(even_row, SOUTH, NORTH), shift(row)),
    )
    rest = jnp.zeros((ROWS - FACES * PER_FACE, BLK), jnp.float32)
    for out_ref, which, by in plans:
        for face in range(FACES):
            at = PER_FACE * face
            source = face + by
            source = jnp.where(source >= FACES, source - FACES, source)
            out_ref[at : at + PER_FACE, :] = strips_ref[which, source, :PER_FACE, :]
        out_ref[FACES * PER_FACE :, :] = rest
    for face in range(FACES):
        at = PER_FACE * face
        if face % 2:
            a, b = (SOUTH, face + 2), (EAST, face - 2)
        else:
            a, b = (NORTH, face - 2), (WEST, face + 2)
        own_a_ref[at : at + PER_FACE, :] = strips_ref[a[0], a[1] % FACES, :PER_FACE, :]
        own_b_ref[at : at + PER_FACE, :] = strips_ref[b[0], b[1] % FACES, :PER_FACE, :]
    own_a_ref[FACES * PER_FACE :, :] = rest
    own_b_ref[FACES * PER_FACE :, :] = rest
    odd, _ = row_codes((ROWS, BLK))
    use_a = jnp.where(odd, (row == 0).astype(jnp.int32), (row == side - 1).astype(jnp.int32))
    turn_ref[...] = jnp.where(use_a == 1, own_a_ref[...], own_b_ref[...])


TABLES = (
    ("reach", (2 * BLK, BLK), jnp.bfloat16),
    ("same", (BLK, BLK), jnp.float32),
    ("order", (BLK, 2 * BLK), jnp.bfloat16),
    ("spread", (2 * BLK, BLK), jnp.bfloat16),
    ("band_x", (2 * BLK, BLK), jnp.bfloat16),
    ("band_y", (BLK, 2 * BLK), jnp.bfloat16),
)
CONSTANTS = (
    ("coef", (8, BLK), jnp.float32),
    ("gain", (BLK, BLK), jnp.float32),
    ("taps", (TAPS, 2 * ROWS, BLK), jnp.int32),
    ("weights", (TAPS, 2 * ROWS, BLK), jnp.float32),
)


def tables_kernel(reach, same, order, spread, band_x, band_y):
    lower, plane, cell = plane_row((BLK, BLK), 0)
    _, plane_src, _ = plane_row((BLK, BLK), 1)
    for ref, value, axis in (
        (order, lane_order(), 1),
        (band_x, band_matrix(), 0),
        (band_y, band_matrix(), 1),
    ):
        ref[...] = jnp.concatenate([value, value], axis=axis)
    to = iota((BLK, BLK), 1)
    low = weight_of(jnp.where(to < 3, 3 + to - cell, 0))
    high = weight_of(jnp.where(to >= BLK - 3, 3 + cell - (to - (BLK - 3)), 0))
    value = jnp.where(plane < FACES * LEV, jnp.where(lower, low, high), 0.0).astype(jnp.bfloat16)
    reach[...] = jnp.concatenate([value, value], axis=0)
    spread[...] = jnp.concatenate([lane_order()] * 2, axis=0)
    same[...] = jnp.where(plane == plane_src, 1.0, 0.0)


def seam_rows(place, low_turned):
    odd, depth = row_codes((ROWS, BLK))
    at_low = (place == 0).astype(jnp.int32)
    is_turned = odd.astype(jnp.int32) == at_low ^ (1 - low_turned)
    return is_turned, jnp.where(place == 0, DEPTH - 1 - depth, depth)


def constants_kernel(
    side, wave_ref, visc_ref, start_ref, offset_ref, coef_ref, gain_ref, taps_ref, weights_ref
):
    col, row = position(side)
    for axis, place in enumerate((col, row)):
        is_turned, h_of = seam_rows(place, axis)
        first, offset = [
            jnp.where(h_of == 0, ref[0:1, :], jnp.where(h_of == 1, ref[1:2, :], ref[2:3, :]))
            for ref in (start_ref, offset_ref)
        ]
        at = axis * ROWS
        for m, weight in enumerate(lagrange_weights(offset)):
            tap = jnp.where(is_turned, BLK - 1 - first - m, first + m)
            taps_ref[m, at : at + ROWS, :] = tap
            weights_ref[m, at : at + ROWS, :] = weight
    _, plane, _ = plane_row((BLK, BLK), 0)
    level_of = plane - 3 * ((plane * 171) >> 9)
    gain = jnp.zeros((BLK, BLK), jnp.float32)
    for level in range(LEV):
        a, b = [
            jnp.broadcast_to(ref[:, level : level + 1] * (1.0 / SCALE), (1, BLK))
            for ref in (wave_ref, visc_ref)
        ]
        coef_ref[level : level + 1, :] = a
        coef_ref[LEV + level : LEV + level + 1, :] = b
        gain = jnp.where(level_of == level, a + b, gain)
    coef_ref[2 * LEV :, :] = jnp.zeros((8 - 2 * LEV, BLK), jnp.float32)
    gain_ref[...] = gain


def first_kernel(side, state_ref, coef_ref, order_ref, *rest):
    outs = rest[:7]
    columns_ref, rows_ref, strips_ref = rest[7:]
    clear_rest(rows_ref)
    columns = jnp.zeros((BLK // 8, 8, BLK), jnp.float32)
    for plane in range(FACES * LEV):
        face, level = divmod(plane, LEV)
        a, b = coef_ref[level : level + 1, :], coef_ref[LEV + level : LEV + level + 1, :]
        q = a * state_ref[face, level] + b * state_ref[face, LEV + level]
        columns = take_edges(tiles_of(q), plane, columns, rows_ref)
    columns_ref[...] = rows_from_columns(columns, order_ref[...])
    pack(columns_ref, rows_ref, side, outs, strips_ref)


def ghosts_of(side, received, own_a_ref, own_b_ref, taps_ref, weights_ref):
    turned, far, near, mirror, core = [ref[...] for ref in received]
    col, row = position(side)
    even_col, even_row = lax.rem(col, 2) == 0, lax.rem(row, 2) == 0
    alone = ((row == 0) & (col == side - 1)) | ((col == 0) & (row == side - 1))
    pairs = (
        (
            jnp.where(even_col, mirror, core),
            jnp.where(even_col, core, mirror),
            jnp.where(alone, own_a_ref[...], turned),
            col,
            0,
        ),
        (
            jnp.where(even_row, far, near),
            jnp.where(even_row, near, far),
            jnp.where(alone, own_b_ref[...], turned),
            row,
            1,
        ),
    )
    seams = []
    for low, high, crossed, place, low_turned in pairs:
        is_turned, _ = seam_rows(place, low_turned)
        seams.append(jnp.where(is_turned, crossed, jnp.where(place == 0, low, high)))
    raw = jnp.concatenate(seams, axis=0)
    mixed = jnp.zeros((2 * ROWS, BLK), jnp.float32)
    for m in range(TAPS):
        source = jnp.take_along_axis(raw, taps_ref[m], axis=1, mode="promise_in_bounds")
        mixed = mixed + weights_ref[m] * source
    rest = jnp.zeros((HALF - ROWS, BLK), jnp.float32)
    ghosts = []
    for index, (low, high, _, place, _) in enumerate(pairs):
        made = mixed[index * ROWS : (index + 1) * ROWS, :]
        ghosts.append(
            jnp.concatenate(
                [
                    jnp.where(place == 0, made, low),
                    rest,
                    jnp.where(place == side - 1, made, high),
                    rest,
                ],
                axis=0,
            )
        )
    return ghosts


def ghost_additions(ghosts):
    row = iota((HALF, 1), 0)
    cell = row - 3 * ((row * 171) >> 9)
    halves = []
    both = jnp.concatenate(ghosts, axis=1)
    for half, step, index in ((both[:HALF], -1, cell), (both[HALF:], 1, 2 - cell)):
        one = pltpu.roll(half, step % HALF, 0)
        two = pltpu.roll(half, (2 * step) % HALF, 0)
        near, next_ = jnp.where(index <= 1, 7.0, 0.0), jnp.where(index == 0, 9.0, 0.0)
        halves.append(4.0 * half + near * one + next_ * two)
    adds = jnp.concatenate(halves, axis=0)
    return adds[:, :BLK], adds[:, BLK:]


def corner_part(ghosts, same):
    turned = ghosts.T
    cell = plane_row((HALF, BLK), 0)[2]
    halves = []
    for first in (0, BLK - 3):
        lines = [turned[first + at : first + at + 1, :] for at in range(3)]
        halves.append(jnp.where(cell == 0, lines[0], jnp.where(cell == 1, lines[1], lines[2])))
    return jnp.concatenate(split2(jnp.concatenate(halves, axis=0) * same), axis=1)


def edge_kernel(side, *refs):
    across, along = ghosts_of(side, refs[:5], *refs[5:9])
    reach_ref, same_ref, gain_ref, old_columns_ref, old_rows_ref = refs[9:14]
    add_x_ref, add_y_ref = refs[14:16]
    outs = refs[16:23]
    columns_ref, rows_ref, strips_ref = refs[23:]
    add_x, add_y = ghost_additions((across, along))
    same = same_ref[...]
    corners = jnp.dot(
        jnp.concatenate([corner_part(along, same), corner_part(across, same)], axis=0),
        reach_ref[...],
        preferred_element_type=jnp.float32,
    )
    gain = gain_ref[...]
    columns_ref[...] = old_columns_ref[...] + gain * (add_x + corners[:BLK])
    rows_ref[...] = old_rows_ref[...] + gain * (add_y + corners[BLK:])
    add_x_ref[...] = add_x
    add_y_ref[...] = add_y
    pack(columns_ref, rows_ref, side, outs, strips_ref)


def spread_lanes(add_x, spread_ref):
    high, low = split2(add_x.T)
    return tiles_of(
        jnp.dot(
            jnp.concatenate([high, low], axis=1),
            spread_ref[...],
            preferred_element_type=jnp.float32,
        )
    )


def edge_additions(plane, add_x, add_y):
    lane = lane_of_tile()
    turned = pltpu.roll(add_x, (BLK - 3 - 6 * plane) % BLK, 2)
    add = jnp.where((lane < 3) | (lane >= BLK - 3), turned, 0.0)
    at = 3 * plane
    pad = jnp.zeros((5, BLK), jnp.float32)
    bottom = add[:1] + jnp.concatenate([add_y[at : at + 3], pad], axis=0)[None]
    top = add[-1:] + jnp.concatenate([pad, add_y[HALF + at : HALF + at + 3]], axis=0)[None]
    return jnp.concatenate([bottom, add[1:-1], top], axis=0)


def inner_kernel(first, last, state_ref, *refs):
    coef_ref, band_x_ref, band_y_ref, order_ref, spread_ref = refs[:5]
    refs = refs[5:]
    if not first:
        add_x, add_y = spread_lanes(refs[0][...], spread_ref), refs[1][...]
        refs = refs[2:]
    new_ref = refs[0]
    if not last:
        columns_ref, rows_ref = refs[1:]
    if not last:
        clear_rest(rows_ref)
    columns = jnp.zeros((BLK // 8, 8, BLK), jnp.float32)
    group = 2
    for begin in range(0, FACES * LEV, group):
        fields, highs, lows = [], [], []
        for plane in range(begin, begin + group):
            face, level = divmod(plane, LEV)
            a, b = coef_ref[level : level + 1, :], coef_ref[LEV + level : LEV + level + 1, :]
            pressure = tiles_of(state_ref[face, level])
            rate = tiles_of(state_ref[face, LEV + level])
            if not first:
                add = edge_additions(plane, add_x, add_y)
                pressure, rate = pressure + add, rate + add
            high, low = split2((a * pressure + b * rate).reshape(BLK, BLK))
            fields.append((pressure, rate))
            highs.append(high)
            lows.append(low)
        by_x = jnp.dot(
            jnp.concatenate(
                [jnp.concatenate(pair, axis=1) for pair in zip(highs, lows)], axis=0
            ),
            band_x_ref[...],
            preferred_element_type=jnp.float32,
        )
        by_y = jnp.dot(
            band_y_ref[...],
            jnp.concatenate(
                [jnp.concatenate(highs, axis=1), jnp.concatenate(lows, axis=1)], axis=0
            ),
            preferred_element_type=jnp.float32,
        )
        for place, (pressure, rate) in enumerate(fields):
            plane = begin + place
            face, level = divmod(plane, LEV)
            a, b = coef_ref[level : level + 1, :], coef_ref[LEV + level : LEV + level + 1, :]
            at = place * BLK
            rate = rate + tiles_of(by_x[at : at + BLK, :] + by_y[:, at : at + BLK])
            pressure = pressure + rate
            new_ref[face, level] = pressure.reshape(BLK, BLK)
            new_ref[face, LEV + level] = rate.reshape(BLK, BLK)
            if not last:
                columns = take_edges(a * pressure + b * rate, plane, columns, rows_ref)
    if not last:
        columns_ref[...] = rows_from_columns(columns, order_ref[...])


def final_kernel(side, *refs):
    spread_ref, state_ref, out_hbm, buffer, sems = refs[9:]
    add_x, add_y = ghost_additions(ghosts_of(side, refs[:5], *refs[5:9]))
    add_x = spread_lanes(add_x, spread_ref)
    copies = []
    for face in range(FACES):
        for level in range(LEV):
            add = edge_additions(face * LEV + level, add_x, add_y)
            for channel in (level, LEV + level):
                value = tiles_of(state_ref[face, channel]) + add
                buffer[face, channel] = value.reshape(BLK, BLK)
        copy = pltpu.make_async_copy(buffer.at[face], out_hbm.at[face], sems.at[face])
        copy.start()
        copies.append(copy)
    for copy in copies:
        copy.wait()


def exchange(payloads, side):
    def at(row, col):
        return row * side + col

    cells = [(row, col) for row in range(side) for col in range(side)]

    def swap(place, odd_first):
        return (place ^ 1) if not odd_first else (place + (1 if place % 2 else -1)) % side

    core = [(at(r, c), at(r, swap(c, False))) for r, c in cells]
    mirror = [(at(r, c), at(r, swap(c, True))) for r, c in cells]
    near = [(at(r, c), at(swap(r, False), c)) for r, c in cells]
    far = [(at(r, c), at(swap(r, True), c)) for r, c in cells]
    edge = side - 1
    turn = set()
    for x in range(edge):
        turn |= {(at(0, x), at(edge - x, edge)), (at(edge - x, edge), at(0, x))}
    for x in range(1, side):
        turn |= {(at(edge, x), at(edge - x, 0)), (at(edge - x, 0), at(edge, x))}
    spare = [pair for pair in mirror if is_inner(pair[0] // side, pair[0] % side, side)]
    first_end, last_end = at(1, edge - 1), at(edge - 1, 1)
    left = [b for a, b in spare if a in (first_end, last_end)]
    spare = [pair for pair in spare if not {*pair} & {first_end, last_end}]
    spare += [(at(0, edge), first_end), (at(edge, 0), last_end), (left[0], left[1])]
    turn |= {(a, b) for a, b in spare} | {(b, a) for a, b in spare}
    turn_out, far_out, near_out, mirror_out, core_out = payloads
    turn_in = lax.ppermute(turn_out, "tile", sorted(turn))
    far_in = lax.ppermute(far_out, "tile", far)
    near_in = lax.ppermute(near_out, "tile", near)
    mirror_in = lax.ppermute(mirror_out, "tile", mirror)
    core_in = lax.ppermute(core_out, "tile", core)
    return turn_in, far_in, near_in, mirror_in, core_in


def call(kernel, name, outs, ins, scratch=(), out_hbm=False, cost=0, aliases=None):
    hbm = pl.BlockSpec(memory_space=pltpu.HBM)
    vmem = pl.BlockSpec(memory_space=pltpu.VMEM)
    return pl.pallas_call(
        kernel,
        out_shape=outs,
        in_specs=[vmem] * len(ins),
        out_specs=[hbm if out_hbm else vmem] * len(outs),
        scratch_shapes=list(scratch),
        compiler_params=pltpu.CompilerParams(vmem_limit_bytes=VMEM_LIMIT),
        cost_estimate=pl.CostEstimate(flops=cost, bytes_accessed=cost // 500, transcendentals=0),
        input_output_aliases=aliases or {},
        name=name,
    )(*ins)


def on_device(state, wave_coef, visc_coef, stencil_start, stencil_offset):
    side = math.isqrt(lax.axis_size("tile"))
    field = state[0]

    def array(*shape, dtype=jnp.float32):
        return jax.ShapeDtypeStruct(shape, dtype)

    tile = array(BLK, BLK)
    strip = array(ROWS, BLK)
    whole = array(*field.shape)
    work = [
        pltpu.VMEM((BLK, BLK), jnp.float32),
        pltpu.VMEM((BLK, BLK), jnp.float32),
        pltpu.VMEM((4, FACES, 16, BLK), jnp.float32),
    ]
    values = call(
        tables_kernel,
        "tables",
        [array(*shape, dtype=kind) for _, shape, kind in TABLES],
        [],
        cost=4_000_000_000,
    )
    made = dict(zip((name for name, _, _ in TABLES), values))
    values = call(
        lambda *refs: constants_kernel(side, *refs),
        "constants",
        [array(*shape, dtype=kind) for _, shape, kind in CONSTANTS],
        [wave_coef[None], visc_coef[None], stencil_start, stencil_offset],
        cost=1_000_000_000,
    )
    made.update(zip((name for name, _, _ in CONSTANTS), values))
    sent = call(
        lambda *refs: first_kernel(side, *refs),
        "first_edges",
        [strip] * 7,
        [field, made["coef"], made["order"]],
        work,
        cost=1_000_000_000,
    )
    adds = []
    names = ("coef", "band_x", "band_y", "order", "spread")
    for step in range(SUBSTEPS):
        first, last = step == 0, step == SUBSTEPS - 1
        received = exchange(sent[:5], side)
        field, *edges = call(
            lambda *refs, first=first, last=last: inner_kernel(first, last, *refs),
            "inner",
            [whole] + ([] if last else [tile] * 2),
            [field, *(made[name] for name in names), *adds],
            cost=2_000_000_000,
            aliases=None if first else {0: 0},
        )
        ghosts = [*received, *sent[5:], made["taps"], made["weights"]]
        if last:
            break
        updates = call(
            lambda *refs: edge_kernel(side, *refs),
            "edges",
            [tile] * 2 + [strip] * 7,
            [*ghosts, made["reach"], made["same"], made["gain"], *edges],
            work,
        )
        adds, sent = updates[:2], updates[2:]
    (field,) = call(
        lambda *refs: final_kernel(side, *refs),
        "final",
        [whole],
        [*ghosts, made["spread"], field],
        [pltpu.VMEM(field.shape, jnp.float32), pltpu.SemaphoreType.DMA((FACES,))],
        out_hbm=True,
    )
    return field[None]


def solution(mesh):
    placed = (P(("member", "tile"), None, None, None, None), P(), P(), P(), P())
    return jax.shard_map(
        on_device,
        mesh=mesh,
        in_specs=placed,
        out_specs=P(("member", "tile"), None, None, None, None),
        check_vma=False,
    )
```

```python
import math

import jax
import jax.numpy as jnp
from jax import lax
from jax.experimental import pallas as pl
from jax.experimental.pallas import tpu as pltpu
from jax.sharding import PartitionSpec as P

SUBSTEPS = 4
FACES = 6
LEV = 3
DEPTH = 3
BLK = 128
PER_FACE = LEV * DEPTH
ROWS = 56
TAPS = 4
HALF = 64
WEST, EAST, SOUTH, NORTH = 0, 1, 2, 3
SCALE = 20.0
VMEM_LIMIT = 16 * 1024 * 1024


def whole_vmem():
    return pl.BlockSpec(memory_space=pltpu.VMEM)


def iota(shape, dim):
    return lax.broadcasted_iota(jnp.int32, shape, dim)


def weight_of(distance):
    return jnp.where(
        distance == 1, 9.0, jnp.where(distance == 2, 7.0, jnp.where(distance == 3, 4.0, 0.0))
    )


def split2(x):
    high = x.astype(jnp.bfloat16)
    low = (x - high.astype(jnp.float32)).astype(jnp.bfloat16)
    return high, low


def lagrange_weights(t):
    return (
        -(t - 1.0) * (t - 2.0) * (t - 3.0) / 6.0,
        t * (t - 2.0) * (t - 3.0) / 2.0,
        -t * (t - 1.0) * (t - 3.0) / 2.0,
        t * (t - 1.0) * (t - 2.0) / 6.0,
    )


def band_matrix():
    gap = jnp.abs(iota((BLK, BLK), 0) - iota((BLK, BLK), 1))
    return jnp.where(gap == 0, -40.0, weight_of(gap)).astype(jnp.bfloat16)


def position(side):
    index = lax.axis_index("tile")
    return lax.rem(index, side), lax.div(index, side)


def is_inner(row, col, side):
    return 0 < row < side - 1 and 0 < col < side - 1


def row_codes(shape):
    row = iota(shape, 0)
    block = (row * 57) >> 9
    odd = (block & 1) == 1
    depth = row - 3 * ((row * 171) >> 9)
    return odd, depth


def plane_row(shape, dim):
    row = iota(shape, dim)
    lower = row < HALF
    inside = jnp.where(lower, row, row - HALF)
    plane = (inside * 171) >> 9
    return lower, plane, inside - 3 * plane


def tiles_of(plane_value):
    return plane_value.reshape(BLK // 8, 8, BLK)


def lane_of_tile():
    return iota((1, 8, BLK), 2)


def take_edges(q, plane, columns, rows_ref):
    lane, at = lane_of_tile(), 6 * plane
    turned = pltpu.roll(q, (at + 3) % BLK, 2)
    columns = jnp.where((lane >= at) & (lane < at + 6), turned, columns)
    low, high = 3 * plane, HALF + 3 * plane
    rows_ref[low : low + 3, :] = q[0, :3, :]
    rows_ref[high : high + 3, :] = q[BLK // 8 - 1, 5:, :]
    return columns


def lane_order():
    lower, plane, cell = plane_row((BLK, BLK), 0)
    lane = 6 * plane + cell + jnp.where(lower, 3, 0)
    right = (lane == iota((BLK, BLK), 1)) & (plane < FACES * LEV)
    return jnp.where(right, 1.0, 0.0).astype(jnp.bfloat16)


def rows_from_columns(columns, order):
    high, low = split2(columns.reshape(BLK, BLK))
    return lax.dot_general(
        order,
        jnp.concatenate([high, low], axis=1),
        (((1,), (1,)), ((), ())),
        preferred_element_type=jnp.float32,
    )


def clear_rest(rows_ref):
    used = FACES * PER_FACE
    rest = jnp.zeros((HALF - used, BLK), jnp.float32)
    rows_ref[used:HALF, :] = rest
    rows_ref[HALF + used :, :] = rest


def pack(columns_ref, rows_ref, side, outs, strips_ref):
    turn_ref, far_ref, near_ref, mirror_ref, core_ref, own_a_ref, own_b_ref = outs
    col, row = position(side)
    for face in range(FACES):
        at = PER_FACE * face
        strips_ref[WEST, face, :PER_FACE, :] = columns_ref[at : at + PER_FACE, :]
        strips_ref[EAST, face, :PER_FACE, :] = columns_ref[HALF + at : HALF + at + PER_FACE, :]
        strips_ref[SOUTH, face, :PER_FACE, :] = rows_ref[at : at + PER_FACE, :]
        strips_ref[NORTH, face, :PER_FACE, :] = rows_ref[HALF + at : HALF + at + PER_FACE, :]
    even_col, even_row = lax.rem(col, 2) == 0, lax.rem(row, 2) == 0

    def shift(place):
        return jnp.where(place == 0, 1, jnp.where(place == side - 1, FACES - 1, 0))

    middle = (col > 0) & (col < side - 1)
    up, down = jnp.where(even_row, NORTH, SOUTH), jnp.where(even_row, SOUTH, NORTH)
    plans = (
        (core_ref, jnp.where(even_col, EAST, WEST), 0),
        (mirror_ref, jnp.where(even_col, WEST, EAST), shift(col)),
        (near_ref, jnp.where(middle, down, up), jnp.where(middle, shift(row), 0)),
        (far_ref, jnp.where(middle, up, down), jnp.where(middle, 0, shift(row))),
    )
    rest = jnp.zeros((ROWS - FACES * PER_FACE, BLK), jnp.float32)
    for out_ref, which, by in plans:
        for face in range(FACES):
            at = PER_FACE * face
            source = face + by
            source = jnp.where(source >= FACES, source - FACES, source)
            out_ref[at : at + PER_FACE, :] = strips_ref[which, source, :PER_FACE, :]
        out_ref[FACES * PER_FACE :, :] = rest
    for face in range(FACES):
        at = PER_FACE * face
        if face % 2:
            a, b = (SOUTH, face + 2), (EAST, face - 2)
        else:
            a, b = (NORTH, face - 2), (WEST, face + 2)
        own_a_ref[at : at + PER_FACE, :] = strips_ref[a[0], a[1] % FACES, :PER_FACE, :]
        own_b_ref[at : at + PER_FACE, :] = strips_ref[b[0], b[1] % FACES, :PER_FACE, :]
    own_a_ref[FACES * PER_FACE :, :] = rest
    own_b_ref[FACES * PER_FACE :, :] = rest
    odd, _ = row_codes((ROWS, BLK))
    use_a = jnp.where(odd, (row == 0).astype(jnp.int32), (row == side - 1).astype(jnp.int32))
    turn_ref[...] = jnp.where(use_a == 1, own_a_ref[...], own_b_ref[...])


TABLES = (
    ("corner", (BLK, BLK), jnp.int32),
    ("order", (BLK, 2 * BLK), jnp.bfloat16),
    ("spread", (2 * BLK, BLK), jnp.bfloat16),
    ("band_x", (2 * BLK, BLK), jnp.bfloat16),
    ("band_y", (BLK, 2 * BLK), jnp.bfloat16),
)
CONSTANTS = (
    ("coef", (8, BLK), jnp.float32),
    ("gain", (BLK, BLK), jnp.float32),
    ("taps", (TAPS, 2 * ROWS, BLK), jnp.int32),
    ("weights", (TAPS, 2 * ROWS, BLK), jnp.float32),
)


def tables_kernel(corner, order, spread, band_x, band_y):
    for ref, value, axis in (
        (order, lane_order(), 1),
        (band_x, band_matrix(), 0),
        (band_y, band_matrix(), 1),
    ):
        ref[...] = jnp.concatenate([value, value], axis=axis)
    spread[...] = jnp.concatenate([lane_order()] * 2, axis=0)
    _, plane, _ = plane_row((BLK, BLK), 0)
    to = iota((BLK, BLK), 1)
    low, high = 3 * plane + to, HALF + 3 * plane + to - (BLK - 3)
    corner[...] = jnp.where(to < 3, low, jnp.where(to >= BLK - 3, high, 0))


def seam_rows(place, low_turned):
    odd, depth = row_codes((ROWS, BLK))
    at_low = (place == 0).astype(jnp.int32)
    is_turned = odd.astype(jnp.int32) == at_low ^ (1 - low_turned)
    return is_turned, jnp.where(place == 0, DEPTH - 1 - depth, depth)


def constants_kernel(
    side, wave_ref, visc_ref, start_ref, offset_ref, coef_ref, gain_ref, taps_ref, weights_ref
):
    col, row = position(side)
    for axis, place in enumerate((col, row)):
        is_turned, h_of = seam_rows(place, axis)
        first, offset = [
            jnp.where(h_of == 0, ref[0:1, :], jnp.where(h_of == 1, ref[1:2, :], ref[2:3, :]))
            for ref in (start_ref, offset_ref)
        ]
        at = axis * ROWS
        for m, weight in enumerate(lagrange_weights(offset)):
            tap = jnp.where(is_turned, BLK - 1 - first - m, first + m)
            taps_ref[m, at : at + ROWS, :] = tap
            weights_ref[m, at : at + ROWS, :] = weight
    _, plane, _ = plane_row((BLK, BLK), 0)
    level_of = plane - 3 * ((plane * 171) >> 9)
    gain = jnp.zeros((BLK, BLK), jnp.float32)
    for level in range(LEV):
        a, b = [
            jnp.broadcast_to(ref[:, level : level + 1] * (1.0 / SCALE), (1, BLK))
            for ref in (wave_ref, visc_ref)
        ]
        coef_ref[level : level + 1, :] = a
        coef_ref[LEV + level : LEV + level + 1, :] = b
        gain = jnp.where(level_of == level, a + b, gain)
    coef_ref[2 * LEV :, :] = jnp.zeros((8 - 2 * LEV, BLK), jnp.float32)
    gain_ref[...] = gain


def first_kernel(side, state_ref, coef_ref, order_ref, *rest):
    outs = rest[:7]
    columns_ref, rows_ref, strips_ref = rest[7:]
    clear_rest(rows_ref)
    columns = jnp.zeros((BLK // 8, 8, BLK), jnp.float32)
    for plane in range(FACES * LEV):
        face, level = divmod(plane, LEV)
        a, b = coef_ref[level : level + 1, :], coef_ref[LEV + level : LEV + level + 1, :]
        q = a * state_ref[face, level] + b * state_ref[face, LEV + level]
        columns = take_edges(tiles_of(q), plane, columns, rows_ref)
    columns_ref[...] = rows_from_columns(columns, order_ref[...])
    pack(columns_ref, rows_ref, side, outs, strips_ref)


def ghosts_of(side, received, own_a_ref, own_b_ref, taps_ref, weights_ref):
    far, turned, near, mirror, core = [ref[...] for ref in received]
    col, row = position(side)
    even_col, even_row = lax.rem(col, 2) == 0, lax.rem(row, 2) == 0
    middle = (col > 0) & (col < side - 1)
    near, far = jnp.where(middle, far, near), jnp.where(middle, near, far)
    alone = ((row == 0) & (col == side - 1)) | ((col == 0) & (row == side - 1))
    pairs = (
        (
            jnp.where(even_col, mirror, core),
            jnp.where(even_col, core, mirror),
            jnp.where(alone, own_a_ref[...], turned),
            col,
            0,
        ),
        (
            jnp.where(even_row, far, near),
            jnp.where(even_row, near, far),
            jnp.where(alone, own_b_ref[...], turned),
            row,
            1,
        ),
    )
    seams = []
    for low, high, crossed, place, low_turned in pairs:
        is_turned, _ = seam_rows(place, low_turned)
        seams.append(jnp.where(is_turned, crossed, jnp.where(place == 0, low, high)))
    raw = jnp.concatenate(seams, axis=0)
    mixed = jnp.zeros((2 * ROWS, BLK), jnp.float32)
    for m in range(TAPS):
        source = jnp.take_along_axis(raw, taps_ref[m], axis=1, mode="promise_in_bounds")
        mixed = mixed + weights_ref[m] * source
    rest = jnp.zeros((HALF - ROWS, BLK), jnp.float32)
    ghosts = []
    for index, (low, high, _, place, _) in enumerate(pairs):
        made = mixed[index * ROWS : (index + 1) * ROWS, :]
        ghosts.append(
            jnp.concatenate(
                [
                    jnp.where(place == 0, made, low),
                    rest,
                    jnp.where(place == side - 1, made, high),
                    rest,
                ],
                axis=0,
            )
        )
    return ghosts


def ghost_additions(ghosts):
    row = iota((HALF, 1), 0)
    cell = row - 3 * ((row * 171) >> 9)
    halves = []
    both = jnp.concatenate(ghosts, axis=1)
    for half, step, index in ((both[:HALF], -1, cell), (both[HALF:], 1, 2 - cell)):
        one = pltpu.roll(half, step % HALF, 0)
        two = pltpu.roll(half, (2 * step) % HALF, 0)
        near, next_ = jnp.where(index <= 1, 7.0, 0.0), jnp.where(index == 0, 9.0, 0.0)
        halves.append(4.0 * half + near * one + next_ * two)
    adds = jnp.concatenate(halves, axis=0)
    return adds[:, :BLK], adds[:, BLK:]


def corner_part(adds, corner):
    turned = adds.T
    cell = plane_row((HALF, BLK), 0)[2]
    halves = []
    for first in (0, BLK - 3):
        lines = [turned[first + at : first + at + 1, :] for at in range(3)]
        halves.append(jnp.where(cell == 0, lines[0], jnp.where(cell == 1, lines[1], lines[2])))
    lines = jnp.concatenate(halves, axis=0)
    taken = jnp.take_along_axis(lines, corner, axis=1, mode="promise_in_bounds")
    lane = iota((1, BLK), 1)
    return jnp.where((lane < 3) | (lane >= BLK - 3), taken, 0.0)


def edge_kernel(side, *refs):
    across, along = ghosts_of(side, refs[:5], *refs[5:9])
    corner_ref, gain_ref, old_columns_ref, old_rows_ref = refs[9:13]
    add_x_ref, add_y_ref = refs[13:15]
    outs = refs[15:22]
    columns_ref, rows_ref, strips_ref = refs[22:]
    add_x, add_y = ghost_additions((across, along))
    gain, corner = gain_ref[...], corner_ref[...]
    columns_ref[...] = old_columns_ref[...] + gain * (add_x + corner_part(add_y, corner))
    rows_ref[...] = old_rows_ref[...] + gain * (add_y + corner_part(add_x, corner))
    add_x_ref[...] = add_x
    add_y_ref[...] = add_y
    pack(columns_ref, rows_ref, side, outs, strips_ref)


def spread_lanes(add_x, spread_ref):
    high, low = split2(add_x.T)
    return tiles_of(
        jnp.dot(
            jnp.concatenate([high, low], axis=1),
            spread_ref[...],
            preferred_element_type=jnp.float32,
        )
    )


def edge_additions(plane, add_x, add_y):
    lane = lane_of_tile()
    turned = pltpu.roll(add_x, (BLK - 3 - 6 * plane) % BLK, 2)
    add = jnp.where((lane < 3) | (lane >= BLK - 3), turned, 0.0)
    at = 3 * plane
    pad = jnp.zeros((5, BLK), jnp.float32)
    bottom = add[:1] + jnp.concatenate([add_y[at : at + 3], pad], axis=0)[None]
    top = add[-1:] + jnp.concatenate([pad, add_y[HALF + at : HALF + at + 3]], axis=0)[None]
    return jnp.concatenate([bottom, add[1:-1], top], axis=0)


def inner_kernel(first, last, state_ref, *refs):
    coef_ref, band_x_ref, band_y_ref, order_ref, spread_ref = refs[:5]
    refs = refs[5:]
    if not first:
        add_x, add_y = spread_lanes(refs[0][...], spread_ref), refs[1][...]
        refs = refs[2:]
    new_ref = refs[0]
    if not last:
        columns_ref, rows_ref = refs[1:]
    if not last:
        clear_rest(rows_ref)
    columns = jnp.zeros((BLK // 8, 8, BLK), jnp.float32)
    group = 2
    for begin in range(0, FACES * LEV, group):
        fields, highs, lows = [], [], []
        for plane in range(begin, begin + group):
            face, level = divmod(plane, LEV)
            a, b = coef_ref[level : level + 1, :], coef_ref[LEV + level : LEV + level + 1, :]
            pressure = tiles_of(state_ref[face, level])
            rate = tiles_of(state_ref[face, LEV + level])
            if not first:
                add = edge_additions(plane, add_x, add_y)
                pressure, rate = pressure + add, rate + add
            high, low = split2((a * pressure + b * rate).reshape(BLK, BLK))
            fields.append((pressure, rate))
            highs.append(high)
            lows.append(low)
        by_x = jnp.dot(
            jnp.concatenate(
                [jnp.concatenate(pair, axis=1) for pair in zip(highs, lows)], axis=0
            ),
            band_x_ref[...],
            preferred_element_type=jnp.float32,
        )
        by_y = jnp.dot(
            band_y_ref[...],
            jnp.concatenate(
                [jnp.concatenate(highs, axis=1), jnp.concatenate(lows, axis=1)], axis=0
            ),
            preferred_element_type=jnp.float32,
        )
        for place, (pressure, rate) in enumerate(fields):
            plane = begin + place
            face, level = divmod(plane, LEV)
            a, b = coef_ref[level : level + 1, :], coef_ref[LEV + level : LEV + level + 1, :]
            at = place * BLK
            rate = rate + tiles_of(by_x[at : at + BLK, :] + by_y[:, at : at + BLK])
            pressure = pressure + rate
            new_ref[face, level] = pressure.reshape(BLK, BLK)
            new_ref[face, LEV + level] = rate.reshape(BLK, BLK)
            if not last:
                columns = take_edges(a * pressure + b * rate, plane, columns, rows_ref)
    if not last:
        columns_ref[...] = rows_from_columns(columns, order_ref[...])


def final_kernel(side, *refs):
    spread_ref, state_ref, out_hbm, buffer, sems = refs[9:]
    add_x, add_y = ghost_additions(ghosts_of(side, refs[:5], *refs[5:9]))
    add_x = spread_lanes(add_x, spread_ref)
    copies = []
    for face in range(FACES):
        for level in range(LEV):
            add = edge_additions(face * LEV + level, add_x, add_y)
            for channel in (level, LEV + level):
                value = tiles_of(state_ref[face, channel]) + add
                buffer[face, channel] = value.reshape(BLK, BLK)
        copy = pltpu.make_async_copy(buffer.at[face], out_hbm.at[face], sems.at[face])
        copy.start()
        copies.append(copy)
    for copy in copies:
        copy.wait()


def exchange(payloads, side):
    def at(row, col):
        return row * side + col

    cells = [(row, col) for row in range(side) for col in range(side)]

    def swap(place, odd_first):
        return (place ^ 1) if not odd_first else (place + (1 if place % 2 else -1)) % side

    core = [(at(r, c), at(r, swap(c, False))) for r, c in cells]
    mirror = [(at(r, c), at(r, swap(c, True))) for r, c in cells]
    edge = side - 1
    near = [(at(r, c), at(swap(r, 0 < c < edge), c)) for r, c in cells]
    far = [(at(r, c), at(swap(r, not 0 < c < edge), c)) for r, c in cells]
    turn = set()
    for x in range(edge):
        turn |= {(at(0, x), at(edge - x, edge)), (at(edge - x, edge), at(0, x))}
    for x in range(1, side):
        turn |= {(at(edge, x), at(edge - x, 0)), (at(edge - x, 0), at(edge, x))}
    spare = [pair for pair in mirror if is_inner(pair[0] // side, pair[0] % side, side)]
    first_end, last_end = at(1, edge - 1), at(edge - 1, 1)
    left = [b for a, b in spare if a in (first_end, last_end)]
    spare = [pair for pair in spare if not {*pair} & {first_end, last_end}]
    spare += [(at(0, edge), first_end), (at(edge, 0), last_end), (left[0], left[1])]
    turn |= {(a, b) for a, b in spare} | {(b, a) for a, b in spare}
    turn_out, far_out, near_out, mirror_out, core_out = payloads
    turn_in = lax.ppermute(turn_out, "tile", sorted(turn))
    far_in = lax.ppermute(far_out, "tile", far)
    near_in = lax.ppermute(near_out, "tile", near)
    mirror_in = lax.ppermute(mirror_out, "tile", mirror)
    core_in = lax.ppermute(core_out, "tile", core)
    return far_in, turn_in, near_in, mirror_in, core_in


def call(kernel, name, outs, ins, scratch=(), out_hbm=False, cost=0, aliases=None):
    hbm = pl.BlockSpec(memory_space=pltpu.HBM)
    vmem = pl.BlockSpec(memory_space=pltpu.VMEM)
    return pl.pallas_call(
        kernel,
        out_shape=outs,
        in_specs=[vmem] * len(ins),
        out_specs=[hbm if out_hbm else vmem] * len(outs),
        scratch_shapes=list(scratch),
        compiler_params=pltpu.CompilerParams(vmem_limit_bytes=VMEM_LIMIT),
        cost_estimate=pl.CostEstimate(flops=cost, bytes_accessed=cost // 500, transcendentals=0),
        input_output_aliases=aliases or {},
        name=name,
    )(*ins)


def on_device(state, wave_coef, visc_coef, stencil_start, stencil_offset):
    side = math.isqrt(lax.axis_size("tile"))
    field = state[0]

    def array(*shape, dtype=jnp.float32):
        return jax.ShapeDtypeStruct(shape, dtype)

    tile = array(BLK, BLK)
    strip = array(ROWS, BLK)
    whole = array(*field.shape)
    work = [
        pltpu.VMEM((BLK, BLK), jnp.float32),
        pltpu.VMEM((BLK, BLK), jnp.float32),
        pltpu.VMEM((4, FACES, 16, BLK), jnp.float32),
    ]
    values = call(
        tables_kernel,
        "tables",
        [array(*shape, dtype=kind) for _, shape, kind in TABLES],
        [],
        cost=4_000_000_000,
    )
    made = dict(zip((name for name, _, _ in TABLES), values))
    values = call(
        lambda *refs: constants_kernel(side, *refs),
        "constants",
        [array(*shape, dtype=kind) for _, shape, kind in CONSTANTS],
        [wave_coef[None], visc_coef[None], stencil_start, stencil_offset],
        cost=1_000_000_000,
    )
    made.update(zip((name for name, _, _ in CONSTANTS), values))
    sent = call(
        lambda *refs: first_kernel(side, *refs),
        "first_edges",
        [strip] * 7,
        [field, made["coef"], made["order"]],
        work,
        cost=1_000_000_000,
    )
    adds = []
    names = ("coef", "band_x", "band_y", "order", "spread")
    for step in range(SUBSTEPS):
        first, last = step == 0, step == SUBSTEPS - 1
        received = exchange(sent[:5], side)
        field, *edges = call(
            lambda *refs, first=first, last=last: inner_kernel(first, last, *refs),
            "inner",
            [whole] + ([] if last else [tile] * 2),
            [field, *(made[name] for name in names), *adds],
            cost=2_000_000_000,
            aliases=None if first else {0: 0},
        )
        ghosts = [*received, *sent[5:], made["taps"], made["weights"]]
        if last:
            break
        updates = call(
            lambda *refs: edge_kernel(side, *refs),
            "edges",
            [tile] * 2 + [strip] * 7,
            [*ghosts, made["corner"], made["gain"], *edges],
            work,
        )
        adds, sent = updates[:2], updates[2:]
    (field,) = call(
        lambda *refs: final_kernel(side, *refs),
        "final",
        [whole],
        [*ghosts, made["spread"], field],
        [pltpu.VMEM(field.shape, jnp.float32), pltpu.SemaphoreType.DMA((FACES,))],
        out_hbm=True,
    )
    return field[None]


def solution(mesh):
    placed = (P(("member", "tile"), None, None, None, None), P(), P(), P(), P())
    return jax.shard_map(
        on_device,
        mesh=mesh,
        in_specs=placed,
        out_specs=P(("member", "tile"), None, None, None, None),
        check_vma=False,
    )
```

```python
import math

import jax
import jax.numpy as jnp
from jax import lax
from jax.experimental import pallas as pl
from jax.experimental.pallas import tpu as pltpu
from jax.sharding import PartitionSpec as P

SUBSTEPS = 4
FACES = 6
LEV = 3
DEPTH = 3
BLK = 128
PER_FACE = LEV * DEPTH
ROWS = 56
TAPS = 4
HALF = 64
WEST, EAST, SOUTH, NORTH = 0, 1, 2, 3
SCALE = 20.0
VMEM_LIMIT = 16 * 1024 * 1024


def whole_vmem():
    return pl.BlockSpec(memory_space=pltpu.VMEM)


def iota(shape, dim):
    return lax.broadcasted_iota(jnp.int32, shape, dim)


def weight_of(distance):
    return jnp.where(
        distance == 1, 9.0, jnp.where(distance == 2, 7.0, jnp.where(distance == 3, 4.0, 0.0))
    )


def split2(x):
    high = x.astype(jnp.bfloat16)
    low = (x - high.astype(jnp.float32)).astype(jnp.bfloat16)
    return high, low


def lagrange_weights(t):
    return (
        -(t - 1.0) * (t - 2.0) * (t - 3.0) / 6.0,
        t * (t - 2.0) * (t - 3.0) / 2.0,
        -t * (t - 1.0) * (t - 3.0) / 2.0,
        t * (t - 1.0) * (t - 2.0) / 6.0,
    )


def band_matrix():
    gap = jnp.abs(iota((BLK, BLK), 0) - iota((BLK, BLK), 1))
    return jnp.where(gap == 0, -40.0, weight_of(gap)).astype(jnp.bfloat16)


def position(side):
    index = lax.axis_index("tile")
    return lax.rem(index, side), lax.div(index, side)


def is_inner(row, col, side):
    return 0 < row < side - 1 and 0 < col < side - 1


def row_codes(shape):
    row = iota(shape, 0)
    block = (row * 57) >> 9
    odd = (block & 1) == 1
    depth = row - 3 * ((row * 171) >> 9)
    return odd, depth


def plane_row(shape, dim):
    row = iota(shape, dim)
    lower = row < HALF
    inside = jnp.where(lower, row, row - HALF)
    plane = (inside * 171) >> 9
    return lower, plane, inside - 3 * plane


def tiles_of(plane_value):
    return plane_value.reshape(BLK // 8, 8, BLK)


def lane_of_tile():
    return iota((1, 8, BLK), 2)


def take_edges(q, plane, columns, rows_ref):
    lane, at = lane_of_tile(), 6 * plane
    turned = pltpu.roll(q, (at + 3) % BLK, 2)
    columns = jnp.where((lane >= at) & (lane < at + 6), turned, columns)
    low, high = 3 * plane, HALF + 3 * plane
    rows_ref[low : low + 3, :] = q[0, :3, :]
    rows_ref[high : high + 3, :] = q[BLK // 8 - 1, 5:, :]
    return columns


def lane_order():
    lower, plane, cell = plane_row((BLK, BLK), 0)
    lane = 6 * plane + cell + jnp.where(lower, 3, 0)
    right = (lane == iota((BLK, BLK), 1)) & (plane < FACES * LEV)
    return jnp.where(right, 1.0, 0.0).astype(jnp.bfloat16)


def rows_from_columns(columns, order):
    high, low = split2(columns.reshape(BLK, BLK))
    return lax.dot_general(
        order,
        jnp.concatenate([high, low], axis=1),
        (((1,), (1,)), ((), ())),
        preferred_element_type=jnp.float32,
    )


def clear_rest(rows_ref):
    used = FACES * PER_FACE
    rest = jnp.zeros((HALF - used, BLK), jnp.float32)
    rows_ref[used:HALF, :] = rest
    rows_ref[HALF + used :, :] = rest


def pack(columns, rows, side, outs, strips_ref):
    turn_ref, far_ref, near_ref, mirror_ref, core_ref, own_a_ref, own_b_ref = outs
    col, row = position(side)
    for face in range(FACES):
        at = PER_FACE * face
        strips_ref[WEST, face, :PER_FACE, :] = columns[at : at + PER_FACE, :]
        strips_ref[EAST, face, :PER_FACE, :] = columns[HALF + at : HALF + at + PER_FACE, :]
        strips_ref[SOUTH, face, :PER_FACE, :] = rows[at : at + PER_FACE, :]
        strips_ref[NORTH, face, :PER_FACE, :] = rows[HALF + at : HALF + at + PER_FACE, :]
    even_col, even_row = lax.rem(col, 2) == 0, lax.rem(row, 2) == 0

    def shift(place):
        return jnp.where(place == 0, 1, jnp.where(place == side - 1, FACES - 1, 0))

    middle = (col > 0) & (col < side - 1)
    up, down = jnp.where(even_row, NORTH, SOUTH), jnp.where(even_row, SOUTH, NORTH)
    plans = (
        (mirror_ref, jnp.where(even_col, WEST, EAST), shift(col)),
        (near_ref, jnp.where(middle, down, up), jnp.where(middle, shift(row), 0)),
        (far_ref, jnp.where(middle, up, down), jnp.where(middle, 0, shift(row))),
    )
    rest = jnp.zeros((ROWS - FACES * PER_FACE, BLK), jnp.float32)
    core_ref[...] = jnp.where(even_col, columns[HALF : HALF + ROWS, :], columns[:ROWS, :])
    for out_ref, which, by in plans:
        for face in range(FACES):
            at = PER_FACE * face
            source = face + by
            source = jnp.where(source >= FACES, source - FACES, source)
            out_ref[at : at + PER_FACE, :] = strips_ref[which, source, :PER_FACE, :]
        out_ref[FACES * PER_FACE :, :] = rest
    for face in range(FACES):
        at = PER_FACE * face
        if face % 2:
            a, b = (SOUTH, face + 2), (EAST, face - 2)
        else:
            a, b = (NORTH, face - 2), (WEST, face + 2)
        own_a_ref[at : at + PER_FACE, :] = strips_ref[a[0], a[1] % FACES, :PER_FACE, :]
        own_b_ref[at : at + PER_FACE, :] = strips_ref[b[0], b[1] % FACES, :PER_FACE, :]
    own_a_ref[FACES * PER_FACE :, :] = rest
    own_b_ref[FACES * PER_FACE :, :] = rest
    odd, _ = row_codes((ROWS, BLK))
    use_a = jnp.where(odd, (row == 0).astype(jnp.int32), (row == side - 1).astype(jnp.int32))
    turn_ref[...] = jnp.where(use_a == 1, own_a_ref[...], own_b_ref[...])


TABLES = (
    ("corner", (BLK, BLK), jnp.int32),
    ("order", (BLK, 2 * BLK), jnp.bfloat16),
    ("spread", (2 * BLK, BLK), jnp.bfloat16),
    ("band_x", (2 * BLK, BLK), jnp.bfloat16),
    ("band_y", (BLK, 2 * BLK), jnp.bfloat16),
)
CONSTANTS = (
    ("coef", (8, BLK), jnp.float32),
    ("gain", (BLK, BLK), jnp.float32),
    ("taps", (TAPS, 2 * ROWS, BLK), jnp.int32),
    ("weights", (TAPS, 2 * ROWS, BLK), jnp.float32),
)


def tables_kernel(corner, order, spread, band_x, band_y):
    for ref, value, axis in (
        (order, lane_order(), 1),
        (band_x, band_matrix(), 0),
        (band_y, band_matrix(), 1),
    ):
        ref[...] = jnp.concatenate([value, value], axis=axis)
    spread[...] = jnp.concatenate([lane_order()] * 2, axis=0)
    _, plane, _ = plane_row((BLK, BLK), 0)
    to = iota((BLK, BLK), 1)
    low, high = 3 * plane + to, HALF + 3 * plane + to - (BLK - 3)
    corner[...] = jnp.where(to < 3, low, jnp.where(to >= BLK - 3, high, 0))


def seam_rows(place, low_turned):
    odd, depth = row_codes((ROWS, BLK))
    at_low = (place == 0).astype(jnp.int32)
    is_turned = odd.astype(jnp.int32) == at_low ^ (1 - low_turned)
    return is_turned, jnp.where(place == 0, DEPTH - 1 - depth, depth)


def constants_kernel(
    side, wave_ref, visc_ref, start_ref, offset_ref, coef_ref, gain_ref, taps_ref, weights_ref
):
    col, row = position(side)
    for axis, place in enumerate((col, row)):
        is_turned, h_of = seam_rows(place, axis)
        first, offset = [
            jnp.where(h_of == 0, ref[0:1, :], jnp.where(h_of == 1, ref[1:2, :], ref[2:3, :]))
            for ref in (start_ref, offset_ref)
        ]
        at = axis * ROWS
        for m, weight in enumerate(lagrange_weights(offset)):
            tap = jnp.where(is_turned, BLK - 1 - first - m, first + m)
            taps_ref[m, at : at + ROWS, :] = tap
            weights_ref[m, at : at + ROWS, :] = weight
    _, plane, _ = plane_row((BLK, BLK), 0)
    level_of = plane - 3 * ((plane * 171) >> 9)
    gain = jnp.zeros((BLK, BLK), jnp.float32)
    for level in range(LEV):
        a, b = [
            jnp.broadcast_to(ref[:, level : level + 1] * (1.0 / SCALE), (1, BLK))
            for ref in (wave_ref, visc_ref)
        ]
        coef_ref[level : level + 1, :] = a
        coef_ref[LEV + level : LEV + level + 1, :] = b
        gain = jnp.where(level_of == level, a + b, gain)
    coef_ref[2 * LEV :, :] = jnp.zeros((8 - 2 * LEV, BLK), jnp.float32)
    gain_ref[...] = gain


def first_kernel(side, state_ref, coef_ref, order_ref, *rest):
    outs = rest[:7]
    rows_ref, strips_ref = rest[7:]
    clear_rest(rows_ref)
    columns = jnp.zeros((BLK // 8, 8, BLK), jnp.float32)
    for plane in range(FACES * LEV):
        face, level = divmod(plane, LEV)
        a, b = coef_ref[level : level + 1, :], coef_ref[LEV + level : LEV + level + 1, :]
        q = a * state_ref[face, level] + b * state_ref[face, LEV + level]
        columns = take_edges(tiles_of(q), plane, columns, rows_ref)
    packed = rows_from_columns(columns, order_ref[...])
    pack(packed, rows_ref[...], side, outs, strips_ref)


def ghosts_of(side, received, own_a_ref, own_b_ref, taps_ref, weights_ref):
    far, turned, near, mirror, core = [ref[...] for ref in received]
    col, row = position(side)
    even_col, even_row = lax.rem(col, 2) == 0, lax.rem(row, 2) == 0
    middle = (col > 0) & (col < side - 1)
    near, far = jnp.where(middle, far, near), jnp.where(middle, near, far)
    alone = ((row == 0) & (col == side - 1)) | ((col == 0) & (row == side - 1))
    pairs = (
        (
            jnp.where(even_col, mirror, core),
            jnp.where(even_col, core, mirror),
            jnp.where(alone, own_a_ref[...], turned),
            col,
            0,
        ),
        (
            jnp.where(even_row, far, near),
            jnp.where(even_row, near, far),
            jnp.where(alone, own_b_ref[...], turned),
            row,
            1,
        ),
    )
    seams = []
    for low, high, crossed, place, low_turned in pairs:
        is_turned, _ = seam_rows(place, low_turned)
        seams.append(jnp.where(is_turned, crossed, jnp.where(place == 0, low, high)))
    raw = jnp.concatenate(seams, axis=0)
    mixed = jnp.zeros((2 * ROWS, BLK), jnp.float32)
    for m in range(TAPS):
        source = jnp.take_along_axis(raw, taps_ref[m], axis=1, mode="promise_in_bounds")
        mixed = mixed + weights_ref[m] * source
    rest = jnp.zeros((HALF - ROWS, BLK), jnp.float32)
    ghosts = []
    for index, (low, high, _, place, _) in enumerate(pairs):
        made = mixed[index * ROWS : (index + 1) * ROWS, :]
        ghosts.append(
            jnp.concatenate(
                [
                    jnp.where(place == 0, made, low),
                    rest,
                    jnp.where(place == side - 1, made, high),
                    rest,
                ],
                axis=0,
            )
        )
    return ghosts


def ghost_additions(ghosts):
    row = iota((HALF, 1), 0)
    cell = row - 3 * ((row * 171) >> 9)
    halves = []
    both = jnp.concatenate(ghosts, axis=1)
    for half, step, index in ((both[:HALF], -1, cell), (both[HALF:], 1, 2 - cell)):
        one = pltpu.roll(half, step % HALF, 0)
        two = pltpu.roll(half, (2 * step) % HALF, 0)
        near, next_ = jnp.where(index <= 1, 7.0, 0.0), jnp.where(index == 0, 9.0, 0.0)
        halves.append(4.0 * half + near * one + next_ * two)
    adds = jnp.concatenate(halves, axis=0)
    return adds[:, :BLK], adds[:, BLK:]


def corner_part(adds, corner):
    turned = adds.T
    cell = plane_row((HALF, BLK), 0)[2]
    halves = []
    for first in (0, BLK - 3):
        lines = [turned[first + at : first + at + 1, :] for at in range(3)]
        halves.append(jnp.where(cell == 0, lines[0], jnp.where(cell == 1, lines[1], lines[2])))
    lines = jnp.concatenate(halves, axis=0)
    taken = jnp.take_along_axis(lines, corner, axis=1, mode="promise_in_bounds")
    lane = iota((1, BLK), 1)
    return jnp.where((lane < 3) | (lane >= BLK - 3), taken, 0.0)


def edge_kernel(side, *refs):
    across, along = ghosts_of(side, refs[:5], *refs[5:9])
    corner_ref, gain_ref, old_columns_ref, old_rows_ref = refs[9:13]
    add_x_ref, add_y_ref = refs[13:15]
    outs = refs[15:22]
    strips_ref = refs[22]
    add_x, add_y = ghost_additions((across, along))
    gain, corner = gain_ref[...], corner_ref[...]
    columns = old_columns_ref[...] + gain * (add_x + corner_part(add_y, corner))
    rows = old_rows_ref[...] + gain * (add_y + corner_part(add_x, corner))
    add_x_ref[...] = add_x
    add_y_ref[...] = add_y
    pack(columns, rows, side, outs, strips_ref)


def spread_lanes(add_x, spread_ref):
    high, low = split2(add_x.T)
    return tiles_of(
        jnp.dot(
            jnp.concatenate([high, low], axis=1),
            spread_ref[...],
            preferred_element_type=jnp.float32,
        )
    )


def edge_additions(plane, add_x, add_y):
    lane = lane_of_tile()
    turned = pltpu.roll(add_x, (BLK - 3 - 6 * plane) % BLK, 2)
    add = jnp.where((lane < 3) | (lane >= BLK - 3), turned, 0.0)
    at = 3 * plane
    pad = jnp.zeros((5, BLK), jnp.float32)
    bottom = add[:1] + jnp.concatenate([add_y[at : at + 3], pad], axis=0)[None]
    top = add[-1:] + jnp.concatenate([pad, add_y[HALF + at : HALF + at + 3]], axis=0)[None]
    return jnp.concatenate([bottom, add[1:-1], top], axis=0)


def inner_kernel(first, last, state_ref, *refs):
    coef_ref, band_x_ref, band_y_ref, order_ref, spread_ref = refs[:5]
    refs = refs[5:]
    if not first:
        add_x, add_y = spread_lanes(refs[0][...], spread_ref), refs[1][...]
        refs = refs[2:]
    new_ref = refs[0]
    if not last:
        columns_ref, rows_ref = refs[1:]
    if not last:
        clear_rest(rows_ref)
    columns = jnp.zeros((BLK // 8, 8, BLK), jnp.float32)
    group = 2
    for begin in range(0, FACES * LEV, group):
        fields, highs, lows = [], [], []
        for plane in range(begin, begin + group):
            face, level = divmod(plane, LEV)
            a, b = coef_ref[level : level + 1, :], coef_ref[LEV + level : LEV + level + 1, :]
            pressure = tiles_of(state_ref[face, level])
            rate = tiles_of(state_ref[face, LEV + level])
            if not first:
                add = edge_additions(plane, add_x, add_y)
                pressure, rate = pressure + add, rate + add
            high, low = split2((a * pressure + b * rate).reshape(BLK, BLK))
            fields.append((pressure, rate))
            highs.append(high)
            lows.append(low)
        by_x = jnp.dot(
            jnp.concatenate(
                [jnp.concatenate(pair, axis=1) for pair in zip(highs, lows)], axis=0
            ),
            band_x_ref[...],
            preferred_element_type=jnp.float32,
        )
        by_y = jnp.dot(
            band_y_ref[...],
            jnp.concatenate(
                [jnp.concatenate(highs, axis=1), jnp.concatenate(lows, axis=1)], axis=0
            ),
            preferred_element_type=jnp.float32,
        )
        for place, (pressure, rate) in enumerate(fields):
            plane = begin + place
            face, level = divmod(plane, LEV)
            a, b = coef_ref[level : level + 1, :], coef_ref[LEV + level : LEV + level + 1, :]
            at = place * BLK
            rate = rate + tiles_of(by_x[at : at + BLK, :] + by_y[:, at : at + BLK])
            pressure = pressure + rate
            new_ref[face, level] = pressure.reshape(BLK, BLK)
            new_ref[face, LEV + level] = rate.reshape(BLK, BLK)
            if not last:
                columns = take_edges(a * pressure + b * rate, plane, columns, rows_ref)
    if not last:
        columns_ref[...] = rows_from_columns(columns, order_ref[...])


def final_kernel(side, *refs):
    spread_ref, state_ref, out_hbm, buffer, sems = refs[9:]
    add_x, add_y = ghost_additions(ghosts_of(side, refs[:5], *refs[5:9]))
    add_x = spread_lanes(add_x, spread_ref)
    copies = []
    for face in range(FACES):
        for level in range(LEV):
            add = edge_additions(face * LEV + level, add_x, add_y)
            for channel in (level, LEV + level):
                value = tiles_of(state_ref[face, channel]) + add
                buffer[face, channel] = value.reshape(BLK, BLK)
        copy = pltpu.make_async_copy(buffer.at[face], out_hbm.at[face], sems.at[face])
        copy.start()
        copies.append(copy)
    for copy in copies:
        copy.wait()


def exchange(payloads, side):
    def at(row, col):
        return row * side + col

    cells = [(row, col) for row in range(side) for col in range(side)]

    def swap(place, odd_first):
        return (place ^ 1) if not odd_first else (place + (1 if place % 2 else -1)) % side

    core = [(at(r, c), at(r, swap(c, False))) for r, c in cells]
    mirror = [(at(r, c), at(r, swap(c, True))) for r, c in cells]
    edge = side - 1
    near = [(at(r, c), at(swap(r, 0 < c < edge), c)) for r, c in cells]
    far = [(at(r, c), at(swap(r, not 0 < c < edge), c)) for r, c in cells]
    turn = set()
    for x in range(edge):
        turn |= {(at(0, x), at(edge - x, edge)), (at(edge - x, edge), at(0, x))}
    for x in range(1, side):
        turn |= {(at(edge, x), at(edge - x, 0)), (at(edge - x, 0), at(edge, x))}
    spare = [pair for pair in mirror if is_inner(pair[0] // side, pair[0] % side, side)]
    first_end, last_end = at(1, edge - 1), at(edge - 1, 1)
    left = [b for a, b in spare if a in (first_end, last_end)]
    spare = [pair for pair in spare if not {*pair} & {first_end, last_end}]
    spare += [(at(0, edge), first_end), (at(edge, 0), last_end), (left[0], left[1])]
    turn |= {(a, b) for a, b in spare} | {(b, a) for a, b in spare}
    turn_out, far_out, near_out, mirror_out, core_out = payloads
    turn_in = lax.ppermute(turn_out, "tile", sorted(turn))
    far_in = lax.ppermute(far_out, "tile", far)
    near_in = lax.ppermute(near_out, "tile", near)
    mirror_in = lax.ppermute(mirror_out, "tile", mirror)
    core_in = lax.ppermute(core_out, "tile", core)
    return far_in, turn_in, near_in, mirror_in, core_in


def call(kernel, name, outs, ins, scratch=(), out_hbm=False, cost=0, aliases=None):
    hbm = pl.BlockSpec(memory_space=pltpu.HBM)
    vmem = pl.BlockSpec(memory_space=pltpu.VMEM)
    return pl.pallas_call(
        kernel,
        out_shape=outs,
        in_specs=[vmem] * len(ins),
        out_specs=[hbm if out_hbm else vmem] * len(outs),
        scratch_shapes=list(scratch),
        compiler_params=pltpu.CompilerParams(vmem_limit_bytes=VMEM_LIMIT),
        cost_estimate=pl.CostEstimate(flops=cost, bytes_accessed=cost // 500, transcendentals=0),
        input_output_aliases=aliases or {},
        name=name,
    )(*ins)


def on_device(state, wave_coef, visc_coef, stencil_start, stencil_offset):
    side = math.isqrt(lax.axis_size("tile"))
    field = state[0]

    def array(*shape, dtype=jnp.float32):
        return jax.ShapeDtypeStruct(shape, dtype)

    tile = array(BLK, BLK)
    strip = array(ROWS, BLK)
    whole = array(*field.shape)
    strips = pltpu.VMEM((4, FACES, 16, BLK), jnp.float32)
    values = call(
        tables_kernel,
        "tables",
        [array(*shape, dtype=kind) for _, shape, kind in TABLES],
        [],
        cost=4_000_000_000,
    )
    made = dict(zip((name for name, _, _ in TABLES), values))
    values = call(
        lambda *refs: constants_kernel(side, *refs),
        "constants",
        [array(*shape, dtype=kind) for _, shape, kind in CONSTANTS],
        [wave_coef[None], visc_coef[None], stencil_start, stencil_offset],
        cost=1_000_000_000,
    )
    made.update(zip((name for name, _, _ in CONSTANTS), values))
    sent = call(
        lambda *refs: first_kernel(side, *refs),
        "first_edges",
        [strip] * 7,
        [field, made["coef"], made["order"]],
        [pltpu.VMEM((BLK, BLK), jnp.float32), strips],
        cost=1_000_000_000,
    )
    adds = []
    names = ("coef", "band_x", "band_y", "order", "spread")
    for step in range(SUBSTEPS):
        first, last = step == 0, step == SUBSTEPS - 1
        received = exchange(sent[:5], side)
        field, *edges = call(
            lambda *refs, first=first, last=last: inner_kernel(first, last, *refs),
            "inner",
            [whole] + ([] if last else [tile] * 2),
            [field, *(made[name] for name in names), *adds],
            cost=2_000_000_000,
            aliases=None if first else {0: 0},
        )
        ghosts = [*received, *sent[5:], made["taps"], made["weights"]]
        if last:
            break
        updates = call(
            lambda *refs: edge_kernel(side, *refs),
            "edges",
            [tile] * 2 + [strip] * 7,
            [*ghosts, made["corner"], made["gain"], *edges],
            [strips],
        )
        adds, sent = updates[:2], updates[2:]
    (field,) = call(
        lambda *refs: final_kernel(side, *refs),
        "final",
        [whole],
        [*ghosts, made["spread"], field],
        [pltpu.VMEM(field.shape, jnp.float32), pltpu.SemaphoreType.DMA((FACES,))],
        out_hbm=True,
    )
    return field[None]


def solution(mesh):
    placed = (P(("member", "tile"), None, None, None, None), P(), P(), P(), P())
    return jax.shard_map(
        on_device,
        mesh=mesh,
        in_specs=placed,
        out_specs=P(("member", "tile"), None, None, None, None),
        check_vma=False,
    )
```

```python
import math

import jax
import jax.numpy as jnp
from jax import lax
from jax.experimental import pallas as pl
from jax.experimental.pallas import tpu as pltpu
from jax.sharding import PartitionSpec as P

SUBSTEPS = 4
FACES = 6
LEV = 3
DEPTH = 3
BLK = 128
PER_FACE = LEV * DEPTH
ROWS = 56
TAPS = 4
HALF = 64
WEST, EAST, SOUTH, NORTH = 0, 1, 2, 3
SCALE = 20.0
VMEM_LIMIT = 16 * 1024 * 1024


def whole_vmem():
    return pl.BlockSpec(memory_space=pltpu.VMEM)


def iota(shape, dim):
    return lax.broadcasted_iota(jnp.int32, shape, dim)


def weight_of(distance):
    return jnp.where(
        distance == 1, 9.0, jnp.where(distance == 2, 7.0, jnp.where(distance == 3, 4.0, 0.0))
    )


def split2(x):
    high = x.astype(jnp.bfloat16)
    low = (x - high.astype(jnp.float32)).astype(jnp.bfloat16)
    return high, low


def lagrange_weights(t):
    return (
        -(t - 1.0) * (t - 2.0) * (t - 3.0) / 6.0,
        t * (t - 2.0) * (t - 3.0) / 2.0,
        -t * (t - 1.0) * (t - 3.0) / 2.0,
        t * (t - 1.0) * (t - 2.0) / 6.0,
    )


def band_matrix():
    gap = jnp.abs(iota((BLK, BLK), 0) - iota((BLK, BLK), 1))
    return jnp.where(gap == 0, -40.0, weight_of(gap)).astype(jnp.bfloat16)


def position(side):
    index = lax.axis_index("tile")
    return lax.rem(index, side), lax.div(index, side)


def is_inner(row, col, side):
    return 0 < row < side - 1 and 0 < col < side - 1


def row_codes(shape):
    row = iota(shape, 0)
    block = (row * 57) >> 9
    odd = (block & 1) == 1
    depth = row - 3 * ((row * 171) >> 9)
    return odd, depth


def plane_row(shape, dim):
    row = iota(shape, dim)
    lower = row < HALF
    inside = jnp.where(lower, row, row - HALF)
    plane = (inside * 171) >> 9
    return lower, plane, inside - 3 * plane


def tiles_of(plane_value):
    return plane_value.reshape(BLK // 8, 8, BLK)


def lane_of_tile():
    return iota((1, 8, BLK), 2)


def take_edges(q, plane, columns, rows_ref):
    lane, at = lane_of_tile(), 6 * plane
    turned = pltpu.roll(q, (at + 3) % BLK, 2)
    columns = jnp.where((lane >= at) & (lane < at + 6), turned, columns)
    low, high = 3 * plane, HALF + 3 * plane
    rows_ref[low : low + 3, :] = q[0, :3, :]
    rows_ref[high : high + 3, :] = q[BLK // 8 - 1, 5:, :]
    return columns


def lane_order():
    lower, plane, cell = plane_row((BLK, BLK), 0)
    lane = 6 * plane + cell + jnp.where(lower, 3, 0)
    right = (lane == iota((BLK, BLK), 1)) & (plane < FACES * LEV)
    return jnp.where(right, 1.0, 0.0).astype(jnp.bfloat16)


def rows_from_columns(columns, order):
    high, low = split2(columns.reshape(BLK, BLK))
    return lax.dot_general(
        order,
        jnp.concatenate([high, low], axis=1),
        (((1,), (1,)), ((), ())),
        preferred_element_type=jnp.float32,
    )


def clear_rest(rows_ref):
    used = FACES * PER_FACE
    rest = jnp.zeros((HALF - used, BLK), jnp.float32)
    rows_ref[used:HALF, :] = rest
    rows_ref[HALF + used :, :] = rest


def pack(columns, rows, side, outs, strips_ref):
    turn_ref, far_ref, near_ref, mirror_ref, core_ref, own_a_ref, own_b_ref = outs
    col, row = position(side)
    for face in range(FACES):
        at = PER_FACE * face
        strips_ref[WEST, face, :PER_FACE, :] = columns[at : at + PER_FACE, :]
        strips_ref[EAST, face, :PER_FACE, :] = columns[HALF + at : HALF + at + PER_FACE, :]
        strips_ref[SOUTH, face, :PER_FACE, :] = rows[at : at + PER_FACE, :]
        strips_ref[NORTH, face, :PER_FACE, :] = rows[HALF + at : HALF + at + PER_FACE, :]
    even_col, even_row = lax.rem(col, 2) == 0, lax.rem(row, 2) == 0

    def shift(place):
        return jnp.where(place == 0, 1, jnp.where(place == side - 1, FACES - 1, 0))

    middle = (col > 0) & (col < side - 1)
    up, down = jnp.where(even_row, NORTH, SOUTH), jnp.where(even_row, SOUTH, NORTH)
    plans = (
        (mirror_ref, jnp.where(even_col, WEST, EAST), shift(col)),
        (near_ref, jnp.where(middle, down, up), jnp.where(middle, shift(row), 0)),
        (far_ref, jnp.where(middle, up, down), jnp.where(middle, 0, shift(row))),
    )
    rest = jnp.zeros((ROWS - FACES * PER_FACE, BLK), jnp.float32)
    core_ref[...] = jnp.where(even_col, columns[HALF : HALF + ROWS, :], columns[:ROWS, :])
    for out_ref, which, by in plans:
        for face in range(FACES):
            at = PER_FACE * face
            source = face + by
            source = jnp.where(source >= FACES, source - FACES, source)
            out_ref[at : at + PER_FACE, :] = strips_ref[which, source, :PER_FACE, :]
        out_ref[FACES * PER_FACE :, :] = rest
    for face in range(FACES):
        at = PER_FACE * face
        if face % 2:
            a, b = (SOUTH, face + 2), (EAST, face - 2)
        else:
            a, b = (NORTH, face - 2), (WEST, face + 2)
        own_a_ref[at : at + PER_FACE, :] = strips_ref[a[0], a[1] % FACES, :PER_FACE, :]
        own_b_ref[at : at + PER_FACE, :] = strips_ref[b[0], b[1] % FACES, :PER_FACE, :]
    own_a_ref[FACES * PER_FACE :, :] = rest
    own_b_ref[FACES * PER_FACE :, :] = rest
    for face in range(FACES):
        at = PER_FACE * face
        if face % 2:
            use_a, a, b = row == 0, (SOUTH, face + 2), (EAST, face - 2)
        else:
            use_a, a, b = row == side - 1, (NORTH, face - 2), (WEST, face + 2)
        which = jnp.where(use_a, a[0], b[0])
        source = jnp.where(use_a, a[1] % FACES, b[1] % FACES)
        turn_ref[at : at + PER_FACE, :] = strips_ref[which, source, :PER_FACE, :]
    turn_ref[FACES * PER_FACE :, :] = rest


TABLES = (
    ("corner", (BLK, BLK), jnp.int32),
    ("order", (BLK, 2 * BLK), jnp.bfloat16),
    ("spread", (2 * BLK, BLK), jnp.bfloat16),
    ("band_x", (2 * BLK, BLK), jnp.bfloat16),
    ("band_y", (BLK, 2 * BLK), jnp.bfloat16),
)
CONSTANTS = (
    ("coef", (8, BLK), jnp.float32),
    ("gain", (BLK, BLK), jnp.float32),
    ("taps", (TAPS, 2 * ROWS, BLK), jnp.int32),
    ("weights", (TAPS, 2 * ROWS, BLK), jnp.float32),
)


def tables_kernel(corner, order, spread, band_x, band_y):
    for ref, value, axis in (
        (order, lane_order(), 1),
        (band_x, band_matrix(), 0),
        (band_y, band_matrix(), 1),
    ):
        ref[...] = jnp.concatenate([value, value], axis=axis)
    spread[...] = jnp.concatenate([lane_order()] * 2, axis=0)
    _, plane, _ = plane_row((BLK, BLK), 0)
    to = iota((BLK, BLK), 1)
    low, high = 3 * plane + to, HALF + 3 * plane + to - (BLK - 3)
    corner[...] = jnp.where(to < 3, low, jnp.where(to >= BLK - 3, high, 0))


def seam_rows(place, low_turned):
    odd, depth = row_codes((ROWS, BLK))
    at_low = (place == 0).astype(jnp.int32)
    is_turned = odd.astype(jnp.int32) == at_low ^ (1 - low_turned)
    return is_turned, jnp.where(place == 0, DEPTH - 1 - depth, depth)


def constants_kernel(
    side, wave_ref, visc_ref, start_ref, offset_ref, coef_ref, gain_ref, taps_ref, weights_ref
):
    col, row = position(side)
    for axis, place in enumerate((col, row)):
        is_turned, h_of = seam_rows(place, axis)
        first, offset = [
            jnp.where(h_of == 0, ref[0:1, :], jnp.where(h_of == 1, ref[1:2, :], ref[2:3, :]))
            for ref in (start_ref, offset_ref)
        ]
        at = axis * ROWS
        for m, weight in enumerate(lagrange_weights(offset)):
            tap = jnp.where(is_turned, BLK - 1 - first - m, first + m)
            taps_ref[m, at : at + ROWS, :] = tap
            weights_ref[m, at : at + ROWS, :] = weight
    _, plane, _ = plane_row((BLK, BLK), 0)
    level_of = plane - 3 * ((plane * 171) >> 9)
    gain = jnp.zeros((BLK, BLK), jnp.float32)
    for level in range(LEV):
        a, b = [
            jnp.broadcast_to(ref[:, level : level + 1] * (1.0 / SCALE), (1, BLK))
            for ref in (wave_ref, visc_ref)
        ]
        coef_ref[level : level + 1, :] = a
        coef_ref[LEV + level : LEV + level + 1, :] = b
        gain = jnp.where(level_of == level, a + b, gain)
    coef_ref[2 * LEV :, :] = jnp.zeros((8 - 2 * LEV, BLK), jnp.float32)
    gain_ref[...] = gain


def first_kernel(side, state_ref, coef_ref, order_ref, *rest):
    outs = rest[:7]
    rows_ref, strips_ref = rest[7:]
    clear_rest(rows_ref)
    columns = jnp.zeros((BLK // 8, 8, BLK), jnp.float32)
    for plane in range(FACES * LEV):
        face, level = divmod(plane, LEV)
        a, b = coef_ref[level : level + 1, :], coef_ref[LEV + level : LEV + level + 1, :]
        q = a * state_ref[face, level] + b * state_ref[face, LEV + level]
        columns = take_edges(tiles_of(q), plane, columns, rows_ref)
    packed = rows_from_columns(columns, order_ref[...])
    pack(packed, rows_ref[...], side, outs, strips_ref)


def ghosts_of(side, received, own_a_ref, own_b_ref, taps_ref, weights_ref):
    far, turned, near, mirror, core = [ref[...] for ref in received]
    col, row = position(side)
    even_col, even_row = lax.rem(col, 2) == 0, lax.rem(row, 2) == 0
    middle = (col > 0) & (col < side - 1)
    near, far = jnp.where(middle, far, near), jnp.where(middle, near, far)
    alone = ((row == 0) & (col == side - 1)) | ((col == 0) & (row == side - 1))
    pairs = (
        (
            jnp.where(even_col, mirror, core),
            jnp.where(even_col, core, mirror),
            jnp.where(alone, own_a_ref[...], turned),
            col,
            0,
        ),
        (
            jnp.where(even_row, far, near),
            jnp.where(even_row, near, far),
            jnp.where(alone, own_b_ref[...], turned),
            row,
            1,
        ),
    )
    seams = []
    for low, high, crossed, place, low_turned in pairs:
        is_turned, _ = seam_rows(place, low_turned)
        seams.append(jnp.where(is_turned, crossed, jnp.where(place == 0, low, high)))
    raw = jnp.concatenate(seams, axis=0)
    mixed = jnp.zeros((2 * ROWS, BLK), jnp.float32)
    for m in range(TAPS):
        source = jnp.take_along_axis(raw, taps_ref[m], axis=1, mode="promise_in_bounds")
        mixed = mixed + weights_ref[m] * source
    rest = jnp.zeros((HALF - ROWS, BLK), jnp.float32)
    ghosts = []
    for index, (low, high, _, place, _) in enumerate(pairs):
        made = mixed[index * ROWS : (index + 1) * ROWS, :]
        ghosts.append(
            jnp.concatenate(
                [
                    jnp.where(place == 0, made, low),
                    rest,
                    jnp.where(place == side - 1, made, high),
                    rest,
                ],
                axis=0,
            )
        )
    return ghosts


def ghost_additions(ghosts):
    row = iota((HALF, 1), 0)
    cell = row - 3 * ((row * 171) >> 9)
    halves = []
    both = jnp.concatenate(ghosts, axis=1)
    for half, step, index in ((both[:HALF], -1, cell), (both[HALF:], 1, 2 - cell)):
        one = pltpu.roll(half, step % HALF, 0)
        two = pltpu.roll(half, (2 * step) % HALF, 0)
        near, next_ = jnp.where(index <= 1, 7.0, 0.0), jnp.where(index == 0, 9.0, 0.0)
        halves.append(4.0 * half + near * one + next_ * two)
    adds = jnp.concatenate(halves, axis=0)
    return adds[:, :BLK], adds[:, BLK:]


def corner_part(adds, corner):
    turned = adds.T
    cell = plane_row((HALF, BLK), 0)[2]
    halves = []
    for first in (0, BLK - 3):
        lines = [turned[first + at : first + at + 1, :] for at in range(3)]
        halves.append(jnp.where(cell == 0, lines[0], jnp.where(cell == 1, lines[1], lines[2])))
    lines = jnp.concatenate(halves, axis=0)
    taken = jnp.take_along_axis(lines, corner, axis=1, mode="promise_in_bounds")
    lane = iota((1, BLK), 1)
    return jnp.where((lane < 3) | (lane >= BLK - 3), taken, 0.0)


def edge_kernel(side, *refs):
    across, along = ghosts_of(side, refs[:5], *refs[5:9])
    corner_ref, gain_ref, old_columns_ref, old_rows_ref = refs[9:13]
    add_x_ref, add_y_ref = refs[13:15]
    outs = refs[15:22]
    strips_ref = refs[22]
    add_x, add_y = ghost_additions((across, along))
    gain, corner = gain_ref[...], corner_ref[...]
    columns = old_columns_ref[...] + gain * (add_x + corner_part(add_y, corner))
    rows = old_rows_ref[...] + gain * (add_y + corner_part(add_x, corner))
    add_x_ref[...] = add_x
    add_y_ref[...] = add_y
    pack(columns, rows, side, outs, strips_ref)


def spread_lanes(add_x, spread_ref):
    high, low = split2(add_x.T)
    return tiles_of(
        jnp.dot(
            jnp.concatenate([high, low], axis=1),
            spread_ref[...],
            preferred_element_type=jnp.float32,
        )
    )


def edge_additions(plane, add_x, add_y):
    lane = lane_of_tile()
    turned = pltpu.roll(add_x, (BLK - 3 - 6 * plane) % BLK, 2)
    add = jnp.where((lane < 3) | (lane >= BLK - 3), turned, 0.0)
    at = 3 * plane
    pad = jnp.zeros((5, BLK), jnp.float32)
    bottom = add[:1] + jnp.concatenate([add_y[at : at + 3], pad], axis=0)[None]
    top = add[-1:] + jnp.concatenate([pad, add_y[HALF + at : HALF + at + 3]], axis=0)[None]
    return jnp.concatenate([bottom, add[1:-1], top], axis=0)


def inner_kernel(first, last, state_ref, *refs):
    coef_ref, band_x_ref, band_y_ref, order_ref, spread_ref = refs[:5]
    refs = refs[5:]
    if not first:
        add_x, add_y = spread_lanes(refs[0][...], spread_ref), refs[1][...]
        refs = refs[2:]
    new_ref = refs[0]
    if not last:
        columns_ref, rows_ref = refs[1:]
    if not last:
        clear_rest(rows_ref)
    columns = jnp.zeros((BLK // 8, 8, BLK), jnp.float32)
    group = 2
    for begin in range(0, FACES * LEV, group):
        fields, highs, lows = [], [], []
        for plane in range(begin, begin + group):
            face, level = divmod(plane, LEV)
            a, b = coef_ref[level : level + 1, :], coef_ref[LEV + level : LEV + level + 1, :]
            pressure = tiles_of(state_ref[face, level])
            rate = tiles_of(state_ref[face, LEV + level])
            if not first:
                add = edge_additions(plane, add_x, add_y)
                pressure, rate = pressure + add, rate + add
            high, low = split2((a * pressure + b * rate).reshape(BLK, BLK))
            fields.append((pressure, rate))
            highs.append(high)
            lows.append(low)
        by_x = jnp.dot(
            jnp.concatenate(
                [jnp.concatenate(pair, axis=1) for pair in zip(highs, lows)], axis=0
            ),
            band_x_ref[...],
            preferred_element_type=jnp.float32,
        )
        by_y = jnp.dot(
            band_y_ref[...],
            jnp.concatenate(
                [jnp.concatenate(highs, axis=1), jnp.concatenate(lows, axis=1)], axis=0
            ),
            preferred_element_type=jnp.float32,
        )
        for place, (pressure, rate) in enumerate(fields):
            plane = begin + place
            face, level = divmod(plane, LEV)
            a, b = coef_ref[level : level + 1, :], coef_ref[LEV + level : LEV + level + 1, :]
            at = place * BLK
            rate = rate + tiles_of(by_x[at : at + BLK, :] + by_y[:, at : at + BLK])
            pressure = pressure + rate
            new_ref[face, level] = pressure.reshape(BLK, BLK)
            new_ref[face, LEV + level] = rate.reshape(BLK, BLK)
            if not last:
                columns = take_edges(a * pressure + b * rate, plane, columns, rows_ref)
    if not last:
        columns_ref[...] = rows_from_columns(columns, order_ref[...])


def final_kernel(side, *refs):
    spread_ref, state_ref, out_hbm, buffer, sems = refs[9:]
    add_x, add_y = ghost_additions(ghosts_of(side, refs[:5], *refs[5:9]))
    add_x = spread_lanes(add_x, spread_ref)
    copies = []
    for face in range(FACES):
        for level in range(LEV):
            add = edge_additions(face * LEV + level, add_x, add_y)
            for channel in (level, LEV + level):
                value = tiles_of(state_ref[face, channel]) + add
                buffer[face, channel] = value.reshape(BLK, BLK)
        copy = pltpu.make_async_copy(buffer.at[face], out_hbm.at[face], sems.at[face])
        copy.start()
        copies.append(copy)
    for copy in copies:
        copy.wait()


def exchange(payloads, side):
    def at(row, col):
        return row * side + col

    cells = [(row, col) for row in range(side) for col in range(side)]

    def swap(place, odd_first):
        return (place ^ 1) if not odd_first else (place + (1 if place % 2 else -1)) % side

    core = [(at(r, c), at(r, swap(c, False))) for r, c in cells]
    mirror = [(at(r, c), at(r, swap(c, True))) for r, c in cells]
    edge = side - 1
    near = [(at(r, c), at(swap(r, 0 < c < edge), c)) for r, c in cells]
    far = [(at(r, c), at(swap(r, not 0 < c < edge), c)) for r, c in cells]
    turn = set()
    for x in range(edge):
        turn |= {(at(0, x), at(edge - x, edge)), (at(edge - x, edge), at(0, x))}
    for x in range(1, side):
        turn |= {(at(edge, x), at(edge - x, 0)), (at(edge - x, 0), at(edge, x))}
    spare = [pair for pair in mirror if is_inner(pair[0] // side, pair[0] % side, side)]
    first_end, last_end = at(1, edge - 1), at(edge - 1, 1)
    left = [b for a, b in spare if a in (first_end, last_end)]
    spare = [pair for pair in spare if not {*pair} & {first_end, last_end}]
    spare += [(at(0, edge), first_end), (at(edge, 0), last_end), (left[0], left[1])]
    turn |= {(a, b) for a, b in spare} | {(b, a) for a, b in spare}
    turn_out, far_out, near_out, mirror_out, core_out = payloads
    turn_in = lax.ppermute(turn_out, "tile", sorted(turn))
    far_in = lax.ppermute(far_out, "tile", far)
    near_in = lax.ppermute(near_out, "tile", near)
    mirror_in = lax.ppermute(mirror_out, "tile", mirror)
    core_in = lax.ppermute(core_out, "tile", core)
    return far_in, turn_in, near_in, mirror_in, core_in


def call(kernel, name, outs, ins, scratch=(), out_hbm=False, cost=0, aliases=None):
    hbm = pl.BlockSpec(memory_space=pltpu.HBM)
    vmem = pl.BlockSpec(memory_space=pltpu.VMEM)
    return pl.pallas_call(
        kernel,
        out_shape=outs,
        in_specs=[vmem] * len(ins),
        out_specs=[hbm if out_hbm else vmem] * len(outs),
        scratch_shapes=list(scratch),
        compiler_params=pltpu.CompilerParams(vmem_limit_bytes=VMEM_LIMIT),
        cost_estimate=pl.CostEstimate(flops=cost, bytes_accessed=cost // 500, transcendentals=0),
        input_output_aliases=aliases or {},
        name=name,
    )(*ins)


def on_device(state, wave_coef, visc_coef, stencil_start, stencil_offset):
    side = math.isqrt(lax.axis_size("tile"))
    field = state[0]

    def array(*shape, dtype=jnp.float32):
        return jax.ShapeDtypeStruct(shape, dtype)

    tile = array(BLK, BLK)
    strip = array(ROWS, BLK)
    whole = array(*field.shape)
    strips = pltpu.VMEM((4, FACES, 16, BLK), jnp.float32)
    values = call(
        tables_kernel,
        "tables",
        [array(*shape, dtype=kind) for _, shape, kind in TABLES],
        [],
        cost=4_000_000_000,
    )
    made = dict(zip((name for name, _, _ in TABLES), values))
    values = call(
        lambda *refs: constants_kernel(side, *refs),
        "constants",
        [array(*shape, dtype=kind) for _, shape, kind in CONSTANTS],
        [wave_coef[None], visc_coef[None], stencil_start, stencil_offset],
        cost=1_000_000_000,
    )
    made.update(zip((name for name, _, _ in CONSTANTS), values))
    sent = call(
        lambda *refs: first_kernel(side, *refs),
        "first_edges",
        [strip] * 7,
        [field, made["coef"], made["order"]],
        [pltpu.VMEM((BLK, BLK), jnp.float32), strips],
        cost=1_000_000_000,
    )
    adds = []
    names = ("coef", "band_x", "band_y", "order", "spread")
    for step in range(SUBSTEPS):
        first, last = step == 0, step == SUBSTEPS - 1
        received = exchange(sent[:5], side)
        field, *edges = call(
            lambda *refs, first=first, last=last: inner_kernel(first, last, *refs),
            "inner",
            [whole] + ([] if last else [tile] * 2),
            [field, *(made[name] for name in names), *adds],
            cost=2_000_000_000,
            aliases=None if first else {0: 0},
        )
        ghosts = [*received, *sent[5:], made["taps"], made["weights"]]
        if last:
            break
        updates = call(
            lambda *refs: edge_kernel(side, *refs),
            "edges",
            [tile] * 2 + [strip] * 7,
            [*ghosts, made["corner"], made["gain"], *edges],
            [strips],
        )
        adds, sent = updates[:2], updates[2:]
    (field,) = call(
        lambda *refs: final_kernel(side, *refs),
        "final",
        [whole],
        [*ghosts, made["spread"], field],
        [pltpu.VMEM(field.shape, jnp.float32), pltpu.SemaphoreType.DMA((FACES,))],
        out_hbm=True,
    )
    return field[None]


def solution(mesh):
    placed = (P(("member", "tile"), None, None, None, None), P(), P(), P(), P())
    return jax.shard_map(
        on_device,
        mesh=mesh,
        in_specs=placed,
        out_specs=P(("member", "tile"), None, None, None, None),
        check_vma=False,
    )
```
